256 devices in a mesh: dp: 64 (over z_lo, x, y, core), tp: 4 (over z_hi).
Axes of the slice: x: 4, y: 4, z: 8 (z_hi: 4, z_lo: 2; z = z_hi * 2 + z_lo), core: 2. Of those that a mesh axis runs over, the one named last changes fastest.
Arguments:
- tokens: bfloat16 [32768, 5120], P(('dp', 'tp')), may hold values from -24 to 24
- queries: bfloat16 [32768, 4096], P('dp', 'tp'), may hold values from -6 to 6
- grad_out: bfloat16 [32768, 4096], P('dp', 'tp'), may hold values from -6 to 6
- key_value_master_weight: float32 [2, 5120, 512], P(None, 'dp', 'tp'), may hold values from -6 to 6
- key_value_first_moment: float32 [2, 5120, 512], P(None, 'dp', 'tp'), may hold values from -6 to 6
- key_value_second_moment: float32 [2, 5120, 512], P(None, 'dp', 'tp'), may hold values from 0.5 to 8
- writer: int32 [64], replicated, may hold values from 0 to 63, each once
Outputs:
- grad_x: bfloat16 [32768, 5120], P(('dp', 'tp'))
- grad_q: bfloat16 [32768, 4096], P('dp', 'tp')
- new_master: float32 [2, 5120, 512], P(None, 'dp', 'tp')
- new_first: float32 [2, 5120, 512], P(None, 'dp', 'tp')
- new_second: float32 [2, 5120, 512], P(None, 'dp', 'tp')
- saved: bfloat16 [4096, 1280], P('dp', 'tp')
The draws below stay inside these ranges and needn't reach their ends.
Inputs may be any that keep to these rules, and one draw needn't show every extreme that they name: writer is a permutation: each of the 64 replicas writes exactly one save shard.
All inputs are finite; a program needn't handle non-finite values.
Results may differ from the reference program's by a relative error of at most 0.017.
Values may be sent and summed in bfloat16 or wider, within the bound.
No kernel may reach another device: no remote copies, remote signals or barrier semaphores. Data moves between devices by JAX's collectives and lax.ppermute only.
A program may use at most 128 MiB of HBM per device.

```python
import math
import jax
import jax.numpy as jnp
from jax import lax

MODEL_DIM = 5120
QUERY_HEADS = 32
KEY_VALUE_HEADS = 4
HEAD_SIZE = 128
SEQUENCE_TOKENS = 512
TOKENS = 32768
PIECE = 320
N_DP = 64
N_TP = 4


def strengthened(entries, own_key, source, target, blocks, factor):
    def block_of(position):
        return (jnp.arange(entries.shape[position]) // (entries.shape[position] // blocks)).reshape((-1,) + (1,) * (entries.ndim - 1 - position))

    near = jax.random.permutation(own_key, blocks)[block_of(target)]
    other_side = (block_of(target) + blocks // 2) % blocks
    return jnp.where((block_of(source) == near) | (block_of(source) == other_side), factor * entries, entries)


def steps_of(rng, dims, pieces, smallest, largest):
    loudness, own = 1.0, jax.random.fold_in(rng, 6)
    for position, shards_of in pieces:
        steps = jnp.exp(jax.random.uniform(jax.random.fold_in(own, position), (shards_of,), jnp.float32, smallest / len(pieces), largest / len(pieces)))
        loudness = loudness * jnp.repeat(steps, dims[position] // shards_of).reshape([-1 if axis == position else 1 for axis in range(len(dims))])
    return loudness


def normal_values(stream_key, extent, spread, reach, cuts=(), kind=jnp.bfloat16):
    drawn = jax.random.normal(stream_key, extent, jnp.float32) * spread
    if len(cuts) > 0:
        drawn = steps_of(stream_key, extent, cuts, -0.22, 0.18) * drawn
    return jnp.clip(drawn, min=-reach, max=reach).astype(kind)


def gaussian_with(rng, shape, spread, limit, shards, heavy, kind=jnp.bfloat16):
    result = spread * jax.random.normal(rng, shape, jnp.float32)
    if shards:
        result = result * steps_of(rng, shape, shards, -0.22, 0.18)
    return jnp.clip(strengthened(result, jax.random.fold_in(rng, 3), *heavy), -limit, limit).astype(kind)


def setup_inputs(seed: int = 0) -> dict:
    keys = jax.random.split(jax.random.key(seed), 8)
    tokens = gaussian_with(keys[0], (TOKENS, MODEL_DIM), 1.0, 24.0, ((0, 256),), (0, 1, 256, 6.0))
    queries = normal_values(keys[1], (TOKENS, QUERY_HEADS * HEAD_SIZE), 1.0, 6.0, ((0, 64), (1, 4)))
    grad_out = normal_values(keys[2], (TOKENS, QUERY_HEADS * HEAD_SIZE), 1.0, 6.0, ((0, 64), (1, 4)))
    key_value_master_weight = normal_values(keys[3], (2, MODEL_DIM, KEY_VALUE_HEADS * HEAD_SIZE), 1.0, 6.0, ((1, 64), (2, 4)), jnp.float32)
    key_value_first_moment = normal_values(keys[4], (2, MODEL_DIM, KEY_VALUE_HEADS * HEAD_SIZE), 1.0, 6.0, ((1, 64), (2, 4)), jnp.float32)
    key_value_second_moment = jnp.clip(jnp.exp(math.log(8.0) - 2.7725887 * jax.random.uniform(keys[5], (2, MODEL_DIM, KEY_VALUE_HEADS * HEAD_SIZE), jnp.float32) ** steps_of(keys[5], (2, MODEL_DIM, KEY_VALUE_HEADS * HEAD_SIZE), ((1, 64), (2, 4)), -0.2, 0.2)), 0.5, 8.0)
    writer = jax.random.permutation(keys[6], N_DP).astype(jnp.int32)
    return {"tokens": tokens, "queries": queries, "grad_out": grad_out, "key_value_master_weight": key_value_master_weight, "key_value_first_moment": key_value_first_moment, "key_value_second_moment": key_value_second_moment, "writer": writer}


norm_eps = 1e-06
rope_base = 1000000.0
beta_one = 0.9
beta_two = 0.95
adam_eps = 1e-08
learn_rate = 0.02
weight_decay = 0.1
step_count = 10.0

def rope_tables(length, head_width):
    half_width = head_width // 2
    index_float = jnp.arange(half_width, dtype=jnp.float32)
    inverse_freq = rope_base ** (-2.0 * index_float / head_width)
    positions = jnp.arange(length, dtype=jnp.float32)
    angles = positions[:, None] * inverse_freq[None, :]
    return (jnp.cos(angles), jnp.sin(angles))

def rotate(field, cosine_table, sine_table):
    half_width = field.shape[-1] // 2
    lower = field[..., :half_width]
    upper = field[..., half_width:]
    cosines = cosine_table[:, None, :]
    sines = sine_table[:, None, :]
    return jnp.concatenate([lower * cosines - upper * sines, upper * cosines + lower * sines], axis=-1)

def unrotate(cotan, cosine_table, sine_table):
    half_width = cotan.shape[-1] // 2
    lower = cotan[..., :half_width]
    upper = cotan[..., half_width:]
    cosines = cosine_table[:, None, :]
    sines = sine_table[:, None, :]
    return jnp.concatenate([lower * cosines + upper * sines, upper * cosines - lower * sines], axis=-1)

def norm_scale(field):
    return lax.rsqrt(lax.optimization_barrier(jnp.mean(field * field, axis=-1, keepdims=True)) + norm_eps)

def norm_back(field, factor, cotan):
    return factor * cotan - field * (factor * factor * factor) * lax.optimization_barrier(jnp.mean(cotan * field, axis=-1, keepdims=True))

def replica_pass(weights_b, token_rows, query_rows, incoming_gradient_rows):
    unit_scale = 1.0 / math.sqrt(MODEL_DIM)
    root_hd = math.sqrt(HEAD_SIZE)
    group_count = QUERY_HEADS // KEY_VALUE_HEADS
    column_total = KEY_VALUE_HEADS * HEAD_SIZE
    token_float = token_rows.astype(jnp.float32)
    token_factor = norm_scale(token_float)
    normed = (token_float * token_factor).astype(jnp.bfloat16)
    normed_float = normed.astype(jnp.float32)
    weights_float = weights_b.astype(jnp.float32)
    key_value_plain = jnp.einsum('sd,jdc->jsc', normed_float, weights_float) * unit_scale
    cosine_table, sine_table = rope_tables(SEQUENCE_TOKENS, HEAD_SIZE)
    key_unrotated = key_value_plain[0].reshape(SEQUENCE_TOKENS, KEY_VALUE_HEADS, HEAD_SIZE)
    key_factor = norm_scale(key_unrotated)
    key_rot = rotate(key_unrotated * key_factor, cosine_table, sine_table).astype(jnp.bfloat16)
    value_halfprecision = key_value_plain[1].reshape(SEQUENCE_TOKENS, KEY_VALUE_HEADS, HEAD_SIZE).astype(jnp.bfloat16)
    q_float = query_rows.astype(jnp.float32).reshape(SEQUENCE_TOKENS, QUERY_HEADS, HEAD_SIZE)
    q_factor = norm_scale(q_float)
    query_rotated = rotate(q_float * q_factor, cosine_table, sine_table).astype(jnp.bfloat16)
    grouped_query = query_rotated.astype(jnp.float32).reshape(SEQUENCE_TOKENS, KEY_VALUE_HEADS, group_count, HEAD_SIZE)
    incoming_gradient = incoming_gradient_rows.astype(jnp.float32).reshape(SEQUENCE_TOKENS, KEY_VALUE_HEADS, group_count, HEAD_SIZE)
    key_float = key_rot.astype(jnp.float32)
    value_float = value_halfprecision.astype(jnp.float32)
    scores = jnp.einsum('sagd,tad->agst', grouped_query, key_float) / root_hd
    rows_pos = jnp.arange(SEQUENCE_TOKENS, dtype=jnp.int32)
    causal = rows_pos[:, None] >= rows_pos[None, :]
    raised = jnp.where(causal, jnp.exp(scores), 0.0)
    attn_probs = raised / lax.optimization_barrier(jnp.sum(raised, axis=-1, keepdims=True))
    probs_b = attn_probs.astype(jnp.bfloat16).astype(jnp.float32)
    d_value = jnp.einsum('agst,sagd->tad', probs_b, incoming_gradient)
    d_probs = jnp.einsum('sagd,tad->agst', incoming_gradient, value_float)
    row_sum = lax.optimization_barrier(jnp.sum(attn_probs * d_probs, axis=-1, keepdims=True))
    d_scores = (attn_probs * (d_probs - row_sum)).astype(jnp.bfloat16).astype(jnp.float32)
    d_query = jnp.einsum('agst,tad->sagd', d_scores, key_float) / root_hd
    d_key = jnp.einsum('agst,sagd->tad', d_scores, grouped_query) / root_hd
    grad_q = norm_back(q_float, q_factor, unrotate(d_query.reshape(SEQUENCE_TOKENS, QUERY_HEADS, HEAD_SIZE), cosine_table, sine_table))
    grad_q = grad_q.astype(jnp.bfloat16).reshape(SEQUENCE_TOKENS, QUERY_HEADS * HEAD_SIZE)
    key_cotan = norm_back(key_unrotated, key_factor, unrotate(d_key, cosine_table, sine_table))
    key_flat = key_cotan.reshape(SEQUENCE_TOKENS, column_total).astype(jnp.bfloat16)
    value_flat = d_value.reshape(SEQUENCE_TOKENS, column_total).astype(jnp.bfloat16)
    stacked = jnp.stack([key_flat, value_flat], axis=0)
    stacked_float = stacked.astype(jnp.float32)
    group_cols = column_total // N_TP
    parts = jnp.einsum('jstc,jdtc->tsd', stacked_float.reshape(2, SEQUENCE_TOKENS, N_TP, group_cols), weights_float.reshape(2, MODEL_DIM, N_TP, group_cols)) * unit_scale
    parts_b = lax.optimization_barrier(parts.astype(jnp.bfloat16))
    d_normed = lax.optimization_barrier(jnp.sum(parts_b.astype(jnp.float32), axis=0))
    grad_x = norm_back(token_float, token_factor, d_normed).astype(jnp.bfloat16)
    grad_part = jnp.einsum('sd,jsc->jdc', normed_float, stacked_float) * unit_scale
    return (grad_x, grad_q, grad_part)

def reference(tokens, queries, grad_out, key_value_master_weight, key_value_first_moment, key_value_second_moment, writer):
    weights_b = key_value_master_weight.astype(jnp.bfloat16)

    def replica_step(carry, inputs):
        token_rows, query_rows, incoming_gradient_rows = inputs
        grad_x, grad_q, grad_part = replica_pass(weights_b, token_rows, query_rows, incoming_gradient_rows)
        return (carry + grad_part, (grad_x, grad_q))
    starting_value = jnp.zeros((2, MODEL_DIM, KEY_VALUE_HEADS * HEAD_SIZE), jnp.float32)
    weight_grad, outputs = lax.scan(replica_step, starting_value, (tokens.reshape(N_DP, SEQUENCE_TOKENS, MODEL_DIM), queries.reshape(N_DP, SEQUENCE_TOKENS, QUERY_HEADS * HEAD_SIZE), grad_out.reshape(N_DP, SEQUENCE_TOKENS, QUERY_HEADS * HEAD_SIZE)))
    grad_x = outputs[0].reshape(TOKENS, MODEL_DIM)
    grad_q = outputs[1].reshape(TOKENS, QUERY_HEADS * HEAD_SIZE)
    new_first = beta_one * key_value_first_moment + (1.0 - beta_one) * weight_grad
    new_second = beta_two * key_value_second_moment + (1.0 - beta_two) * weight_grad * weight_grad
    first_hat = new_first / (1.0 - beta_one ** step_count)
    second_hat = new_second / (1.0 - beta_two ** step_count)
    new_master = key_value_master_weight - learn_rate * (first_hat / (jnp.sqrt(second_hat) + adam_eps) + weight_decay * key_value_master_weight)
    rows_own = MODEL_DIM // N_DP
    column_mine = KEY_VALUE_HEADS * HEAD_SIZE // N_TP
    blocks = new_master.astype(jnp.bfloat16).reshape(2, N_DP, rows_own, N_TP, column_mine)
    blocks = jnp.transpose(blocks, (1, 3, 0, 2, 4)).reshape(N_DP, N_TP, N_DP, PIECE)
    rank_ids = jnp.arange(N_DP, dtype=jnp.int32)
    inverse = jnp.zeros((N_DP,), jnp.int32).at[writer].set(rank_ids)
    chosen = blocks[:, :, inverse, :]
    saved = jnp.transpose(chosen, (2, 0, 1, 3)).reshape(N_DP * N_DP, N_TP * PIECE)
    return (grad_x, grad_q, new_master, new_first, new_second, saved)
```

```python
import math

import jax
import jax.numpy as jnp
from jax import lax
from jax.sharding import Mesh, PartitionSpec as P

HEAD_SIZE = 128


norm_eps = 1e-06
rope_base = 1000000.0
beta_one = 0.9
beta_two = 0.95
adam_eps = 1e-08
learn_rate = 0.02
weight_decay = 0.1
step_count = 10.0


def rope_tables(length, head_width):
    half_width = head_width // 2
    index_float = jnp.arange(half_width, dtype=jnp.float32)
    inverse_freq = rope_base ** (-2.0 * index_float / head_width)
    positions = jnp.arange(length, dtype=jnp.float32)
    angles = positions[:, None] * inverse_freq[None, :]
    return (jnp.cos(angles), jnp.sin(angles))


def rotate(field, cosine_table, sine_table):
    half_width = field.shape[-1] // 2
    lower = field[..., :half_width]
    upper = field[..., half_width:]
    cosines = cosine_table[:, None, :]
    sines = sine_table[:, None, :]
    return jnp.concatenate(
        [lower * cosines - upper * sines, upper * cosines + lower * sines], axis=-1
    )


def unrotate(cotan, cosine_table, sine_table):
    half_width = cotan.shape[-1] // 2
    lower = cotan[..., :half_width]
    upper = cotan[..., half_width:]
    cosines = cosine_table[:, None, :]
    sines = sine_table[:, None, :]
    return jnp.concatenate(
        [lower * cosines + upper * sines, upper * cosines - lower * sines], axis=-1
    )


def norm_scale(field):
    return lax.rsqrt(jnp.mean(field * field, axis=-1, keepdims=True) + norm_eps)


def norm_back(field, factor, cotan):
    return factor * cotan - field * (factor * factor * factor) * jnp.mean(
        cotan * field, axis=-1, keepdims=True
    )


def ring(count, step):
    return [(i, (i + step) % count) for i in range(count)]


STEPS = (1, 3, 2)


def gather_four(shard, axis):
    me = lax.axis_index(axis)
    parts = [shard] + [lax.ppermute(shard, axis, ring(4, step)) for step in STEPS]
    whole = jnp.zeros((4,) + shard.shape, shard.dtype)
    for step, part in zip((0,) + STEPS, parts):
        whole = lax.dynamic_update_index_in_dim(whole, part, (me + 4 - step) % 4, 0)
    return whole


def scatter_sum_four(pieces, axis, pick):
    me = lax.axis_index(axis)
    total = pick(pieces, me).astype(jnp.float32)
    arrived = [lax.ppermute(pick(pieces, (me + step) % 4), axis, ring(4, step)) for step in STEPS]
    for part in arrived:
        total = total + part.astype(jnp.float32)
    return total


def per_device(
    tokens,
    queries,
    grad_out,
    key_value_master_weight,
    key_value_first_moment,
    key_value_second_moment,
    writer,
):
    model_width = tokens.shape[1]
    unit_scale = 1.0 / math.sqrt(model_width)
    root_hd = math.sqrt(HEAD_SIZE)
    bf = jnp.bfloat16
    core = lax.axis_index("c")
    t_index = lax.axis_index("t")
    rows = key_value_master_weight.shape[1]
    own_tokens = tokens.shape[0]
    weights_local = key_value_master_weight.astype(bf)
    outgoing = jnp.broadcast_to(
        weights_local[None, :, None], (2, 2, 4) + weights_local.shape[1:]
    ).reshape(16, rows, HEAD_SIZE)
    stage = lax.all_to_all(outgoing, ("zl", "c", "t"), 0, 0, tiled=True)
    stage = jnp.transpose(stage.reshape(2, 2, 4, rows, HEAD_SIZE), (0, 1, 3, 2, 4))
    stage = stage.reshape(2, 2 * rows, 4 * HEAD_SIZE)
    half = 2 * HEAD_SIZE
    left = gather_four(stage[..., :half], "y")
    right = gather_four(stage[..., half:], "x")
    left = gather_four(left, "x")
    right = gather_four(right, "y")
    left = jnp.transpose(left, (2, 0, 1, 3, 4)).reshape(model_width, half)
    right = jnp.transpose(right, (2, 1, 0, 3, 4)).reshape(model_width, half)
    weights = jnp.concatenate([left, right], axis=1)

    token_float = tokens.astype(jnp.float32)
    token_factor = norm_scale(token_float)
    normed_local = (token_float * token_factor).astype(bf)
    normed_other = lax.ppermute(normed_local, "c", [(0, 1), (1, 0)])
    first = jnp.where(core == 0, normed_local, normed_other)
    second = jnp.where(core == 0, normed_other, normed_local)
    normed = jnp.concatenate([first, second], axis=0)

    plain = jnp.dot(normed, weights, preferred_element_type=jnp.float32) * unit_scale
    length = queries.shape[0]
    cosine_table, sine_table = rope_tables(length, HEAD_SIZE)
    own_cos = lax.dynamic_slice_in_dim(cosine_table, t_index * own_tokens, own_tokens, 0)
    own_sin = lax.dynamic_slice_in_dim(sine_table, t_index * own_tokens, own_tokens, 0)
    own_cos = jnp.concatenate([own_cos, own_cos], axis=0)
    own_sin = jnp.concatenate([own_sin, own_sin], axis=0)
    plain = plain.reshape(2 * own_tokens, 4, HEAD_SIZE)
    key_factor = norm_scale(plain)
    projected = jnp.where(core == 0, rotate(plain * key_factor, own_cos, own_sin), plain).astype(bf)
    projected = jnp.transpose(projected.reshape(2, own_tokens, 4, HEAD_SIZE), (0, 2, 1, 3))
    arrived = lax.all_to_all(
        projected.reshape(8, own_tokens, HEAD_SIZE), ("c", "t"), 0, 0, tiled=True
    )
    arrived = arrived.reshape(2, length, HEAD_SIZE)
    key_rot = arrived[0]
    value = arrived[1]

    q_heads = queries.shape[1] // HEAD_SIZE
    q_float = queries.astype(jnp.float32).reshape(length, q_heads, HEAD_SIZE)
    q_factor = norm_scale(q_float)
    query_rotated = rotate(q_float * q_factor, cosine_table, sine_table).astype(bf)
    incoming = grad_out.reshape(length, q_heads, HEAD_SIZE)
    scores = (
        jnp.einsum("sgd,td->gst", query_rotated, key_rot, preferred_element_type=jnp.float32)
        / root_hd
    )
    rows_pos = jnp.arange(length, dtype=jnp.int32)
    causal = rows_pos[:, None] >= rows_pos[None, :]
    raised = jnp.where(causal, jnp.exp(scores), 0.0)
    attn_probs = raised / jnp.sum(raised, axis=-1, keepdims=True)
    probs_b = attn_probs.astype(bf)
    d_value = jnp.einsum("gst,sgd->td", probs_b, incoming, preferred_element_type=jnp.float32)
    d_probs = jnp.einsum("sgd,td->gst", incoming, value, preferred_element_type=jnp.float32)
    row_sum = jnp.sum(attn_probs * d_probs, axis=-1, keepdims=True)
    d_scores = (attn_probs * (d_probs - row_sum)).astype(bf)
    d_query = (
        jnp.einsum("gst,td->sgd", d_scores, key_rot, preferred_element_type=jnp.float32) / root_hd
    )
    d_key = (
        jnp.einsum("gst,sgd->td", d_scores, query_rotated, preferred_element_type=jnp.float32)
        / root_hd
    )
    grad_q = norm_back(q_float, q_factor, unrotate(d_query, cosine_table, sine_table))
    grad_q = grad_q.astype(bf).reshape(length, q_heads * HEAD_SIZE)

    returning = jnp.stack([d_key.astype(bf), d_value.astype(bf)], axis=0)
    back = lax.all_to_all(
        returning.reshape(8, own_tokens, HEAD_SIZE), ("c", "t"), 0, 0, tiled=True
    )
    back = jnp.transpose(back.reshape(2, 4, own_tokens, HEAD_SIZE), (0, 2, 1, 3))
    back = back.reshape(2 * own_tokens, 4, HEAD_SIZE)
    back_float = back.astype(jnp.float32)
    key_cotan = norm_back(plain, key_factor, unrotate(back_float, own_cos, own_sin)).astype(bf)
    cotan = jnp.where(core == 0, key_cotan, back).reshape(2 * own_tokens, 4 * HEAD_SIZE)

    partial = lax.dot_general(
        normed, cotan, (((0,), (0,)), ((), ())), preferred_element_type=jnp.float32
    ).astype(bf)
    partial = partial.reshape(2, 4, 4, 2 * rows, 4 * HEAD_SIZE)
    left = scatter_sum_four(
        partial[..., :half], "x", lambda a, i: lax.dynamic_index_in_dim(a, i, 1, False)
    ).astype(bf)
    right = scatter_sum_four(
        partial[..., half:], "y", lambda a, i: lax.dynamic_index_in_dim(a, i, 2, False)
    ).astype(bf)
    left = scatter_sum_four(left, "y", lambda a, i: lax.dynamic_index_in_dim(a, i, 1, False))
    right = scatter_sum_four(right, "x", lambda a, i: lax.dynamic_index_in_dim(a, i, 1, False))
    summed = jnp.concatenate([left, right], axis=-1).astype(bf)
    summed = jnp.transpose(summed.reshape(2, 2, rows, 4, HEAD_SIZE), (0, 1, 3, 2, 4))
    final = lax.all_to_all(
        summed.reshape(16, rows, HEAD_SIZE), ("zl", "c", "t"), 0, 0, tiled=True
    ).reshape(2, 2, 4, rows, HEAD_SIZE)
    weight_grad = jnp.sum(final.astype(jnp.float32), axis=(0, 2)) * unit_scale

    features = (
        lax.dot_general(cotan, weights, (((1,), (1,)), ((), ())), preferred_element_type=jnp.float32)
        * unit_scale
    )
    features = features.reshape(2, own_tokens, model_width)
    mine = jnp.where(core == 0, features[0], features[1])
    other = jnp.where(core == 0, features[1], features[0]).astype(bf)
    d_normed = mine + lax.ppermute(other, "c", [(0, 1), (1, 0)]).astype(jnp.float32)
    grad_x = norm_back(token_float, token_factor, d_normed).astype(bf)

    new_first = beta_one * key_value_first_moment + (1.0 - beta_one) * weight_grad
    new_second = beta_two * key_value_second_moment + (1.0 - beta_two) * weight_grad * weight_grad
    first_hat = new_first / (1.0 - beta_one**step_count)
    second_hat = new_second / (1.0 - beta_two**step_count)
    new_master = key_value_master_weight - learn_rate * (
        first_hat / (jnp.sqrt(second_hat) + adam_eps) + weight_decay * key_value_master_weight
    )
    replicas = writer.shape[0]
    flat_saved = new_master.astype(bf).reshape(replicas, -1)
    rank_ids = jnp.arange(replicas, dtype=jnp.int32)
    inverse = jnp.sum(jnp.where(writer[None, :] == rank_ids[:, None], rank_ids[None, :], 0), axis=1)
    saved = lax.all_to_all(flat_saved[inverse], ("zl", "x", "y", "c"), 0, 0, tiled=True)
    return (grad_x, grad_q, new_master, new_first, new_second, saved)


def solution(mesh):
    fine = Mesh(mesh.devices.reshape(2, 4, 4, 2, 4), ("zl", "x", "y", "c", "t"))
    dp = ("zl", "x", "y", "c")
    every = dp + ("t",)
    weight = P(None, dp, "t")
    return jax.shard_map(
        per_device,
        mesh=fine,
        in_specs=(P(every, None), P(dp, "t"), P(dp, "t"), weight, weight, weight, P()),
        out_specs=(P(every, None), P(dp, "t"), weight, weight, weight, P(dp, "t")),
        check_vma=False,
    )
```

```python
import functools
import math

import jax
import jax.numpy as jnp
from jax import lax
from jax.experimental import pallas as pl
from jax.experimental.pallas import tpu as pltpu
from jax.sharding import Mesh, PartitionSpec as P

HEAD_SIZE = 128


norm_eps = 1e-06
rope_base = 1000000.0
beta_one = 0.9
beta_two = 0.95
adam_eps = 1e-08
learn_rate = 0.02
weight_decay = 0.1
step_count = 10.0


def rope_tables(length, head_width):
    half_width = head_width // 2
    index_float = jnp.arange(half_width, dtype=jnp.float32)
    inverse_freq = rope_base ** (-2.0 * index_float / head_width)
    positions = jnp.arange(length, dtype=jnp.float32)
    angles = positions[:, None] * inverse_freq[None, :]
    return (jnp.cos(angles), jnp.sin(angles))


BF = jnp.bfloat16
F32 = jnp.float32
HALF = HEAD_SIZE // 2
PLACES = (0, -1, 1, 2)
NT = (((1,), (1,)), ((), ()))
TT = (((0,), (0,)), ((), ()))


def dot(left, right, dims=None):
    if dims is None:
        dims = (((1,), (0,)), ((), ()))
    return lax.dot_general(left, right, dims, preferred_element_type=F32)


def params(mebibytes=48):
    return pltpu.CompilerParams(vmem_limit_bytes=mebibytes * 1024 * 1024)


def norm_scale(field):
    return lax.rsqrt(jnp.mean(field * field, axis=-1, keepdims=True) + norm_eps)


def norm_back(field, factor, cotan):
    return factor * cotan - field * (factor * factor * factor) * jnp.mean(
        cotan * field, axis=-1, keepdims=True
    )


def turn(field, cosines, sines):
    return field * cosines + pltpu.roll(field, HALF, 1) * sines


def query_kernel(q_ref, cos_ref, sin_ref, out_ref):
    field = q_ref[...].astype(F32)
    out_ref[...] = turn(field * norm_scale(field), cos_ref[...], sin_ref[...]).astype(BF)


def rotated_queries(queries, cosines, sines):
    length, width = queries.shape
    column = pl.BlockSpec((length, HEAD_SIZE), lambda h: (0, h))
    table = pl.BlockSpec((length, HEAD_SIZE), lambda h: (0, 0))
    return pl.pallas_call(
        query_kernel,
        grid=(width // HEAD_SIZE,),
        in_specs=[column, table, table],
        out_specs=column,
        out_shape=jax.ShapeDtypeStruct(queries.shape, BF),
        compiler_params=params(),
        name="query_rope",
    )(queries, cosines, sines)


def permute_kernel(block, offset_ref, src_ref, out_ref):
    def step(k, carry):
        row = pl.multiple_of(offset_ref[k], 32)
        to = pl.multiple_of(k * block, 32)
        out_ref[pl.ds(to, block), :] = src_ref[pl.ds(row, block), :]
        return carry

    lax.fori_loop(0, src_ref.shape[0] // block, step, 0)


def permute_rows(src, offsets):
    block = src.shape[0] // offsets.shape[0]
    return pl.pallas_call(
        functools.partial(permute_kernel, block),
        in_specs=[
            pl.BlockSpec(memory_space=pltpu.SMEM),
            pl.BlockSpec(memory_space=pltpu.VMEM),
        ],
        out_specs=pl.BlockSpec(memory_space=pltpu.VMEM),
        out_shape=jax.ShapeDtypeStruct(src.shape, src.dtype),
        compiler_params=params(),
        name="permute_rows",
    )(offsets, src)


def project_kernel(scale, core_ref, acc_ref, x_ref, c1_ref, c2_ref, cos_ref, sin_ref, plain_ref, out_ref):
    depth = c1_ref.shape[0]
    plain = acc_ref[...] + dot(x_ref[:, :depth], c1_ref[...]) + dot(x_ref[:, depth:], c2_ref[...])
    plain = plain * scale
    plain_ref[...] = plain
    tokens = cos_ref.shape[0]
    is_key = core_ref[0] == 0
    for s in range(2):
        for h in range(4):
            u = plain[s * tokens : (s + 1) * tokens, h * HEAD_SIZE : (h + 1) * HEAD_SIZE]
            key = turn(u * norm_scale(u), cos_ref[...], sin_ref[...])
            out_ref[s, h] = jnp.where(is_key, key, u).astype(BF)


def project(core, acc, normed_last, c1, c2, cosines, sines, scale):
    tokens = cosines.shape[0]
    vmem = pl.BlockSpec(memory_space=pltpu.VMEM)
    return pl.pallas_call(
        functools.partial(project_kernel, scale),
        in_specs=[pl.BlockSpec(memory_space=pltpu.SMEM)] + [vmem] * 6,
        out_specs=[vmem, vmem],
        out_shape=[
            jax.ShapeDtypeStruct(acc.shape, F32),
            jax.ShapeDtypeStruct((2, 4, tokens, HEAD_SIZE), BF),
        ],
        compiler_params=params(),
        name="project",
    )(core, acc, normed_last, c1, c2, cosines, sines)


def attention_kernel(q_ref, g_ref, k_ref, v_ref, dkv_ref, ds0_ref, ds1_ref, dk_acc, dv_acc):
    head = pl.program_id(0)
    length = q_ref.shape[0]
    mid = length // 2
    scale = 1.0 / math.sqrt(HEAD_SIZE)

    @pl.when(head == 0)
    def _():
        dk_acc[...] = jnp.zeros_like(dk_acc)
        dv_acc[...] = jnp.zeros_like(dv_acc)

    q, g = q_ref[...], g_ref[...]
    k0, k1 = k_ref[:mid], k_ref[mid:]
    v0, v1 = v_ref[:mid], v_ref[mid:]
    row = lax.broadcasted_iota(jnp.int32, (mid, mid), 0)
    column = lax.broadcasted_iota(jnp.int32, (mid, mid), 1)
    allowed = row <= column
    e0 = jnp.exp(dot(k0, q, NT) * scale)
    e0a = jnp.where(allowed, e0[:, :mid], 0.0)
    e0b = e0[:, mid:]
    e1 = jnp.where(allowed, jnp.exp(dot(k1, q[mid:], NT) * scale), 0.0)
    inv_a = 1.0 / jnp.sum(e0a, axis=0, keepdims=True)
    inv_b = 1.0 / (jnp.sum(e0b, axis=0, keepdims=True) + jnp.sum(e1, axis=0, keepdims=True))
    p0a, p0b, p1 = e0a * inv_a, e0b * inv_b, e1 * inv_b
    g_a, g_b = g[:mid], g[mid:]
    dv_acc[:mid] += dot(p0a.astype(BF), g_a) + dot(p0b.astype(BF), g_b)
    dv_acc[mid:] += dot(p1.astype(BF), g_b)
    d0a, d0b, d1 = dot(v0, g_a, NT), dot(v0, g_b, NT), dot(v1, g_b, NT)
    sum_a = jnp.sum(p0a * d0a, axis=0, keepdims=True)
    sum_b = jnp.sum(p0b * d0b, axis=0, keepdims=True) + jnp.sum(p1 * d1, axis=0, keepdims=True)
    s0a = (p0a * (d0a - sum_a)).astype(BF)
    s0b = (p0b * (d0b - sum_b)).astype(BF)
    s1 = (p1 * (d1 - sum_b)).astype(BF)
    ds0_ref[0, :, :mid] = s0a
    ds0_ref[0, :, mid:] = s0b
    ds1_ref[0] = s1
    dk_acc[:mid] += dot(s0a, q[:mid]) + dot(s0b, q[mid:])
    dk_acc[mid:] += dot(s1, q[mid:])

    @pl.when(head == pl.num_programs(0) - 1)
    def _():
        dkv_ref[0] = (dk_acc[...] * scale).astype(BF)
        dkv_ref[1] = dv_acc[...].astype(BF)


def attention(rotated, incoming, key, value):
    length, width = rotated.shape
    heads, mid = width // HEAD_SIZE, length // 2
    column = pl.BlockSpec((length, HEAD_SIZE), lambda h: (0, h))
    whole = pl.BlockSpec((length, HEAD_SIZE), lambda h: (0, 0))
    return pl.pallas_call(
        attention_kernel,
        grid=(heads,),
        in_specs=[column, column, whole, whole],
        out_specs=[
            pl.BlockSpec((2, length, HEAD_SIZE), lambda h: (0, 0, 0)),
            pl.BlockSpec((1, mid, length), lambda h: (h, 0, 0)),
            pl.BlockSpec((1, mid, mid), lambda h: (h, 0, 0)),
        ],
        out_shape=[
            jax.ShapeDtypeStruct((2, length, HEAD_SIZE), BF),
            jax.ShapeDtypeStruct((heads, mid, length), BF),
            jax.ShapeDtypeStruct((heads, mid, mid), BF),
        ],
        scratch_shapes=[pltpu.VMEM((length, HEAD_SIZE), F32)] * 2,
        compiler_params=params(),
        name="attention",
    )(rotated, incoming, key, value)


def grad_query_kernel(q_ref, k_ref, ds0_ref, ds1_ref, cos_ref, sin_ref, out_ref):
    mid = ds0_ref.shape[1]
    scale = 1.0 / math.sqrt(HEAD_SIZE)
    k0, k1 = k_ref[:mid], k_ref[mid:]
    both = dot(k0, ds0_ref[0], TT)
    early = both[:, :mid]
    late = both[:, mid:] + dot(k1, ds1_ref[0], TT)
    cotan = jnp.concatenate([early.T, late.T], axis=0) * scale
    field = q_ref[...].astype(F32)
    cotan = turn(cotan, cos_ref[...], -sin_ref[...])
    out_ref[...] = norm_back(field, norm_scale(field), cotan).astype(BF)


def grad_queries(queries, key, ds0, ds1, cosines, sines):
    length, width = queries.shape
    heads, mid = width // HEAD_SIZE, length // 2
    column = pl.BlockSpec((length, HEAD_SIZE), lambda h: (0, h))
    whole = pl.BlockSpec((length, HEAD_SIZE), lambda h: (0, 0))
    return pl.pallas_call(
        grad_query_kernel,
        grid=(heads,),
        in_specs=[
            column,
            whole,
            pl.BlockSpec((1, mid, length), lambda h: (h, 0, 0)),
            pl.BlockSpec((1, mid, mid), lambda h: (h, 0, 0)),
            whole,
            whole,
        ],
        out_specs=column,
        out_shape=jax.ShapeDtypeStruct(queries.shape, BF),
        compiler_params=params(),
        name="grad_query",
    )(queries, key, ds0, ds1, cosines, sines)


def cotan_kernel(core_ref, back_ref, plain_ref, cos_ref, sin_ref, out_ref):
    tokens = cos_ref.shape[0]
    is_key = core_ref[0] == 0
    for s in range(2):
        for h in range(4):
            rows = slice(s * tokens, (s + 1) * tokens)
            columns = slice(h * HEAD_SIZE, (h + 1) * HEAD_SIZE)
            back = back_ref[s, h].astype(F32)
            u = plain_ref[rows, columns]
            key = norm_back(u, norm_scale(u), turn(back, cos_ref[...], -sin_ref[...]))
            out_ref[rows, columns] = jnp.where(is_key, key, back).astype(BF)


def key_value_cotan(core, back, plain, cosines, sines):
    vmem = pl.BlockSpec(memory_space=pltpu.VMEM)
    return pl.pallas_call(
        cotan_kernel,
        in_specs=[pl.BlockSpec(memory_space=pltpu.SMEM)] + [vmem] * 4,
        out_specs=vmem,
        out_shape=jax.ShapeDtypeStruct(plain.shape, BF),
        compiler_params=params(),
        name="key_value_cotan",
    )(core, back, plain, cosines, sines)


def feature_kernel(scale, block, offset_ref, w_ref, mine_ref, other_ref, kept_ref, sent_ref):
    def step(k, carry):
        row = pl.multiple_of(offset_ref[k], 32)
        weights = w_ref[pl.ds(pl.multiple_of(k * block, 32), block), :]
        kept_ref[pl.ds(row, block), :] = dot(weights, mine_ref[...], NT) * scale
        sent_ref[pl.ds(row, block), :] = (dot(weights, other_ref[...], NT) * scale).astype(BF)
        return carry

    lax.fori_loop(0, offset_ref.shape[0], step, 0)


def features_of(offsets, weights, mine, other, scale):
    vmem = pl.BlockSpec(memory_space=pltpu.VMEM)
    rows = weights.shape[0]
    return pl.pallas_call(
        functools.partial(feature_kernel, scale, rows // offsets.shape[0]),
        in_specs=[pl.BlockSpec(memory_space=pltpu.SMEM)] + [vmem] * 3,
        out_specs=[vmem, vmem],
        out_shape=[
            jax.ShapeDtypeStruct((rows, mine.shape[0]), F32),
            jax.ShapeDtypeStruct((rows, mine.shape[0]), BF),
        ],
        compiler_params=params(),
        name="features",
    )(offsets, weights, mine, other)


def plane_pairs(first, step):
    pairs = []
    for x in range(4):
        for y in range(4):
            for c in range(2):
                along_x = (c == 0) == first
                to_x = (x + step) % 4 if along_x else x
                to_y = y if along_x else (y + step) % 4
                pairs.append(((x * 4 + y) * 2 + c, (to_x * 4 + to_y) * 2 + c))
    return pairs


def far(block, step):
    return lax.ppermute(block, ("x", "y", "c"), plane_pairs(True, step))


def near(block, step):
    return lax.ppermute(block, ("x", "y", "c"), plane_pairs(False, step))


def swap_cores(block):
    return lax.ppermute(block, "c", [(0, 1), (1, 0)])


def per_device(
    tokens,
    queries,
    grad_out,
    key_value_master_weight,
    key_value_first_moment,
    key_value_second_moment,
    writer,
):
    own_tokens, model_width = tokens.shape
    unit_scale = 1.0 / math.sqrt(model_width)
    length = queries.shape[0]
    rows = key_value_master_weight.shape[1]
    columns = 4 * HEAD_SIZE
    core = lax.axis_index("c")
    core_word = core.reshape(1).astype(jnp.int32)
    x_index, y_index = lax.axis_index("x"), lax.axis_index("y")
    t_index = lax.axis_index("t")

    outgoing = jnp.broadcast_to(
        key_value_master_weight.astype(BF)[None, :, None], (2, 2, 4, rows, HEAD_SIZE)
    ).reshape(16, rows, HEAD_SIZE)
    stage = lax.all_to_all(outgoing, ("zl", "c", "t"), 0, 0, tiled=True)
    stage = jnp.transpose(stage.reshape(2, 2, 4, rows, HEAD_SIZE), (0, 1, 3, 2, 4))
    stage = stage.reshape(4 * rows, columns)
    shard = jnp.concatenate([stage, near(stage, 1), near(stage, -1), near(stage, 2)], axis=0)
    cut = shard.shape[0] // 2
    top, bottom = shard[:cut], shard[cut:]
    a1, b2 = far(top, 1), far(bottom, -1)
    a2, b1 = far(bottom, 1), far(top, -1)
    c1, c2 = far(a1, 1), far(b2, -1)

    place = jnp.array(PLACES, jnp.int32)
    far_place = (jnp.where(core == 0, x_index, y_index) + place) % 4
    near_place = (jnp.where(core == 0, y_index, x_index) + place) % 4
    block = 2 * rows
    far_step = jnp.where(core == 0, 4 * block, block)
    near_step = jnp.where(core == 0, block, 4 * block)
    offsets = (
        far_place[:, None, None] * far_step
        + near_place[None, :, None] * near_step
        + jnp.arange(2, dtype=jnp.int32)[None, None, :] * (16 * block)
    )
    offsets = offsets.reshape(32).astype(jnp.int32)

    token_float = tokens.astype(F32)
    token_factor = norm_scale(token_float)
    normed_local = (token_float * token_factor).astype(BF)
    normed_other = swap_cores(normed_local)
    first = jnp.where(core == 0, normed_local, normed_other)
    second = jnp.where(core == 0, normed_other, normed_local)
    normed = jnp.concatenate([first, second], axis=0)
    turned = permute_rows(jnp.transpose(normed), offsets)
    normed = jnp.transpose(turned)

    cosines, sines = rope_tables(length, HEAD_SIZE)
    cosines = jnp.concatenate([cosines, cosines], axis=1)
    sines = jnp.concatenate([-sines, sines], axis=1)
    own_cos = lax.dynamic_slice_in_dim(cosines, t_index * own_tokens, own_tokens, 0)
    own_sin = lax.dynamic_slice_in_dim(sines, t_index * own_tokens, own_tokens, 0)
    rotated = rotated_queries(queries, cosines, sines)

    pieces = [shard, a1, a2, b1, b2]
    acc, at = 0.0, 0
    for piece in pieces:
        acc = acc + dot(normed[:, at : at + piece.shape[0]], piece)
        at += piece.shape[0]
    plain, projected = project(
        core_word, acc, normed[:, at:], c1, c2, own_cos, own_sin, unit_scale
    )
    arrived = lax.all_to_all(
        projected.reshape(8, own_tokens, HEAD_SIZE), ("c", "t"), 0, 0, tiled=True
    )
    arrived = arrived.reshape(2, length, HEAD_SIZE)
    key, value = arrived[0], arrived[1]

    returning, ds0, ds1 = attention(rotated, grad_out, key, value)
    back = lax.all_to_all(
        returning.reshape(8, own_tokens, HEAD_SIZE), ("c", "t"), 0, 0, tiled=True
    )
    cotan = key_value_cotan(
        core_word, back.reshape(2, 4, own_tokens, HEAD_SIZE), plain, own_cos, own_sin
    )

    quarter = 2 * cut
    part = [
        dot(turned[i * quarter : (i + 1) * quarter], cotan).astype(BF) for i in range(4)
    ]
    r1, r2 = far(part[3][:cut], 1), far(part[3][cut:], -1)
    s2, s1 = far(part[2][cut:], 1), far(part[1][:cut], -1)
    d1 = (part[2][:cut].astype(F32) + r1.astype(F32)).astype(BF)
    d2 = (part[1][cut:].astype(F32) + r2.astype(F32)).astype(BF)
    e1, e2 = far(d1, 1), far(d2, -1)
    own_top = part[0][:cut].astype(F32) + s1.astype(F32) + e1.astype(F32)
    own_bottom = part[0][cut:].astype(F32) + s2.astype(F32) + e2.astype(F32)
    own = jnp.concatenate([own_top, own_bottom], axis=0).astype(BF).reshape(4, 4 * rows, columns)
    summed = own[0].astype(F32)
    for index, step in ((1, -1), (2, 1), (3, 2)):
        summed = summed + near(own[index], step).astype(F32)
    summed = jnp.transpose(summed.astype(BF).reshape(2, 2, rows, 4, HEAD_SIZE), (0, 1, 3, 2, 4))
    final = lax.all_to_all(
        summed.reshape(16, rows, HEAD_SIZE), ("zl", "c", "t"), 0, 0, tiled=True
    ).reshape(2, 2, 4, rows, HEAD_SIZE)
    weight_grad = jnp.sum(final.astype(F32), axis=(0, 2)) * unit_scale

    grad_q = grad_queries(queries, key, ds0, ds1, cosines, sines)

    weights = jnp.concatenate([shard, a1, a2, b1, b2, c1, c2], axis=0)
    mine = jnp.where(core == 0, cotan[:own_tokens], cotan[own_tokens:])
    other = jnp.where(core == 0, cotan[own_tokens:], cotan[:own_tokens])
    kept, sent = features_of(offsets, weights, mine, other, unit_scale)
    d_normed = jnp.transpose(kept + swap_cores(sent).astype(F32))
    grad_x = norm_back(token_float, token_factor, d_normed).astype(BF)

    new_first = beta_one * key_value_first_moment + (1.0 - beta_one) * weight_grad
    new_second = beta_two * key_value_second_moment + (1.0 - beta_two) * weight_grad * weight_grad
    first_hat = new_first / (1.0 - beta_one**step_count)
    second_hat = new_second / (1.0 - beta_two**step_count)
    new_master = key_value_master_weight - learn_rate * (
        first_hat / (jnp.sqrt(second_hat) + adam_eps) + weight_decay * key_value_master_weight
    )
    replicas = writer.shape[0]
    flat_saved = new_master.astype(BF).reshape(replicas, -1)
    rank_ids = jnp.arange(replicas, dtype=jnp.int32)
    inverse = jnp.sum(jnp.where(writer[None, :] == rank_ids[:, None], rank_ids[None, :], 0), axis=1)
    saved = lax.all_to_all(flat_saved[inverse], ("zl", "x", "y", "c"), 0, 0, tiled=True)
    return (grad_x, grad_q, new_master, new_first, new_second, saved)


def solution(mesh):
    fine = Mesh(mesh.devices.reshape(2, 4, 4, 2, 4), ("zl", "x", "y", "c", "t"))
    dp = ("zl", "x", "y", "c")
    every = dp + ("t",)
    weight = P(None, dp, "t")
    return jax.shard_map(
        per_device,
        mesh=fine,
        in_specs=(P(every, None), P(dp, "t"), P(dp, "t"), weight, weight, weight, P()),
        out_specs=(P(every, None), P(dp, "t"), weight, weight, weight, P(dp, "t")),
        check_vma=False,
    )
```

```python
import functools
import math

import jax
import jax.numpy as jnp
from jax import lax
from jax.experimental import pallas as pl
from jax.experimental.pallas import tpu as pltpu
from jax.sharding import Mesh, PartitionSpec as P

HEAD_SIZE = 128


norm_eps = 1e-06
rope_base = 1000000.0
beta_one = 0.9
beta_two = 0.95
adam_eps = 1e-08
learn_rate = 0.02
weight_decay = 0.1
step_count = 10.0


def rope_tables(length, head_width):
    half_width = head_width // 2
    index_float = jnp.arange(half_width, dtype=jnp.float32)
    inverse_freq = rope_base ** (-2.0 * index_float / head_width)
    positions = jnp.arange(length, dtype=jnp.float32)
    angles = positions[:, None] * inverse_freq[None, :]
    return (jnp.cos(angles), jnp.sin(angles))


BF = jnp.bfloat16
F32 = jnp.float32
HALF = HEAD_SIZE // 2
PLACES = (0, -1, 1, 2)
NT = (((1,), (1,)), ((), ()))
TT = (((0,), (0,)), ((), ()))


def dot(left, right, dims=None):
    if dims is None:
        dims = (((1,), (0,)), ((), ()))
    return lax.dot_general(left, right, dims, preferred_element_type=F32)


def params(mebibytes=48):
    return pltpu.CompilerParams(vmem_limit_bytes=mebibytes * 1024 * 1024)


def norm_scale(field):
    return lax.rsqrt(jnp.mean(field * field, axis=-1, keepdims=True) + norm_eps)


def norm_back(field, factor, cotan):
    return factor * cotan - field * (factor * factor * factor) * jnp.mean(
        cotan * field, axis=-1, keepdims=True
    )


def turn(field, cosines, sines):
    return field * cosines + pltpu.roll(field, HALF, 1) * sines


def query_kernel(q_ref, cos_ref, sin_ref, out_ref):
    field = q_ref[...].astype(F32)
    out_ref[...] = turn(field * norm_scale(field), cos_ref[...], sin_ref[...]).astype(BF)


def rotated_queries(queries, cosines, sines):
    length, width = queries.shape
    column = pl.BlockSpec((length, HEAD_SIZE), lambda h: (0, h))
    table = pl.BlockSpec((length, HEAD_SIZE), lambda h: (0, 0))
    return pl.pallas_call(
        query_kernel,
        grid=(width // HEAD_SIZE,),
        in_specs=[column, table, table],
        out_specs=column,
        out_shape=jax.ShapeDtypeStruct(queries.shape, BF),
        compiler_params=params(),
        name="query_rope",
    )(queries, cosines, sines)


def permute_kernel(block, offset_ref, early_ref, late_ref, out_ref):
    width = early_ref.shape[1]

    def step(k, carry):
        row = pl.multiple_of(offset_ref[k], 16)
        to = pl.multiple_of(k * block, 16)
        out_ref[pl.ds(to, block), :width] = early_ref[pl.ds(row, block), :]
        out_ref[pl.ds(to, block), width:] = late_ref[pl.ds(row, block), :]
        return carry

    lax.fori_loop(0, early_ref.shape[0] // block, step, 0)


def permute_rows(early, late, offsets):
    rows, width = early.shape
    vmem = pl.BlockSpec(memory_space=pltpu.VMEM)
    return pl.pallas_call(
        functools.partial(permute_kernel, rows // offsets.shape[0]),
        in_specs=[pl.BlockSpec(memory_space=pltpu.SMEM), vmem, vmem],
        out_specs=vmem,
        out_shape=jax.ShapeDtypeStruct((rows, 2 * width), early.dtype),
        compiler_params=params(),
        name="permute_rows",
    )(offsets, early, late)


def project_kernel(scale, order_ref, acc_ref, x_ref, c1_ref, c2_ref, cos_ref, sin_ref, plain_ref, *out_refs):
    depth = c1_ref.shape[0]
    plain = acc_ref[...] + dot(x_ref[:, :depth], c1_ref[...]) + dot(x_ref[:, depth:], c2_ref[...])
    plain_ref[...] = plain * scale
    tokens = cos_ref.shape[0]
    for k in range(4):
        rows = pl.ds(pl.multiple_of(order_ref[k] * tokens, tokens), tokens)
        u = plain_ref[rows, :HEAD_SIZE]
        out_refs[k][0] = turn(u * norm_scale(u), cos_ref[...], sin_ref[...]).astype(BF)
        out_refs[k][1] = plain_ref[rows, HEAD_SIZE:].astype(BF)


def project(order, acc, normed_last, c1, c2, cosines, sines, scale):
    tokens = cosines.shape[0]
    vmem = pl.BlockSpec(memory_space=pltpu.VMEM)
    result = pl.pallas_call(
        functools.partial(project_kernel, scale),
        in_specs=[pl.BlockSpec(memory_space=pltpu.SMEM)] + [vmem] * 6,
        out_specs=[vmem] * 5,
        out_shape=[jax.ShapeDtypeStruct(acc.shape, F32)]
        + [jax.ShapeDtypeStruct((2, tokens, HEAD_SIZE), BF)] * 4,
        compiler_params=params(),
        name="project",
    )(order, acc, normed_last, c1, c2, cosines, sines)
    return result[0], result[1:]


def attention_kernel(order_ref, q_ref, g_ref, *refs):
    kv_refs, dkv_refs = refs[:4], refs[4:8]
    k_ref, ds0_ref, ds1_ref, v_ref, dk_acc, dv_acc = refs[8:]
    head = pl.program_id(0)
    length = q_ref.shape[0]
    tokens = length // 4
    mid = length // 2
    scale = 1.0 / math.sqrt(HEAD_SIZE)

    @pl.when(head == 0)
    def _():
        dk_acc[...] = jnp.zeros_like(dk_acc)
        dv_acc[...] = jnp.zeros_like(dv_acc)
        for k in range(4):
            rows = pl.ds(pl.multiple_of(order_ref[k] * tokens, tokens), tokens)
            k_ref[rows, :] = kv_refs[k][0]
            v_ref[rows, :] = kv_refs[k][1]

    q, g = q_ref[...], g_ref[...]
    k0, k1 = k_ref[:mid], k_ref[mid:]
    v0, v1 = v_ref[:mid], v_ref[mid:]
    row = lax.broadcasted_iota(jnp.int32, (mid, mid), 0)
    column = lax.broadcasted_iota(jnp.int32, (mid, mid), 1)
    allowed = row <= column
    e0 = jnp.exp(dot(k0, q, NT) * scale)
    e0a = jnp.where(allowed, e0[:, :mid], 0.0)
    e0b = e0[:, mid:]
    e1 = jnp.where(allowed, jnp.exp(dot(k1, q[mid:], NT) * scale), 0.0)
    inv_a = 1.0 / jnp.sum(e0a, axis=0, keepdims=True)
    inv_b = 1.0 / (jnp.sum(e0b, axis=0, keepdims=True) + jnp.sum(e1, axis=0, keepdims=True))
    p0a, p0b, p1 = e0a * inv_a, e0b * inv_b, e1 * inv_b
    g_a, g_b = g[:mid], g[mid:]
    dv_acc[:mid] += dot(p0a.astype(BF), g_a) + dot(p0b.astype(BF), g_b)
    dv_acc[mid:] += dot(p1.astype(BF), g_b)
    d0a, d0b, d1 = dot(v0, g_a, NT), dot(v0, g_b, NT), dot(v1, g_b, NT)
    sum_a = jnp.sum(p0a * d0a, axis=0, keepdims=True)
    sum_b = jnp.sum(p0b * d0b, axis=0, keepdims=True) + jnp.sum(p1 * d1, axis=0, keepdims=True)
    s0a = (p0a * (d0a - sum_a)).astype(BF)
    s0b = (p0b * (d0b - sum_b)).astype(BF)
    s1 = (p1 * (d1 - sum_b)).astype(BF)
    ds0_ref[0, :, :mid] = s0a
    ds0_ref[0, :, mid:] = s0b
    ds1_ref[0] = s1
    dk_acc[:mid] += dot(s0a, q[:mid]) + dot(s0b, q[mid:])
    dk_acc[mid:] += dot(s1, q[mid:])

    @pl.when(head == pl.num_programs(0) - 1)
    def _():
        for k in range(4):
            rows = pl.ds(pl.multiple_of(order_ref[k] * tokens, tokens), tokens)
            dkv_refs[k][0] = (dk_acc[rows, :] * scale).astype(BF)
            dkv_refs[k][1] = dv_acc[rows, :].astype(BF)


def attention(order, rotated, incoming, pieces):
    length, width = rotated.shape
    heads, mid = width // HEAD_SIZE, length // 2
    column = pl.BlockSpec((length, HEAD_SIZE), lambda h: (0, h))
    whole = pl.BlockSpec((length, HEAD_SIZE), lambda h: (0, 0))
    piece = pl.BlockSpec(pieces[0].shape, lambda h: (0, 0, 0))
    result = pl.pallas_call(
        attention_kernel,
        grid=(heads,),
        in_specs=[pl.BlockSpec(memory_space=pltpu.SMEM), column, column] + [piece] * 4,
        out_specs=[piece] * 4
        + [
            whole,
            pl.BlockSpec((1, mid, length), lambda h: (h, 0, 0)),
            pl.BlockSpec((1, mid, mid), lambda h: (h, 0, 0)),
        ],
        out_shape=[jax.ShapeDtypeStruct(pieces[0].shape, BF)] * 4
        + [
            jax.ShapeDtypeStruct((length, HEAD_SIZE), BF),
            jax.ShapeDtypeStruct((heads, mid, length), BF),
            jax.ShapeDtypeStruct((heads, mid, mid), BF),
        ],
        scratch_shapes=[pltpu.VMEM((length, HEAD_SIZE), BF)]
        + [pltpu.VMEM((length, HEAD_SIZE), F32)] * 2,
        compiler_params=params(60),
        name="attention",
    )(order, rotated, incoming, *pieces)
    return result[:4], result[4], result[5], result[6]


def grad_query_kernel(q_ref, k_ref, ds0_ref, ds1_ref, cos_ref, sin_ref, out_ref):
    mid = ds0_ref.shape[1]
    scale = 1.0 / math.sqrt(HEAD_SIZE)
    k0, k1 = k_ref[:mid], k_ref[mid:]
    both = dot(k0, ds0_ref[0], TT)
    early = both[:, :mid]
    late = both[:, mid:] + dot(k1, ds1_ref[0], TT)
    cotan = jnp.concatenate([early.T, late.T], axis=0) * scale
    field = q_ref[...].astype(F32)
    cotan = turn(cotan, cos_ref[...], -sin_ref[...])
    out_ref[...] = norm_back(field, norm_scale(field), cotan).astype(BF)


def grad_queries(queries, key, ds0, ds1, cosines, sines):
    length, width = queries.shape
    heads, mid = width // HEAD_SIZE, length // 2
    column = pl.BlockSpec((length, HEAD_SIZE), lambda h: (0, h))
    whole = pl.BlockSpec((length, HEAD_SIZE), lambda h: (0, 0))
    return pl.pallas_call(
        grad_query_kernel,
        grid=(heads,),
        in_specs=[
            column,
            whole,
            pl.BlockSpec((1, mid, length), lambda h: (h, 0, 0)),
            pl.BlockSpec((1, mid, mid), lambda h: (h, 0, 0)),
            whole,
            whole,
        ],
        out_specs=column,
        out_shape=jax.ShapeDtypeStruct(queries.shape, BF),
        compiler_params=params(60),
        name="grad_query",
    )(queries, key, ds0, ds1, cosines, sines)


def cotan_kernel(order_ref, b0_ref, b1_ref, b2_ref, b3_ref, plain_ref, cos_ref, sin_ref, out_ref):
    tokens = cos_ref.shape[0]
    for k, back_ref in enumerate((b0_ref, b1_ref, b2_ref, b3_ref)):
        rows = pl.ds(pl.multiple_of(order_ref[k] * tokens, tokens), tokens)
        u = plain_ref[rows, :HEAD_SIZE]
        back = turn(back_ref[0].astype(F32), cos_ref[...], -sin_ref[...])
        out_ref[rows, :HEAD_SIZE] = norm_back(u, norm_scale(u), back).astype(BF)
        out_ref[rows, HEAD_SIZE:] = back_ref[1]


def key_value_cotan(order, back, plain, cosines, sines):
    vmem = pl.BlockSpec(memory_space=pltpu.VMEM)
    return pl.pallas_call(
        cotan_kernel,
        in_specs=[pl.BlockSpec(memory_space=pltpu.SMEM)] + [vmem] * 7,
        out_specs=vmem,
        out_shape=jax.ShapeDtypeStruct(plain.shape, BF),
        compiler_params=params(),
        name="key_value_cotan",
    )(order, *back, plain, cosines, sines)


def feature_kernel(scale, block, offset_ref, cotan_ref, *refs):
    w_refs = refs[:-4]
    kept_ref, near_ref, sent_ref, scratch = refs[-4:]
    tokens = kept_ref.shape[1]
    cotan = cotan_ref[...]
    at = 0
    for w_ref in w_refs:
        rows = w_ref.shape[0]
        scratch[:rows] = dot(w_ref[...], cotan, NT) * scale

        def step(k, carry, at=at):
            row = pl.ds(pl.multiple_of(offset_ref[at + k], 16), block)
            got = scratch[pl.ds(pl.multiple_of(k * block, 16), block), :]
            kept_ref[row, :] = got[:, :tokens]
            sent_ref[row, :tokens] = got[:, tokens : 2 * tokens].astype(BF)
            near_ref[row, :] = got[:, 2 * tokens : 3 * tokens].astype(BF)
            sent_ref[row, tokens:] = got[:, 3 * tokens :].astype(BF)
            return carry

        lax.fori_loop(0, rows // block, step, 0)
        at += rows // block


def features_of(offsets, cotan, pieces, scale):
    vmem = pl.BlockSpec(memory_space=pltpu.VMEM)
    rows = sum(piece.shape[0] for piece in pieces)
    tokens = cotan.shape[0] // 4
    return pl.pallas_call(
        functools.partial(feature_kernel, scale, rows // offsets.shape[0]),
        in_specs=[pl.BlockSpec(memory_space=pltpu.SMEM)] + [vmem] * (1 + len(pieces)),
        out_specs=[vmem] * 3,
        out_shape=[
            jax.ShapeDtypeStruct((rows, tokens), F32),
            jax.ShapeDtypeStruct((rows, tokens), BF),
            jax.ShapeDtypeStruct((rows, 2 * tokens), BF),
        ],
        scratch_shapes=[
            pltpu.VMEM((max(piece.shape[0] for piece in pieces), cotan.shape[0]), F32)
        ],
        compiler_params=params(),
        name="features",
    )(offsets, cotan, *pieces)


def plane_pairs(first, step):
    pairs = []
    for x in range(4):
        for y in range(4):
            for c in range(2):
                along_x = (c == 0) == first
                to_x = (x + step) % 4 if along_x else x
                to_y = y if along_x else (y + step) % 4
                pairs.append(((x * 4 + y) * 2 + c, (to_x * 4 + to_y) * 2 + c))
    return pairs


def far(block, step):
    return lax.ppermute(block, ("x", "y", "c"), plane_pairs(True, step))


def near(block, step):
    return lax.ppermute(block, ("x", "y", "c"), plane_pairs(False, step))


def swap_cores(block):
    return lax.ppermute(block, "c", [(0, 1), (1, 0)])


def group_pairs(target):
    pairs = []
    for g in range(4):
        for t in range(4):
            to_g, to_t = target(g, t)
            pairs.append((g * 4 + t, (to_g % 4) * 4 + to_t % 4))
    return pairs


def to_heads(block, k):
    return lax.ppermute(block, ("zl", "c", "t"), group_pairs(lambda g, t: (t, g + k)))


def from_heads(block, k):
    return lax.ppermute(block, ("zl", "c", "t"), group_pairs(lambda g, t: (t + k, g)))


def swap_layers(block):
    return lax.ppermute(block, "zl", [(0, 1), (1, 0)])


def normed_turned(first, second):
    field = jnp.concatenate([first, second], axis=0).astype(F32)
    return jnp.transpose((field * norm_scale(field)).astype(BF))


def per_device(
    tokens,
    queries,
    grad_out,
    key_value_master_weight,
    key_value_first_moment,
    key_value_second_moment,
    writer,
):
    own_tokens, model_width = tokens.shape
    unit_scale = 1.0 / math.sqrt(model_width)
    length = queries.shape[0]
    rows = key_value_master_weight.shape[1]
    core = lax.axis_index("c")
    x_index, y_index = lax.axis_index("x"), lax.axis_index("y")
    t_index = lax.axis_index("t")
    g_index = 2 * lax.axis_index("zl") + core

    from_z = swap_layers(tokens)
    own_weight = key_value_master_weight.astype(BF)
    own_weight = jnp.concatenate([own_weight[0], own_weight[1]], axis=1)
    stage = jnp.concatenate([to_heads(own_weight, k) for k in range(4)], axis=0)
    shard = jnp.concatenate([stage, near(stage, 1), near(stage, -1), near(stage, 2)], axis=0)
    cut = shard.shape[0] // 2
    top, bottom = shard[:cut], shard[cut:]
    a1, b2 = far(top, 1), far(bottom, -1)
    a1, b2, top, bottom = lax.optimization_barrier((a1, b2, top, bottom))
    c1, c2 = far(a1, 1), far(b2, -1)
    a2, b1 = far(bottom, 1), far(top, -1)

    place = jnp.array(PLACES, jnp.int32)
    count = jnp.arange(4, dtype=jnp.int32)
    far_place = (jnp.where(core == 0, x_index, y_index) + place) % 4
    near_place = (jnp.where(core == 0, y_index, x_index) + place) % 4
    far_step = jnp.where(core == 0, 8 * rows, 2 * rows)
    near_step = jnp.where(core == 0, 2 * rows, 8 * rows)
    source = (t_index - count) % 4
    offsets = (
        far_place[:, None, None] * far_step
        + near_place[None, :, None] * near_step
        + ((source // 2) * (32 * rows) + (source % 2) * rows)[None, None, :]
    )
    offsets = offsets.reshape(64).astype(jnp.int32)
    sequence_order = ((t_index + count) % 4) ^ g_index
    block_order = (g_index - count) % 4

    early = normed_turned(tokens, swap_cores(tokens))
    late = normed_turned(from_z, swap_cores(from_z))
    turned = permute_rows(early, late, offsets)
    normed = jnp.transpose(turned)

    cosines, sines = rope_tables(length, HEAD_SIZE)
    cosines = jnp.concatenate([cosines, cosines], axis=1)
    sines = jnp.concatenate([-sines, sines], axis=1)
    own_cos = lax.dynamic_slice_in_dim(cosines, t_index * own_tokens, own_tokens, 0)
    own_sin = lax.dynamic_slice_in_dim(sines, t_index * own_tokens, own_tokens, 0)
    rotated = rotated_queries(queries, cosines, sines)

    pieces = [shard, a1, a2, b1, b2]
    acc, at = 0.0, 0
    for piece in pieces:
        acc = acc + dot(normed[:, at : at + piece.shape[0]], piece)
        at += piece.shape[0]
    plain, projected = project(
        sequence_order, acc, normed[:, at:], c1, c2, own_cos, own_sin, unit_scale
    )
    arrived = [from_heads(block, k) for k, block in enumerate(projected)]
    returning, key, ds0, ds1 = attention(block_order, rotated, grad_out, arrived)
    back = [to_heads(block, -k) for k, block in enumerate(returning)]
    cotan = key_value_cotan(sequence_order, back, plain, own_cos, own_sin)

    quarter = 2 * cut
    part = [dot(turned[i * quarter : (i + 1) * quarter], cotan).astype(BF) for i in range(4)]
    r1, r2 = far(part[3][:cut], 1), far(part[3][cut:], -1)
    d1 = (part[2][:cut].astype(F32) + r1.astype(F32)).astype(BF)
    d2 = (part[1][cut:].astype(F32) + r2.astype(F32)).astype(BF)
    s2, s1 = far(part[2][cut:], 1), far(part[1][:cut], -1)
    e1, e2 = far(d1, 1), far(d2, -1)
    own_top = part[0][:cut].astype(F32) + s1.astype(F32) + e1.astype(F32)
    own_bottom = part[0][cut:].astype(F32) + s2.astype(F32) + e2.astype(F32)
    own = jnp.concatenate([own_top, own_bottom], axis=0).astype(BF).reshape(4, 4 * rows, -1)
    summed = own[0].astype(F32)
    for index, step in ((1, -1), (2, 1), (3, 2)):
        summed = summed + near(own[index], step).astype(F32)
    summed = summed.astype(BF).reshape(4, rows, 2 * HEAD_SIZE)
    final = sum(from_heads(summed[k], -k).astype(F32) for k in range(4)) * unit_scale
    weight_grad = jnp.stack([final[:, :HEAD_SIZE], final[:, HEAD_SIZE:]], axis=0)

    grad_q = grad_queries(queries, key, ds0, ds1, cosines, sines)

    kept, kept_z, sent = features_of(
        offsets, cotan, [shard, a1, a2, b1, b2, c1, c2], unit_scale
    )
    swapped = swap_cores(sent).astype(F32)
    to_z = (kept_z.astype(F32) + swapped[:, own_tokens:]).astype(BF)
    d_normed = kept + swapped[:, :own_tokens] + swap_layers(to_z).astype(F32)
    token_float = tokens.astype(F32)
    grad_x = norm_back(token_float, norm_scale(token_float), jnp.transpose(d_normed)).astype(BF)

    new_first = beta_one * key_value_first_moment + (1.0 - beta_one) * weight_grad
    new_second = beta_two * key_value_second_moment + (1.0 - beta_two) * weight_grad * weight_grad
    first_hat = new_first / (1.0 - beta_one**step_count)
    second_hat = new_second / (1.0 - beta_two**step_count)
    new_master = key_value_master_weight - learn_rate * (
        first_hat / (jnp.sqrt(second_hat) + adam_eps) + weight_decay * key_value_master_weight
    )
    replicas = writer.shape[0]
    flat_saved = new_master.astype(BF).reshape(replicas, -1)
    rank_ids = jnp.arange(replicas, dtype=jnp.int32)
    inverse = jnp.sum(jnp.where(writer[None, :] == rank_ids[:, None], rank_ids[None, :], 0), axis=1)
    saved = lax.all_to_all(flat_saved[inverse], ("zl", "x", "y", "c"), 0, 0, tiled=True)
    return (grad_x, grad_q, new_master, new_first, new_second, saved)


def solution(mesh):
    fine = Mesh(mesh.devices.reshape(2, 4, 4, 2, 4), ("zl", "x", "y", "c", "t"))
    dp = ("zl", "x", "y", "c")
    every = dp + ("t",)
    weight = P(None, dp, "t")
    return jax.shard_map(
        per_device,
        mesh=fine,
        in_specs=(P(every, None), P(dp, "t"), P(dp, "t"), weight, weight, weight, P()),
        out_specs=(P(every, None), P(dp, "t"), weight, weight, weight, P(dp, "t")),
        check_vma=False,
    )
```

```python
import functools
import math

import jax
import jax.numpy as jnp
from jax import lax
from jax.experimental import pallas as pl
from jax.experimental.pallas import tpu as pltpu
from jax.sharding import Mesh, PartitionSpec as P

HEAD_SIZE = 128


norm_eps = 1e-06
rope_base = 1000000.0
beta_one = 0.9
beta_two = 0.95
adam_eps = 1e-08
learn_rate = 0.02
weight_decay = 0.1
step_count = 10.0


def rope_tables(length, head_width):
    half_width = head_width // 2
    index_float = jnp.arange(half_width, dtype=jnp.float32)
    inverse_freq = rope_base ** (-2.0 * index_float / head_width)
    positions = jnp.arange(length, dtype=jnp.float32)
    angles = positions[:, None] * inverse_freq[None, :]
    return (jnp.cos(angles), jnp.sin(angles))


BF = jnp.bfloat16
F32 = jnp.float32
HALF = HEAD_SIZE // 2
PLACES = (0, -1, 1, 2)
NT = (((1,), (1,)), ((), ()))
TT = (((0,), (0,)), ((), ()))


def dot(left, right, dims=None):
    if dims is None:
        dims = (((1,), (0,)), ((), ()))
    return lax.dot_general(left, right, dims, preferred_element_type=F32)


def params(mebibytes=48):
    return pltpu.CompilerParams(vmem_limit_bytes=mebibytes * 1024 * 1024)


def norm_scale(field):
    return lax.rsqrt(jnp.mean(field * field, axis=-1, keepdims=True) + norm_eps)


def norm_back(field, factor, cotan):
    return factor * cotan - field * (factor * factor * factor) * jnp.mean(
        cotan * field, axis=-1, keepdims=True
    )


def turn(field, cosines, sines):
    return field * cosines + pltpu.roll(field, HALF, 1) * sines


def query_kernel(q_ref, cos_ref, sin_ref, out_ref):
    field = q_ref[...].astype(F32)
    out_ref[...] = turn(field * norm_scale(field), cos_ref[...], sin_ref[...]).astype(BF)


def rotated_queries(queries, cosines, sines):
    length, width = queries.shape
    column = pl.BlockSpec((length, HEAD_SIZE), lambda h: (0, h))
    table = pl.BlockSpec((length, HEAD_SIZE), lambda h: (0, 0))
    return pl.pallas_call(
        query_kernel,
        grid=(width // HEAD_SIZE,),
        in_specs=[column, table, table],
        out_specs=column,
        out_shape=jax.ShapeDtypeStruct(queries.shape, BF),
        compiler_params=params(),
        name="query_rope",
    )(queries, cosines, sines)


def norm_kernel(in_ref, out_ref):
    field = in_ref[...].astype(F32)
    out_ref[...] = (field * norm_scale(field)).astype(BF)


def normed(tokens):
    block = pl.BlockSpec((tokens.shape[0] // 4, tokens.shape[1]), lambda i: (i, 0))
    return pl.pallas_call(
        norm_kernel,
        grid=(4,),
        in_specs=[block],
        out_specs=block,
        out_shape=jax.ShapeDtypeStruct(tokens.shape, BF),
        compiler_params=params(),
        name="norm",
    )(tokens)


def project_kernel(scale, offset_ref, order_ref, *refs):
    x_refs, (cos_ref, sin_ref), refs = refs[:4], refs[4:6], refs[6:]
    w_refs, (whole_ref, plain_ref), out_refs = refs[:-6], refs[-6:-4], refs[-4:]
    tokens, block = cos_ref.shape[0], whole_ref.shape[0] // offset_ref.shape[0]
    at = 0
    for w_ref in w_refs:
        count = w_ref.shape[0] // block

        def step(k, carry, at=at, w_ref=w_ref):
            row = pl.ds(pl.multiple_of(offset_ref[at + k], 16), block)
            whole_ref[row, :] = w_ref[pl.ds(pl.multiple_of(k * block, 16), block), :]
            return carry

        lax.fori_loop(0, count, step, 0)
        at += count
    chunk = whole_ref.shape[0] // 4
    total = 0.0
    for j in range(4):
        columns = slice(j * chunk, (j + 1) * chunk)
        field = jnp.concatenate([x_ref[:, columns] for x_ref in x_refs], axis=0)
        total = total + dot(field, whole_ref[columns])
    plain_ref[...] = total * scale
    for k in range(4):
        rows = pl.ds(pl.multiple_of(order_ref[k] * tokens, tokens), tokens)
        u = plain_ref[rows, :HEAD_SIZE]
        out_refs[k][0] = turn(u * norm_scale(u), cos_ref[...], sin_ref[...]).astype(BF)
        out_refs[k][1] = plain_ref[rows, HEAD_SIZE:].astype(BF)


def project(offsets, order, blocks, cosines, sines, pieces, scale):
    tokens, width = cosines.shape[0], pieces[0].shape[1]
    vmem = pl.BlockSpec(memory_space=pltpu.VMEM)
    smem = pl.BlockSpec(memory_space=pltpu.SMEM)
    result = pl.pallas_call(
        functools.partial(project_kernel, scale),
        in_specs=[smem, smem] + [vmem] * (6 + len(pieces)),
        out_specs=[vmem] * 6,
        out_shape=[
            jax.ShapeDtypeStruct((blocks[0].shape[1], width), BF),
            jax.ShapeDtypeStruct((4 * tokens, width), F32),
        ]
        + [jax.ShapeDtypeStruct((2, tokens, HEAD_SIZE), BF)] * 4,
        compiler_params=params(),
        name="project",
    )(offsets, order, *blocks, cosines, sines, *pieces)
    return result[0], result[1], result[2:]


def weight_grad_kernel(offset_ref, cotan_ref, *refs):
    x_refs, out_refs, whole = refs[:4], refs[4:-1], refs[-1]
    chunk = whole.shape[0] // 8
    block = whole.shape[0] // offset_ref.shape[0]
    cotan = cotan_ref[...]
    for j in range(8):
        columns = slice(j * chunk, (j + 1) * chunk)
        field = jnp.concatenate([x_ref[:, columns] for x_ref in x_refs], axis=0)
        whole[columns] = dot(field, cotan, TT).astype(BF)
    at = 0
    for out_ref in out_refs:
        count = out_ref.shape[0] // block

        def step(k, carry, at=at, out_ref=out_ref):
            row = pl.ds(pl.multiple_of(offset_ref[at + k], 16), block)
            out_ref[pl.ds(pl.multiple_of(k * block, 16), block), :] = whole[row, :]
            return carry

        lax.fori_loop(0, count, step, 0)
        at += count


def weight_grads(offsets, blocks, cotan):
    vmem = pl.BlockSpec(memory_space=pltpu.VMEM)
    rows, width = blocks[0].shape[1], cotan.shape[1]
    return pl.pallas_call(
        weight_grad_kernel,
        in_specs=[pl.BlockSpec(memory_space=pltpu.SMEM)] + [vmem] * 5,
        out_specs=[vmem] * 4,
        out_shape=[jax.ShapeDtypeStruct((rows // 4, width), BF)] * 4,
        scratch_shapes=[pltpu.VMEM((rows, width), BF)],
        compiler_params=params(),
        name="weight_grads",
    )(offsets, cotan, *blocks)


def attention_kernel(order_ref, q_ref, g_ref, *refs):
    kv_refs, dkv_refs = refs[:4], refs[4:8]
    k_ref, ds0_ref, ds1_ref, v_ref, dk_acc, dv_acc = refs[8:]
    head = pl.program_id(0)
    length = q_ref.shape[0]
    tokens = length // 4
    mid = length // 2
    scale = 1.0 / math.sqrt(HEAD_SIZE)

    @pl.when(head == 0)
    def _():
        dk_acc[...] = jnp.zeros_like(dk_acc)
        dv_acc[...] = jnp.zeros_like(dv_acc)
        for k in range(4):
            rows = pl.ds(pl.multiple_of(order_ref[k] * tokens, tokens), tokens)
            k_ref[rows, :] = kv_refs[k][0]
            v_ref[rows, :] = kv_refs[k][1]

    q, g = q_ref[...], g_ref[...]
    k0, k1 = k_ref[:mid], k_ref[mid:]
    v0, v1 = v_ref[:mid], v_ref[mid:]
    row = lax.broadcasted_iota(jnp.int32, (mid, mid), 0)
    column = lax.broadcasted_iota(jnp.int32, (mid, mid), 1)
    allowed = row <= column
    e0 = jnp.exp(dot(k0, q, NT) * scale)
    e0a = jnp.where(allowed, e0[:, :mid], 0.0)
    e0b = e0[:, mid:]
    e1 = jnp.where(allowed, jnp.exp(dot(k1, q[mid:], NT) * scale), 0.0)
    inv_a = 1.0 / jnp.sum(e0a, axis=0, keepdims=True)
    inv_b = 1.0 / (jnp.sum(e0b, axis=0, keepdims=True) + jnp.sum(e1, axis=0, keepdims=True))
    p0a, p0b, p1 = e0a * inv_a, e0b * inv_b, e1 * inv_b
    g_a, g_b = g[:mid], g[mid:]
    dv_acc[:mid] += dot(p0a.astype(BF), g_a) + dot(p0b.astype(BF), g_b)
    dv_acc[mid:] += dot(p1.astype(BF), g_b)
    d0a, d0b, d1 = dot(v0, g_a, NT), dot(v0, g_b, NT), dot(v1, g_b, NT)
    sum_a = jnp.sum(p0a * d0a, axis=0, keepdims=True)
    sum_b = jnp.sum(p0b * d0b, axis=0, keepdims=True) + jnp.sum(p1 * d1, axis=0, keepdims=True)
    s0a = (p0a * (d0a - sum_a)).astype(BF)
    s0b = (p0b * (d0b - sum_b)).astype(BF)
    s1 = (p1 * (d1 - sum_b)).astype(BF)
    ds0_ref[0, :, :mid] = s0a
    ds0_ref[0, :, mid:] = s0b
    ds1_ref[0] = s1
    dk_acc[:mid] += dot(s0a, q[:mid]) + dot(s0b, q[mid:])
    dk_acc[mid:] += dot(s1, q[mid:])

    @pl.when(head == pl.num_programs(0) - 1)
    def _():
        for k in range(4):
            rows = pl.ds(pl.multiple_of(order_ref[k] * tokens, tokens), tokens)
            dkv_refs[k][0] = (dk_acc[rows, :] * scale).astype(BF)
            dkv_refs[k][1] = dv_acc[rows, :].astype(BF)


def attention(order, rotated, incoming, pieces):
    length, width = rotated.shape
    heads, mid = width // HEAD_SIZE, length // 2
    column = pl.BlockSpec((length, HEAD_SIZE), lambda h: (0, h))
    whole = pl.BlockSpec((length, HEAD_SIZE), lambda h: (0, 0))
    piece = pl.BlockSpec(pieces[0].shape, lambda h: (0, 0, 0))
    result = pl.pallas_call(
        attention_kernel,
        grid=(heads,),
        in_specs=[pl.BlockSpec(memory_space=pltpu.SMEM), column, column] + [piece] * 4,
        out_specs=[piece] * 4
        + [
            whole,
            pl.BlockSpec((1, mid, length), lambda h: (h, 0, 0)),
            pl.BlockSpec((1, mid, mid), lambda h: (h, 0, 0)),
        ],
        out_shape=[jax.ShapeDtypeStruct(pieces[0].shape, BF)] * 4
        + [
            jax.ShapeDtypeStruct((length, HEAD_SIZE), BF),
            jax.ShapeDtypeStruct((heads, mid, length), BF),
            jax.ShapeDtypeStruct((heads, mid, mid), BF),
        ],
        scratch_shapes=[pltpu.VMEM((length, HEAD_SIZE), BF)]
        + [pltpu.VMEM((length, HEAD_SIZE), F32)] * 2,
        compiler_params=params(60),
        name="attention",
    )(order, rotated, incoming, *pieces)
    return result[:4], result[4], result[5], result[6]


def grad_query_kernel(q_ref, k_ref, ds0_ref, ds1_ref, cos_ref, sin_ref, out_ref):
    mid = ds0_ref.shape[1]
    scale = 1.0 / math.sqrt(HEAD_SIZE)
    k0, k1 = k_ref[:mid], k_ref[mid:]
    both = dot(k0, ds0_ref[0], TT)
    early = both[:, :mid]
    late = both[:, mid:] + dot(k1, ds1_ref[0], TT)
    cotan = jnp.concatenate([early.T, late.T], axis=0) * scale
    field = q_ref[...].astype(F32)
    cotan = turn(cotan, cos_ref[...], -sin_ref[...])
    out_ref[...] = norm_back(field, norm_scale(field), cotan).astype(BF)


def grad_queries(queries, key, ds0, ds1, cosines, sines):
    length, width = queries.shape
    heads, mid = width // HEAD_SIZE, length // 2
    column = pl.BlockSpec((length, HEAD_SIZE), lambda h: (0, h))
    whole = pl.BlockSpec((length, HEAD_SIZE), lambda h: (0, 0))
    return pl.pallas_call(
        grad_query_kernel,
        grid=(heads,),
        in_specs=[
            column,
            whole,
            pl.BlockSpec((1, mid, length), lambda h: (h, 0, 0)),
            pl.BlockSpec((1, mid, mid), lambda h: (h, 0, 0)),
            whole,
            whole,
        ],
        out_specs=column,
        out_shape=jax.ShapeDtypeStruct(queries.shape, BF),
        compiler_params=params(60),
        name="grad_query",
    )(queries, key, ds0, ds1, cosines, sines)


def cotan_kernel(order_ref, b0_ref, b1_ref, b2_ref, b3_ref, plain_ref, cos_ref, sin_ref, out_ref):
    tokens = cos_ref.shape[0]
    for k, back_ref in enumerate((b0_ref, b1_ref, b2_ref, b3_ref)):
        rows = pl.ds(pl.multiple_of(order_ref[k] * tokens, tokens), tokens)
        u = plain_ref[rows, :HEAD_SIZE]
        back = turn(back_ref[0].astype(F32), cos_ref[...], -sin_ref[...])
        out_ref[rows, :HEAD_SIZE] = norm_back(u, norm_scale(u), back).astype(BF)
        out_ref[rows, HEAD_SIZE:] = back_ref[1]


def key_value_cotan(order, back, plain, cosines, sines):
    vmem = pl.BlockSpec(memory_space=pltpu.VMEM)
    return pl.pallas_call(
        cotan_kernel,
        in_specs=[pl.BlockSpec(memory_space=pltpu.SMEM)] + [vmem] * 7,
        out_specs=vmem,
        out_shape=jax.ShapeDtypeStruct(plain.shape, BF),
        compiler_params=params(),
        name="key_value_cotan",
    )(order, *back, plain, cosines, sines)


def grad_token_kernel(x_ref, kept_ref, core_ref, layer_ref, *refs):
    out_ref = refs[-1]
    cotan = kept_ref[...] + core_ref[...].astype(F32) + layer_ref[...].astype(F32)
    field = x_ref[...].astype(F32)
    out_ref[...] = norm_back(field, norm_scale(field), cotan).astype(BF)


def grad_tokens(tokens, kept, from_core, from_layer, start, given=None):
    step, width = 16, tokens.shape[1]
    first = start // step
    here = pl.BlockSpec((step, width), lambda i: (first + i, 0))
    specs = [here, here, here, pl.BlockSpec((step, width), lambda i: (i, 0))]
    operands = [tokens, kept, from_core, from_layer]
    if given is not None:
        specs.append(pl.BlockSpec(memory_space=pl.ANY))
        operands.append(given)
    return pl.pallas_call(
        grad_token_kernel,
        grid=(from_layer.shape[0] // step,),
        in_specs=specs,
        out_specs=here,
        out_shape=jax.ShapeDtypeStruct(tokens.shape, BF),
        input_output_aliases={} if given is None else {4: 0},
        compiler_params=params(),
        name="grad_tokens",
    )(*operands)


def plane_pairs(first, step):
    pairs = []
    for x in range(4):
        for y in range(4):
            for c in range(2):
                along_x = (c == 0) == first
                to_x = (x + step) % 4 if along_x else x
                to_y = y if along_x else (y + step) % 4
                pairs.append(((x * 4 + y) * 2 + c, (to_x * 4 + to_y) * 2 + c))
    return pairs


def far(block, step):
    return lax.ppermute(block, ("x", "y", "c"), plane_pairs(True, step))


def near(block, step):
    return lax.ppermute(block, ("x", "y", "c"), plane_pairs(False, step))


def swap_cores(block):
    return lax.ppermute(block, "c", [(0, 1), (1, 0)])


def group_pairs(target):
    pairs = []
    for g in range(4):
        for t in range(4):
            to_g, to_t = target(g, t)
            pairs.append((g * 4 + t, (to_g % 4) * 4 + to_t % 4))
    return pairs


def to_heads(block, k):
    return lax.ppermute(block, ("zl", "c", "t"), group_pairs(lambda g, t: (t, g + k)))


def from_heads(block, k):
    return lax.ppermute(block, ("zl", "c", "t"), group_pairs(lambda g, t: (t + k, g)))


def swap_layers(block):
    return lax.ppermute(block, "zl", [(0, 1), (1, 0)])


def after(first, *later):
    return lax.optimization_barrier((first,) + later)[1:]


def per_device(
    tokens,
    queries,
    grad_out,
    key_value_master_weight,
    key_value_first_moment,
    key_value_second_moment,
    writer,
):
    own_tokens, model_width = tokens.shape
    unit_scale = 1.0 / math.sqrt(model_width)
    length = queries.shape[0]
    rows = key_value_master_weight.shape[1]
    core = lax.axis_index("c")
    x_index, y_index = lax.axis_index("x"), lax.axis_index("y")
    t_index = lax.axis_index("t")
    g_index = 2 * lax.axis_index("zl") + core

    own_weight = key_value_master_weight.astype(BF)
    own_weight = jnp.concatenate([own_weight[0], own_weight[1]], axis=1)
    stage = jnp.concatenate([to_heads(own_weight, k) for k in range(4)], axis=0)
    own_block = normed(tokens)
    from_core = swap_cores(own_block)
    from_z = swap_layers(after(stage, own_block)[0])
    shard = jnp.concatenate([stage, near(stage, 1), near(stage, -1), near(stage, 2)], axis=0)
    pieces = [shard, far(shard, 1), far(shard, -1), far(shard, 2)]
    (from_z,) = after(pieces, from_z)
    blocks = [own_block, from_core, from_z, swap_cores(from_z)]

    place = jnp.array(PLACES, jnp.int32)
    count = jnp.arange(4, dtype=jnp.int32)
    far_place = (jnp.where(core == 0, x_index, y_index) + place) % 4
    near_place = (jnp.where(core == 0, y_index, x_index) + place) % 4
    far_step = jnp.where(core == 0, 8 * rows, 2 * rows)
    near_step = jnp.where(core == 0, 2 * rows, 8 * rows)
    source = (t_index - count) % 4
    offsets = (
        far_place[:, None, None] * far_step
        + near_place[None, :, None] * near_step
        + ((source // 2) * (32 * rows) + (source % 2) * rows)[None, None, :]
    )
    offsets = offsets.reshape(64).astype(jnp.int32)
    sequence_order = ((t_index + count) % 4) ^ g_index
    block_order = (g_index - count) % 4

    cosines, sines = rope_tables(length, HEAD_SIZE)
    cosines = jnp.concatenate([cosines, cosines], axis=1)
    sines = jnp.concatenate([-sines, sines], axis=1)
    own_cos = lax.dynamic_slice_in_dim(cosines, t_index * own_tokens, own_tokens, 0)
    own_sin = lax.dynamic_slice_in_dim(sines, t_index * own_tokens, own_tokens, 0)
    rotated = rotated_queries(queries, cosines, sines)

    weights, plain, projected = project(
        offsets, sequence_order, blocks, own_cos, own_sin,
        pieces, unit_scale,
    )
    arrived = [from_heads(block, k) for k, block in enumerate(projected)]
    returning, key, ds0, ds1 = attention(block_order, rotated, grad_out, arrived)
    back = [to_heads(block, -k) for k, block in enumerate(returning)]
    cotan = key_value_cotan(sequence_order, back, plain, own_cos, own_sin)

    part = weight_grads(offsets, blocks, cotan)
    arriving = [far(part[1], -1), far(part[2], 1), far(part[3], 2)]

    rows_of = after(part[0], cotan)[0].reshape(4, own_tokens, -1)
    sent = dot(jnp.concatenate([rows_of[1], rows_of[3]], axis=0), weights, NT) * unit_scale
    sent = sent.astype(BF)
    swapped = swap_cores(sent)
    (kept_from,) = after(sent, jnp.concatenate([rows_of[0], rows_of[2]], axis=0))
    kept = dot(kept_from, weights, NT) * unit_scale
    to_z = (kept[own_tokens:] + swapped[own_tokens:].astype(F32)).astype(BF)
    cuts = (0, 16, 64, own_tokens)
    to_z = [to_z[cuts[i] : cuts[i + 1]] for i in range(3)]
    z_first = swap_layers(to_z[0])

    own = part[0].astype(F32)
    for piece in arriving:
        own = own + piece.astype(F32)
    own = own.astype(BF).reshape(4, 4 * rows, -1)
    own, to_z[1] = after(z_first, own, to_z[1])
    z_second = swap_layers(to_z[1])
    summed = own[0].astype(F32)
    for index, step in ((1, -1), (2, 1), (3, 2)):
        summed = summed + near(own[index], step).astype(F32)

    (ds0,) = after(own, ds0)
    grad_q = grad_queries(queries, key, ds0, ds1, cosines, sines)
    (summed,) = after((grad_q, z_second), summed)

    summed = summed.astype(BF).reshape(4, rows, 2 * HEAD_SIZE)
    final = sum(from_heads(summed[k], -k).astype(F32) for k in range(4)) * unit_scale
    weight_grad = jnp.stack([final[:, :HEAD_SIZE], final[:, HEAD_SIZE:]], axis=0)

    z_first, z_second, to_z[2] = after(final, z_first, z_second, to_z[2])
    grad_x = grad_tokens(tokens, kept, swapped, z_first, 0)
    grad_x = grad_tokens(tokens, kept, swapped, z_second, cuts[1], grad_x)
    grad_x = grad_tokens(tokens, kept, swapped, swap_layers(to_z[2]), cuts[2], grad_x)

    new_first = beta_one * key_value_first_moment + (1.0 - beta_one) * weight_grad
    new_second = beta_two * key_value_second_moment + (1.0 - beta_two) * weight_grad * weight_grad
    first_hat = new_first / (1.0 - beta_one**step_count)
    second_hat = new_second / (1.0 - beta_two**step_count)
    new_master = key_value_master_weight - learn_rate * (
        first_hat / (jnp.sqrt(second_hat) + adam_eps) + weight_decay * key_value_master_weight
    )
    replicas = writer.shape[0]
    flat_saved = new_master.astype(BF).reshape(replicas, -1)
    rank_ids = jnp.arange(replicas, dtype=jnp.int32)
    inverse = jnp.sum(jnp.where(writer[None, :] == rank_ids[:, None], rank_ids[None, :], 0), axis=1)
    saved = lax.all_to_all(flat_saved[inverse], ("zl", "x", "y", "c"), 0, 0, tiled=True)
    return (grad_x, grad_q, new_master, new_first, new_second, saved)


def solution(mesh):
    fine = Mesh(mesh.devices.reshape(2, 4, 4, 2, 4), ("zl", "x", "y", "c", "t"))
    dp = ("zl", "x", "y", "c")
    every = dp + ("t",)
    weight = P(None, dp, "t")
    return jax.shard_map(
        per_device,
        mesh=fine,
        in_specs=(P(every, None), P(dp, "t"), P(dp, "t"), weight, weight, weight, P()),
        out_specs=(P(every, None), P(dp, "t"), weight, weight, weight, P(dp, "t")),
        check_vma=False,
    )
```

```python
import functools
import math

import jax
import jax.numpy as jnp
from jax import lax
from jax.experimental import pallas as pl
from jax.experimental.pallas import tpu as pltpu
from jax.sharding import Mesh, PartitionSpec as P

HEAD_SIZE = 128


norm_eps = 1e-06
rope_base = 1000000.0
beta_one = 0.9
beta_two = 0.95
adam_eps = 1e-08
learn_rate = 0.02
weight_decay = 0.1
step_count = 10.0


def rope_tables(length, head_width):
    half_width = head_width // 2
    index_float = jnp.arange(half_width, dtype=jnp.float32)
    inverse_freq = rope_base ** (-2.0 * index_float / head_width)
    positions = jnp.arange(length, dtype=jnp.float32)
    angles = positions[:, None] * inverse_freq[None, :]
    return (jnp.cos(angles), jnp.sin(angles))


BF = jnp.bfloat16
F32 = jnp.float32
HALF = HEAD_SIZE // 2
PLACES = (0, -1, 1, 2)
NT = (((1,), (1,)), ((), ()))
TT = (((0,), (0,)), ((), ()))


def dot(left, right, dims=None):
    if dims is None:
        dims = (((1,), (0,)), ((), ()))
    return lax.dot_general(left, right, dims, preferred_element_type=F32)


def params(mebibytes=20):
    return pltpu.CompilerParams(vmem_limit_bytes=mebibytes * 1024 * 1024)


def norm_scale(field):
    return lax.rsqrt(jnp.mean(field * field, axis=-1, keepdims=True) + norm_eps)


def norm_back(field, factor, cotan):
    return factor * cotan - field * (factor * factor * factor) * jnp.mean(
        cotan * field, axis=-1, keepdims=True
    )


def turn(field, cosines, sines):
    return field * cosines + pltpu.roll(field, HALF, 1) * sines


def query_kernel(q_ref, cos_ref, sin_ref, out_ref):
    field = q_ref[...].astype(F32)
    out_ref[...] = turn(field * norm_scale(field), cos_ref[...], sin_ref[...]).astype(BF)


def rotated_queries(queries, cosines, sines):
    length, width = queries.shape
    column = pl.BlockSpec((length, HEAD_SIZE), lambda h: (0, h))
    table = pl.BlockSpec((length, HEAD_SIZE), lambda h: (0, 0))
    return pl.pallas_call(
        query_kernel,
        grid=(width // HEAD_SIZE,),
        in_specs=[column, table, table],
        out_specs=column,
        out_shape=jax.ShapeDtypeStruct(queries.shape, BF),
        compiler_params=params(),
        name="query_rope",
    )(queries, cosines, sines)


def norm_kernel(in_ref, out_ref):
    field = in_ref[...].astype(F32)
    out_ref[...] = (field * norm_scale(field)).astype(BF)


def normed(tokens):
    block = pl.BlockSpec((tokens.shape[0] // 4, tokens.shape[1]), lambda i: (i, 0))
    return pl.pallas_call(
        norm_kernel,
        grid=(4,),
        in_specs=[block],
        out_specs=block,
        out_shape=jax.ShapeDtypeStruct(tokens.shape, BF),
        compiler_params=params(),
        name="norm",
    )(tokens)


def project_early_kernel(scale, offset_ref, first_ref, second_ref, *refs):
    w_refs, whole_ref, plain_ref = refs[:-2], refs[-2], refs[-1]
    block = whole_ref.shape[0] // offset_ref.shape[0]
    at = 0
    for w_ref in w_refs:
        count = w_ref.shape[0] // block
        for k in range(count):
            row = pl.ds(pl.multiple_of(offset_ref[at + k], 16), block)
            whole_ref[row, :] = w_ref[k * block : (k + 1) * block]
        at += count
    plain_ref[...] = rows_times(first_ref, second_ref, whole_ref) * scale


def rows_times(first_ref, second_ref, whole_ref):
    chunk = whole_ref.shape[0] // 4
    total = 0.0
    for j in range(4):
        columns = slice(j * chunk, (j + 1) * chunk)
        field = jnp.concatenate([first_ref[:, columns], second_ref[:, columns]], axis=0)
        total = total + dot(field, whole_ref[columns])
    return total


def project_early(offsets, first, second, pieces, scale):
    vmem = pl.BlockSpec(memory_space=pltpu.VMEM)
    shape = (first.shape[1], pieces[0].shape[1])
    return pl.pallas_call(
        functools.partial(project_early_kernel, scale),
        in_specs=[pl.BlockSpec(memory_space=pltpu.SMEM)] + [vmem] * (2 + len(pieces)),
        out_specs=[vmem, vmem],
        out_shape=[
            jax.ShapeDtypeStruct(shape, BF),
            jax.ShapeDtypeStruct((2 * first.shape[0], shape[1]), F32),
        ],
        compiler_params=params(48),
        name="project_early",
    )(offsets, first, second, *pieces)


def project_kernel(scale, order_ref, first_ref, second_ref, whole_ref, early_ref, cos_ref, sin_ref, plain_ref, *out_refs):
    tokens = cos_ref.shape[0]
    plain_ref[: 2 * tokens] = early_ref[...]
    plain_ref[2 * tokens :] = rows_times(first_ref, second_ref, whole_ref) * scale
    for k in range(4):
        rows = pl.ds(pl.multiple_of(order_ref[k] * tokens, tokens), tokens)
        u = plain_ref[rows, :HEAD_SIZE]
        out_refs[k][0] = turn(u * norm_scale(u), cos_ref[...], sin_ref[...]).astype(BF)
        out_refs[k][1] = plain_ref[rows, HEAD_SIZE:].astype(BF)


def project(order, first, second, weights, early, cosines, sines, scale):
    tokens = cosines.shape[0]
    vmem = pl.BlockSpec(memory_space=pltpu.VMEM)
    result = pl.pallas_call(
        functools.partial(project_kernel, scale),
        in_specs=[pl.BlockSpec(memory_space=pltpu.SMEM)] + [vmem] * 6,
        out_specs=[vmem] * 5,
        out_shape=[jax.ShapeDtypeStruct((4 * tokens, weights.shape[1]), F32)]
        + [jax.ShapeDtypeStruct((2, tokens, HEAD_SIZE), BF)] * 4,
        compiler_params=params(),
        name="project",
    )(order, first, second, weights, early, cosines, sines)
    return result[0], result[1:]


def sum_kernel(*refs):
    in_refs, out_refs = refs[:4], refs[4:]
    rows = out_refs[0].shape[0]
    for index, out_ref in enumerate(out_refs):
        part = slice(index * rows, (index + 1) * rows)
        total = sum(ref[part].astype(F32) for ref in in_refs[-3:]) + in_refs[0][part].astype(F32)
        out_ref[...] = total.astype(out_ref.dtype)


def sum_of(own, arrived, first_type):
    shape = (own.shape[0] // 4, own.shape[1])
    vmem = pl.BlockSpec(memory_space=pltpu.VMEM)
    return pl.pallas_call(
        sum_kernel,
        in_specs=[vmem] * 4,
        out_specs=[vmem] * 4,
        out_shape=[jax.ShapeDtypeStruct(shape, first_type)] + [jax.ShapeDtypeStruct(shape, BF)] * 3,
        compiler_params=params(),
        name="sum",
    )(own, *arrived)


def weight_grad_kernel(offset_ref, cotan_ref, *refs):
    x_refs, out_refs, whole = refs[:4], refs[4:-1], refs[-1]
    chunk = whole.shape[0] // 8
    block = whole.shape[0] // offset_ref.shape[0]
    cotan = cotan_ref[...]
    for j in range(8):
        columns = slice(j * chunk, (j + 1) * chunk)
        field = jnp.concatenate([x_ref[:, columns] for x_ref in x_refs], axis=0)
        whole[columns] = dot(field, cotan, TT).astype(BF)
    at = 0
    for out_ref in out_refs:
        count = out_ref.shape[0] // block

        def step(k, carry, at=at, out_ref=out_ref):
            row = pl.ds(pl.multiple_of(offset_ref[at + k], 16), block)
            out_ref[pl.ds(pl.multiple_of(k * block, 16), block), :] = whole[row, :]
            return carry

        lax.fori_loop(0, count, step, 0)
        at += count


def weight_grads(offsets, blocks, cotan):
    vmem = pl.BlockSpec(memory_space=pltpu.VMEM)
    rows, width = blocks[0].shape[1], cotan.shape[1]
    return pl.pallas_call(
        weight_grad_kernel,
        in_specs=[pl.BlockSpec(memory_space=pltpu.SMEM)] + [vmem] * 5,
        out_specs=[vmem] * 4,
        out_shape=[jax.ShapeDtypeStruct((rows // 4, width), BF)] * 4,
        scratch_shapes=[pltpu.VMEM((rows, width), BF)],
        compiler_params=params(),
        name="weight_grads",
    )(offsets, cotan, *blocks)


def attention_kernel(order_ref, q_ref, g_ref, *refs):
    kv_refs, dkv_refs = refs[:4], refs[4:8]
    k_ref, ds0_ref, ds1_ref, v_ref, dk_acc, dv_acc = refs[8:]
    step = pl.program_id(0)
    length, width = q_ref.shape
    tokens, mid, heads = length // 4, length // 2, width // HEAD_SIZE
    scale = 1.0 / math.sqrt(HEAD_SIZE)

    @pl.when(step == 0)
    def _():
        dk_acc[...] = jnp.zeros_like(dk_acc)
        dv_acc[...] = jnp.zeros_like(dv_acc)
        for k in range(4):
            rows = pl.ds(pl.multiple_of(order_ref[k] * tokens, tokens), tokens)
            k_ref[rows, :] = kv_refs[k][0]
            v_ref[rows, :] = kv_refs[k][1]

    early, late = slice(0, mid), slice(mid, length)
    row = lax.broadcasted_iota(jnp.int32, (mid, mid), 0)
    column = lax.broadcasted_iota(jnp.int32, (mid, mid), 1)
    allowed = row <= column
    factor = scale * math.log2(math.e)
    each = range(heads)

    def at(ref, rows, h):
        return ref[rows, h * HEAD_SIZE : (h + 1) * HEAD_SIZE]

    def products(left_ref, right_ref):
        return [
            [
                dot(left_ref[early], at(right_ref, early, h), NT),
                dot(left_ref[early], at(right_ref, late, h), NT),
                dot(left_ref[late], at(right_ref, late, h), NT),
            ]
            for h in each
        ]

    def add(acc, terms, right_ref):
        acc[early] += sum(
            dot(terms[h][0], at(right_ref, early, h)) + dot(terms[h][1], at(right_ref, late, h))
            for h in each
        )
        acc[late] += sum(dot(terms[h][2], at(right_ref, late, h)) for h in each)

    def column_sums(terms):
        first, second, third = (jnp.sum(term, axis=0, keepdims=True) for term in terms)
        return first, second + third

    scores = products(k_ref, q_ref)
    d_probs = products(v_ref, g_ref)
    probs = []
    for h in each:
        a, b, c = scores[h]
        a = jnp.where(allowed, jnp.exp2(a * factor), 0.0)
        b = jnp.exp2(b * factor)
        c = jnp.where(allowed, jnp.exp2(c * factor), 0.0)
        sum_a, sum_b = column_sums((a, b, c))
        inv_a, inv_b = 1.0 / sum_a, 1.0 / sum_b
        probs.append((a * inv_a, b * inv_b, c * inv_b))
    add(dv_acc, [[term.astype(BF) for term in probs[h]] for h in each], g_ref)
    d_scores = []
    for h in each:
        sum_a, sum_b = column_sums([p * d for p, d in zip(probs[h], d_probs[h])])
        d_scores.append(
            [
                (p * (d - total)).astype(BF)
                for p, d, total in zip(probs[h], d_probs[h], (sum_a, sum_b, sum_b))
            ]
        )
        ds0_ref[h, :, :mid] = d_scores[h][0]
        ds0_ref[h, :, mid:] = d_scores[h][1]
        ds1_ref[h] = d_scores[h][2]
    add(dk_acc, d_scores, q_ref)

    @pl.when(step == pl.num_programs(0) - 1)
    def _():
        for k in range(4):
            rows = pl.ds(pl.multiple_of(order_ref[k] * tokens, tokens), tokens)
            dkv_refs[k][0] = (dk_acc[rows, :] * scale).astype(BF)
            dkv_refs[k][1] = dv_acc[rows, :].astype(BF)


def attention(order, rotated, incoming, pieces):
    length, width = rotated.shape
    heads, mid, pair = width // HEAD_SIZE, length // 2, 2
    columns = pl.BlockSpec((length, pair * HEAD_SIZE), lambda h: (0, h))
    whole = pl.BlockSpec((length, HEAD_SIZE), lambda h: (0, 0))
    piece = pl.BlockSpec(pieces[0].shape, lambda h: (0, 0, 0))
    result = pl.pallas_call(
        attention_kernel,
        grid=(heads // pair,),
        in_specs=[pl.BlockSpec(memory_space=pltpu.SMEM), columns, columns] + [piece] * 4,
        out_specs=[piece] * 4
        + [
            whole,
            pl.BlockSpec((pair, mid, length), lambda h: (h, 0, 0)),
            pl.BlockSpec((pair, mid, mid), lambda h: (h, 0, 0)),
        ],
        out_shape=[jax.ShapeDtypeStruct(pieces[0].shape, BF)] * 4
        + [
            jax.ShapeDtypeStruct((length, HEAD_SIZE), BF),
            jax.ShapeDtypeStruct((heads, mid, length), BF),
            jax.ShapeDtypeStruct((heads, mid, mid), BF),
        ],
        scratch_shapes=[pltpu.VMEM((length, HEAD_SIZE), BF)]
        + [pltpu.VMEM((length, HEAD_SIZE), F32)] * 2,
        compiler_params=params(32),
        name="attention",
    )(order, rotated, incoming, *pieces)
    return result[:4], result[4], result[5], result[6]


def grad_query_kernel(q_ref, k_ref, ds0_ref, ds1_ref, cos_ref, sin_ref, *refs):
    out_ref = refs[-1]
    mid = ds0_ref.shape[1]
    scale = 1.0 / math.sqrt(HEAD_SIZE)
    k0, k1 = k_ref[:mid], k_ref[mid:]
    both = dot(k0, ds0_ref[0], TT)
    early = both[:, :mid]
    late = both[:, mid:] + dot(k1, ds1_ref[0], TT)
    cotan = jnp.concatenate([early.T, late.T], axis=0) * scale
    field = q_ref[...].astype(F32)
    cotan = turn(cotan, cos_ref[...], -sin_ref[...])
    out_ref[...] = norm_back(field, norm_scale(field), cotan).astype(BF)


def grad_queries(queries, key, ds0, ds1, cosines, sines, first, given=None):
    length, width = queries.shape
    heads, mid = width // HEAD_SIZE, length // 2
    column = pl.BlockSpec((length, HEAD_SIZE), lambda h: (0, first + h))
    whole = pl.BlockSpec((length, HEAD_SIZE), lambda h: (0, 0))
    specs = [
        column,
        whole,
        pl.BlockSpec((1, mid, length), lambda h: (first + h, 0, 0)),
        pl.BlockSpec((1, mid, mid), lambda h: (first + h, 0, 0)),
        whole,
        whole,
    ]
    operands = [queries, key, ds0, ds1, cosines, sines]
    if given is not None:
        specs.append(pl.BlockSpec(memory_space=pl.ANY))
        operands.append(given)
    return pl.pallas_call(
        grad_query_kernel,
        grid=(heads // 2,),
        in_specs=specs,
        out_specs=column,
        out_shape=jax.ShapeDtypeStruct(queries.shape, BF),
        input_output_aliases={} if given is None else {6: 0},
        compiler_params=params(16),
        name="grad_query",
    )(*operands)


def cotan_kernel(order_ref, b0_ref, b1_ref, b2_ref, b3_ref, plain_ref, cos_ref, sin_ref, out_ref):
    tokens = cos_ref.shape[0]
    for k, back_ref in enumerate((b0_ref, b1_ref, b2_ref, b3_ref)):
        rows = pl.ds(pl.multiple_of(order_ref[k] * tokens, tokens), tokens)
        u = plain_ref[rows, :HEAD_SIZE]
        back = turn(back_ref[0].astype(F32), cos_ref[...], -sin_ref[...])
        out_ref[rows, :HEAD_SIZE] = norm_back(u, norm_scale(u), back).astype(BF)
        out_ref[rows, HEAD_SIZE:] = back_ref[1]


def key_value_cotan(order, back, plain, cosines, sines):
    vmem = pl.BlockSpec(memory_space=pltpu.VMEM)
    return pl.pallas_call(
        cotan_kernel,
        in_specs=[pl.BlockSpec(memory_space=pltpu.SMEM)] + [vmem] * 7,
        out_specs=vmem,
        out_shape=jax.ShapeDtypeStruct(plain.shape, BF),
        compiler_params=params(),
        name="key_value_cotan",
    )(order, *back, plain, cosines, sines)


def grad_token_kernel(x_ref, mine_ref, layer_ref, *refs):
    out_ref = refs[-1]
    cotan = mine_ref[...].astype(F32) + layer_ref[...].astype(F32)
    field = x_ref[...].astype(F32)
    out_ref[...] = norm_back(field, norm_scale(field), cotan).astype(BF)


def grad_tokens(tokens, mine, from_layer, start, given=None):
    step, width = 16, tokens.shape[1]
    first = start // step
    here = pl.BlockSpec((step, width), lambda i: (first + i, 0))
    specs = [here, here, pl.BlockSpec((step, width), lambda i: (i, 0))]
    operands = [tokens, mine, from_layer]
    if given is not None:
        specs.append(pl.BlockSpec(memory_space=pl.ANY))
        operands.append(given)
    return pl.pallas_call(
        grad_token_kernel,
        grid=(from_layer.shape[0] // step,),
        in_specs=specs,
        out_specs=here,
        out_shape=jax.ShapeDtypeStruct(tokens.shape, BF),
        input_output_aliases={} if given is None else {3: 0},
        compiler_params=params(60),
        name="grad_tokens",
    )(*operands)


def plane_pairs(first, step):
    pairs = []
    for x in range(4):
        for y in range(4):
            for c in range(2):
                along_x = (c == 0) == first
                to_x = (x + step) % 4 if along_x else x
                to_y = y if along_x else (y + step) % 4
                pairs.append(((x * 4 + y) * 2 + c, (to_x * 4 + to_y) * 2 + c))
    return pairs


def far(block, step):
    return lax.ppermute(block, ("x", "y", "c"), plane_pairs(True, step))


def near(block, step):
    return lax.ppermute(block, ("x", "y", "c"), plane_pairs(False, step))


def swap_cores(block):
    return lax.ppermute(block, "c", [(0, 1), (1, 0)])


def group_pairs(target):
    pairs = []
    for g in range(4):
        for t in range(4):
            to_g, to_t = target(g, t)
            pairs.append((g * 4 + t, (to_g % 4) * 4 + to_t % 4))
    return pairs


def to_heads(block, k):
    return lax.ppermute(block, ("zl", "c", "t"), group_pairs(lambda g, t: (t, g + k)))


def from_heads(block, k):
    return lax.ppermute(block, ("zl", "c", "t"), group_pairs(lambda g, t: (t + k, g)))


def swap_layers(block):
    return lax.ppermute(block, "zl", [(0, 1), (1, 0)])


def after(first, *later):
    return lax.optimization_barrier((first,) + later)[1:]


def per_device(
    tokens,
    queries,
    grad_out,
    key_value_master_weight,
    key_value_first_moment,
    key_value_second_moment,
    writer,
):
    own_tokens, model_width = tokens.shape
    unit_scale = 1.0 / math.sqrt(model_width)
    length = queries.shape[0]
    rows = key_value_master_weight.shape[1]
    core = lax.axis_index("c")
    x_index, y_index = lax.axis_index("x"), lax.axis_index("y")
    t_index = lax.axis_index("t")
    g_index = 2 * lax.axis_index("zl") + core

    own_weight = key_value_master_weight.astype(BF)
    own_weight = jnp.concatenate([own_weight[0], own_weight[1]], axis=1)
    stage_parts = [to_heads(own_weight, k) for k in range(4)]
    stage = jnp.concatenate(stage_parts, axis=0)
    own_block = normed(tokens)
    from_z = swap_layers(after(stage_parts[0], own_block)[0])
    from_core = swap_cores(after(stage, own_block)[0])
    shard = jnp.concatenate([stage, near(stage, 1), near(stage, -1), near(stage, 2)], axis=0)
    pieces = [shard, far(shard, 1), far(shard, -1), far(shard, 2)]

    place = jnp.array(PLACES, jnp.int32)
    count = jnp.arange(4, dtype=jnp.int32)
    far_place = (jnp.where(core == 0, x_index, y_index) + place) % 4
    near_place = (jnp.where(core == 0, y_index, x_index) + place) % 4
    far_step = jnp.where(core == 0, 8 * rows, 2 * rows)
    near_step = jnp.where(core == 0, 2 * rows, 8 * rows)
    source = (t_index - count) % 4
    offsets = (
        far_place[:, None, None] * far_step
        + near_place[None, :, None] * near_step
        + ((source // 2) * (32 * rows) + (source % 2) * rows)[None, None, :]
    )
    offsets = offsets.reshape(64).astype(jnp.int32)
    sequence_order = ((t_index + count) % 4) ^ g_index
    block_order = (g_index - count) % 4

    cosines, sines = rope_tables(length, HEAD_SIZE)
    cosines = jnp.concatenate([cosines, cosines], axis=1)
    sines = jnp.concatenate([-sines, sines], axis=1)
    own_cos = lax.dynamic_slice_in_dim(cosines, t_index * own_tokens, own_tokens, 0)
    own_sin = lax.dynamic_slice_in_dim(sines, t_index * own_tokens, own_tokens, 0)
    rotated = rotated_queries(queries, cosines, sines)

    from_core, from_z, own_cos, own_sin, sequence_order, block_order, offsets = after(
        (pieces, rotated), from_core, from_z, own_cos, own_sin, sequence_order, block_order, offsets
    )
    blocks = [own_block, from_core, from_z, swap_cores(from_z)]
    weights, plain_early = project_early(offsets, blocks[0], blocks[1], pieces, unit_scale)
    plain, projected = project(
        sequence_order, blocks[2], blocks[3], weights, plain_early, own_cos, own_sin, unit_scale
    )
    arrived = [from_heads(block, k) for k, block in enumerate(projected)]
    returning, key, ds0, ds1 = attention(block_order, rotated, grad_out, arrived)
    back = [to_heads(block, -k) for k, block in enumerate(returning)]
    grad_q = grad_queries(queries, key, ds0, ds1, cosines, sines, 0)
    (back,) = after(grad_q, back)
    cotan = key_value_cotan(sequence_order, back, plain, own_cos, own_sin)

    part = weight_grads(offsets, blocks, cotan)
    arriving = [far(part[1], -1), far(part[2], 1), far(part[3], 2)]

    rows_of = after(part[0], cotan)[0].reshape(4, own_tokens, -1)
    sent = dot(jnp.concatenate([rows_of[1], rows_of[3]], axis=0), weights, NT) * unit_scale
    sent = sent.astype(BF)
    swapped = swap_cores(sent)
    (kept_from,) = after(sent, jnp.concatenate([rows_of[0], rows_of[2]], axis=0))
    kept = dot(kept_from, weights, NT) * unit_scale
    to_z = (kept[own_tokens:] + swapped[own_tokens:].astype(F32)).astype(BF)
    cuts = (0, 32, 80, own_tokens)
    to_z = [to_z[cuts[i] : cuts[i + 1]] for i in range(3)]
    z_first = swap_layers(to_z[0])

    kept, swapped = after(to_z, kept, swapped)
    mine = (kept[:own_tokens] + swapped[:own_tokens].astype(F32)).astype(BF)
    grad_x = grad_tokens(tokens, mine, z_first, 0)
    own_part, to_z[1], mine = after(grad_x, part[0], to_z[1], mine)
    own = sum_of(own_part, arriving, F32)
    z_second = swap_layers(to_z[1])
    summed = sum_of(own[0], [near(own[1], -1), near(own[2], 1), near(own[3], 2)], BF)
    grad_q = grad_queries(
        queries, key, after(own, ds0)[0], ds1, cosines, sines, queries.shape[1] // HEAD_SIZE // 2, grad_q
    )
    (summed,) = after((z_second, grad_q), summed)
    final = [from_heads(summed[k], -k) for k in range(4)]
    grad_x = grad_tokens(tokens, mine, after(summed, z_second)[0], cuts[1], grad_x)
    (final,) = after(grad_x, final)
    final = sum(block.astype(F32) for block in final) * unit_scale
    weight_grad = jnp.stack([final[:, :HEAD_SIZE], final[:, HEAD_SIZE:]], axis=0)

    (to_z[2],) = after(final, to_z[2])
    grad_x = grad_tokens(tokens, mine, swap_layers(to_z[2]), cuts[2], grad_x)

    new_first = beta_one * key_value_first_moment + (1.0 - beta_one) * weight_grad
    new_second = beta_two * key_value_second_moment + (1.0 - beta_two) * weight_grad * weight_grad
    first_hat = new_first / (1.0 - beta_one**step_count)
    second_hat = new_second / (1.0 - beta_two**step_count)
    new_master = key_value_master_weight - learn_rate * (
        first_hat / (jnp.sqrt(second_hat) + adam_eps) + weight_decay * key_value_master_weight
    )
    replicas = writer.shape[0]
    pieces = new_master.astype(BF).reshape(replicas, 2, -1)
    rank_ids = jnp.arange(replicas, dtype=jnp.int32)
    inverse = jnp.sum(jnp.where(writer[None, :] == rank_ids[:, None], rank_ids[None, :], 0), axis=1)
    outgoing = pieces.at[inverse].get(mode="promise_in_bounds")
    saved = lax.all_to_all(outgoing, ("zl", "x", "y", "c"), 0, 0, tiled=True)
    saved = after(grad_x, saved)[0].reshape(replicas, -1)
    return (grad_x, grad_q, new_master, new_first, new_second, saved)


def solution(mesh):
    fine = Mesh(mesh.devices.reshape(2, 4, 4, 2, 4), ("zl", "x", "y", "c", "t"))
    dp = ("zl", "x", "y", "c")
    every = dp + ("t",)
    weight = P(None, dp, "t")
    return jax.shard_map(
        per_device,
        mesh=fine,
        in_specs=(P(every, None), P(dp, "t"), P(dp, "t"), weight, weight, weight, P()),
        out_specs=(P(every, None), P(dp, "t"), weight, weight, weight, P(dp, "t")),
        check_vma=False,
    )
```

```python
import functools
import math

import jax
import jax.numpy as jnp
from jax import lax
from jax.experimental import pallas as pl
from jax.experimental.pallas import tpu as pltpu
from jax.sharding import Mesh, PartitionSpec as P

HEAD_SIZE = 128


norm_eps = 1e-06
rope_base = 1000000.0
beta_one = 0.9
beta_two = 0.95
adam_eps = 1e-08
learn_rate = 0.02
weight_decay = 0.1
step_count = 10.0


def rope_tables(length, head_width):
    half_width = head_width // 2
    index_float = jnp.arange(half_width, dtype=jnp.float32)
    inverse_freq = rope_base ** (-2.0 * index_float / head_width)
    positions = jnp.arange(length, dtype=jnp.float32)
    angles = positions[:, None] * inverse_freq[None, :]
    return (jnp.cos(angles), jnp.sin(angles))


BF = jnp.bfloat16
F32 = jnp.float32
HALF = HEAD_SIZE // 2
PLACES = (0, -1, 1, 2)
NT = (((1,), (1,)), ((), ()))
TT = (((0,), (0,)), ((), ()))


def dot(left, right, dims=None):
    if dims is None:
        dims = (((1,), (0,)), ((), ()))
    return lax.dot_general(left, right, dims, preferred_element_type=F32)


def params(mebibytes=20):
    return pltpu.CompilerParams(vmem_limit_bytes=mebibytes * 1024 * 1024)


def norm_scale(field):
    return lax.rsqrt(jnp.mean(field * field, axis=-1, keepdims=True) + norm_eps)


def norm_back(field, factor, cotan):
    return factor * cotan - field * (factor * factor * factor) * jnp.mean(
        cotan * field, axis=-1, keepdims=True
    )


def turn(field, cosines, sines):
    return field * cosines + pltpu.roll(field, HALF, 1) * sines


def query_kernel(q_ref, cos_ref, sin_ref, out_ref):
    field = q_ref[...].astype(F32)
    out_ref[...] = turn(field * norm_scale(field), cos_ref[...], sin_ref[...]).astype(BF)


def rotated_queries(queries, cosines, sines):
    length, width = queries.shape
    column = pl.BlockSpec((length, HEAD_SIZE), lambda h: (0, h))
    table = pl.BlockSpec((length, HEAD_SIZE), lambda h: (0, 0))
    return pl.pallas_call(
        query_kernel,
        grid=(width // HEAD_SIZE,),
        in_specs=[column, table, table],
        out_specs=column,
        out_shape=jax.ShapeDtypeStruct(queries.shape, BF),
        compiler_params=params(),
        name="query_rope",
    )(queries, cosines, sines)


def norm_kernel(in_ref, out_ref):
    field = in_ref[...].astype(F32)
    out_ref[...] = (field * norm_scale(field)).astype(BF)


def normed(tokens):
    block = pl.BlockSpec((tokens.shape[0] // 4, tokens.shape[1]), lambda i: (i, 0))
    return pl.pallas_call(
        norm_kernel,
        grid=(4,),
        in_specs=[block],
        out_specs=block,
        out_shape=jax.ShapeDtypeStruct(tokens.shape, BF),
        compiler_params=params(),
        name="norm",
    )(tokens)


def project_early_kernel(scale, offset_ref, first_ref, second_ref, *refs):
    w_refs, whole_ref, plain_ref = refs[:-2], refs[-2], refs[-1]
    block = whole_ref.shape[0] // offset_ref.shape[0]
    at = 0
    for w_ref in w_refs:
        count = w_ref.shape[0] // block
        for k in range(count):
            row = pl.ds(pl.multiple_of(offset_ref[at + k], 16), block)
            whole_ref[row, :] = w_ref[k * block : (k + 1) * block]
        at += count
    plain_ref[...] = rows_times(first_ref, second_ref, whole_ref) * scale


def rows_times(first_ref, second_ref, whole_ref):
    chunk = whole_ref.shape[0] // 4
    total = 0.0
    for j in range(4):
        columns = slice(j * chunk, (j + 1) * chunk)
        field = jnp.concatenate([first_ref[:, columns], second_ref[:, columns]], axis=0)
        total = total + dot(field, whole_ref[columns])
    return total


def project_early(offsets, first, second, pieces, scale):
    vmem = pl.BlockSpec(memory_space=pltpu.VMEM)
    shape = (first.shape[1], pieces[0].shape[1])
    return pl.pallas_call(
        functools.partial(project_early_kernel, scale),
        in_specs=[pl.BlockSpec(memory_space=pltpu.SMEM)] + [vmem] * (2 + len(pieces)),
        out_specs=[vmem, vmem],
        out_shape=[
            jax.ShapeDtypeStruct(shape, BF),
            jax.ShapeDtypeStruct((2 * first.shape[0], shape[1]), F32),
        ],
        compiler_params=params(48),
        name="project_early",
    )(offsets, first, second, *pieces)


def project_kernel(scale, order_ref, first_ref, second_ref, whole_ref, early_ref, cos_ref, sin_ref, plain_ref, *out_refs):
    tokens = cos_ref.shape[0]
    plain_ref[: 2 * tokens] = early_ref[...]
    plain_ref[2 * tokens :] = rows_times(first_ref, second_ref, whole_ref) * scale
    for k in range(4):
        rows = pl.ds(pl.multiple_of(order_ref[k] * tokens, tokens), tokens)
        u = plain_ref[rows, :HEAD_SIZE]
        out_refs[k][0] = turn(u * norm_scale(u), cos_ref[...], sin_ref[...]).astype(BF)
        out_refs[k][1] = plain_ref[rows, HEAD_SIZE:].astype(BF)


def project(order, first, second, weights, early, cosines, sines, scale):
    tokens = cosines.shape[0]
    vmem = pl.BlockSpec(memory_space=pltpu.VMEM)
    result = pl.pallas_call(
        functools.partial(project_kernel, scale),
        in_specs=[pl.BlockSpec(memory_space=pltpu.SMEM)] + [vmem] * 6,
        out_specs=[vmem] * 5,
        out_shape=[jax.ShapeDtypeStruct((4 * tokens, weights.shape[1]), F32)]
        + [jax.ShapeDtypeStruct((2, tokens, HEAD_SIZE), BF)] * 4,
        compiler_params=params(),
        name="project",
    )(order, first, second, weights, early, cosines, sines)
    return result[0], result[1:]


def sum_kernel(*refs):
    in_refs, out_refs = refs[:4], refs[4:]
    rows = out_refs[0].shape[0]
    for index, out_ref in enumerate(out_refs):
        part = slice(index * rows, (index + 1) * rows)
        total = sum(ref[part].astype(F32) for ref in in_refs[-3:]) + in_refs[0][part].astype(F32)
        out_ref[...] = total.astype(out_ref.dtype)


def sum_of(own, arrived, first_type):
    shape = (own.shape[0] // 4, own.shape[1])
    vmem = pl.BlockSpec(memory_space=pltpu.VMEM)
    return pl.pallas_call(
        sum_kernel,
        in_specs=[vmem] * 4,
        out_specs=[vmem] * 4,
        out_shape=[jax.ShapeDtypeStruct(shape, first_type)] + [jax.ShapeDtypeStruct(shape, BF)] * 3,
        compiler_params=params(),
        name="sum",
    )(own, *arrived)


def turn_kernel(offset_ref, first_ref, second_ref, out_ref, scratch):
    rows = first_ref.shape[0]
    block = scratch.shape[0] // offset_ref.shape[0]
    chunk = scratch.shape[0] // 8
    for j in range(8):
        columns = slice(j * chunk, (j + 1) * chunk)
        scratch[columns, :rows] = first_ref[:, columns].T
        scratch[columns, rows:] = second_ref[:, columns].T
    for k in range(offset_ref.shape[0]):
        row = pl.ds(pl.multiple_of(offset_ref[k], 16), block)
        out_ref[k * block : (k + 1) * block] = scratch[row, :]


def turned(offsets, first, second):
    shape = (first.shape[1], 2 * first.shape[0])
    vmem = pl.BlockSpec(memory_space=pltpu.VMEM)
    return pl.pallas_call(
        turn_kernel,
        in_specs=[pl.BlockSpec(memory_space=pltpu.SMEM), vmem, vmem],
        out_specs=vmem,
        out_shape=jax.ShapeDtypeStruct(shape, BF),
        scratch_shapes=[pltpu.VMEM(shape, BF)],
        compiler_params=params(),
        name="turn",
    )(offsets, first, second)


def weight_grad_kernel(early_ref, late_ref, cotan_ref, *out_refs):
    rows = out_refs[0].shape[0]
    for index, out_ref in enumerate(out_refs):
        part = slice(index * rows, (index + 1) * rows)
        field = jnp.concatenate([early_ref[part], late_ref[part]], axis=1)
        out_ref[...] = dot(field, cotan_ref[...]).astype(BF)


def weight_grads(early, late, cotan):
    vmem = pl.BlockSpec(memory_space=pltpu.VMEM)
    shape = (early.shape[0] // 4, cotan.shape[1])
    return pl.pallas_call(
        weight_grad_kernel,
        in_specs=[vmem] * 3,
        out_specs=[vmem] * 4,
        out_shape=[jax.ShapeDtypeStruct(shape, BF)] * 4,
        compiler_params=params(),
        name="weight_grads",
    )(early, late, cotan)


def attention_kernel(order_ref, q_ref, g_ref, *refs):
    kv_refs, dkv_refs = refs[:4], refs[4:8]
    k_ref, ds0_ref, ds1_ref, v_ref, dk_acc, dv_acc = refs[8:]
    step = pl.program_id(0)
    length, width = q_ref.shape
    tokens, mid, heads = length // 4, length // 2, width // HEAD_SIZE
    scale = 1.0 / math.sqrt(HEAD_SIZE)

    @pl.when(step == 0)
    def _():
        dk_acc[...] = jnp.zeros_like(dk_acc)
        dv_acc[...] = jnp.zeros_like(dv_acc)
        for k in range(4):
            rows = pl.ds(pl.multiple_of(order_ref[k] * tokens, tokens), tokens)
            k_ref[rows, :] = kv_refs[k][0]
            v_ref[rows, :] = kv_refs[k][1]

    early, late = slice(0, mid), slice(mid, length)
    row = lax.broadcasted_iota(jnp.int32, (mid, mid), 0)
    column = lax.broadcasted_iota(jnp.int32, (mid, mid), 1)
    allowed = row <= column
    factor = scale * math.log2(math.e)
    each = range(heads)

    def at(ref, rows, h):
        return ref[rows, h * HEAD_SIZE : (h + 1) * HEAD_SIZE]

    def products(left_ref, right_ref):
        return [
            [
                dot(left_ref[early], at(right_ref, early, h), NT),
                dot(left_ref[early], at(right_ref, late, h), NT),
                dot(left_ref[late], at(right_ref, late, h), NT),
            ]
            for h in each
        ]

    def add(acc, terms, right_ref):
        acc[early] += sum(
            dot(terms[h][0], at(right_ref, early, h)) + dot(terms[h][1], at(right_ref, late, h))
            for h in each
        )
        acc[late] += sum(dot(terms[h][2], at(right_ref, late, h)) for h in each)

    def column_sums(terms):
        first, second, third = (jnp.sum(term, axis=0, keepdims=True) for term in terms)
        return first, second + third

    scores = products(k_ref, q_ref)
    d_probs = products(v_ref, g_ref)
    probs = []
    for h in each:
        a, b, c = scores[h]
        a = jnp.where(allowed, jnp.exp2(a * factor), 0.0)
        b = jnp.exp2(b * factor)
        c = jnp.where(allowed, jnp.exp2(c * factor), 0.0)
        sum_a, sum_b = column_sums((a, b, c))
        inv_a, inv_b = 1.0 / sum_a, 1.0 / sum_b
        probs.append((a * inv_a, b * inv_b, c * inv_b))
    add(dv_acc, [[term.astype(BF) for term in probs[h]] for h in each], g_ref)
    d_scores = []
    for h in each:
        sum_a, sum_b = column_sums([p * d for p, d in zip(probs[h], d_probs[h])])
        d_scores.append(
            [
                (p * (d - total)).astype(BF)
                for p, d, total in zip(probs[h], d_probs[h], (sum_a, sum_b, sum_b))
            ]
        )
        ds0_ref[h, :, :mid] = d_scores[h][0]
        ds0_ref[h, :, mid:] = d_scores[h][1]
        ds1_ref[h] = d_scores[h][2]
    add(dk_acc, d_scores, q_ref)

    @pl.when(step == pl.num_programs(0) - 1)
    def _():
        for k in range(4):
            rows = pl.ds(pl.multiple_of(order_ref[k] * tokens, tokens), tokens)
            dkv_refs[k][0] = (dk_acc[rows, :] * scale).astype(BF)
            dkv_refs[k][1] = dv_acc[rows, :].astype(BF)


def attention(order, rotated, incoming, pieces):
    length, width = rotated.shape
    heads, mid, pair = width // HEAD_SIZE, length // 2, 2
    columns = pl.BlockSpec((length, pair * HEAD_SIZE), lambda h: (0, h))
    whole = pl.BlockSpec((length, HEAD_SIZE), lambda h: (0, 0))
    piece = pl.BlockSpec(pieces[0].shape, lambda h: (0, 0, 0))
    result = pl.pallas_call(
        attention_kernel,
        grid=(heads // pair,),
        in_specs=[pl.BlockSpec(memory_space=pltpu.SMEM), columns, columns] + [piece] * 4,
        out_specs=[piece] * 4
        + [
            whole,
            pl.BlockSpec((pair, mid, length), lambda h: (h, 0, 0)),
            pl.BlockSpec((pair, mid, mid), lambda h: (h, 0, 0)),
        ],
        out_shape=[jax.ShapeDtypeStruct(pieces[0].shape, BF)] * 4
        + [
            jax.ShapeDtypeStruct((length, HEAD_SIZE), BF),
            jax.ShapeDtypeStruct((heads, mid, length), BF),
            jax.ShapeDtypeStruct((heads, mid, mid), BF),
        ],
        scratch_shapes=[pltpu.VMEM((length, HEAD_SIZE), BF)]
        + [pltpu.VMEM((length, HEAD_SIZE), F32)] * 2,
        compiler_params=params(32),
        name="attention",
    )(order, rotated, incoming, *pieces)
    return result[:4], result[4], result[5], result[6]


def grad_query_kernel(q_ref, k_ref, ds0_ref, ds1_ref, cos_ref, sin_ref, *refs):
    out_ref = refs[-1]
    mid = ds0_ref.shape[1]
    scale = 1.0 / math.sqrt(HEAD_SIZE)
    k0, k1 = k_ref[:mid], k_ref[mid:]
    both = dot(k0, ds0_ref[0], TT)
    early = both[:, :mid]
    late = both[:, mid:] + dot(k1, ds1_ref[0], TT)
    cotan = jnp.concatenate([early.T, late.T], axis=0) * scale
    field = q_ref[...].astype(F32)
    cotan = turn(cotan, cos_ref[...], -sin_ref[...])
    out_ref[...] = norm_back(field, norm_scale(field), cotan).astype(BF)


def grad_queries(queries, key, ds0, ds1, cosines, sines, first, given=None):
    length, width = queries.shape
    heads, mid = width // HEAD_SIZE, length // 2
    column = pl.BlockSpec((length, HEAD_SIZE), lambda h: (0, first + h))
    whole = pl.BlockSpec((length, HEAD_SIZE), lambda h: (0, 0))
    specs = [
        column,
        whole,
        pl.BlockSpec((1, mid, length), lambda h: (first + h, 0, 0)),
        pl.BlockSpec((1, mid, mid), lambda h: (first + h, 0, 0)),
        whole,
        whole,
    ]
    operands = [queries, key, ds0, ds1, cosines, sines]
    if given is not None:
        specs.append(pl.BlockSpec(memory_space=pl.ANY))
        operands.append(given)
    return pl.pallas_call(
        grad_query_kernel,
        grid=(heads // 2,),
        in_specs=specs,
        out_specs=column,
        out_shape=jax.ShapeDtypeStruct(queries.shape, BF),
        input_output_aliases={} if given is None else {6: 0},
        compiler_params=params(16),
        name="grad_query",
    )(*operands)


def cotan_kernel(order_ref, b0_ref, b1_ref, b2_ref, b3_ref, plain_ref, cos_ref, sin_ref, out_ref):
    tokens = cos_ref.shape[0]
    for k, back_ref in enumerate((b0_ref, b1_ref, b2_ref, b3_ref)):
        rows = pl.ds(pl.multiple_of(order_ref[k] * tokens, tokens), tokens)
        u = plain_ref[rows, :HEAD_SIZE]
        back = turn(back_ref[0].astype(F32), cos_ref[...], -sin_ref[...])
        out_ref[rows, :HEAD_SIZE] = norm_back(u, norm_scale(u), back).astype(BF)
        out_ref[rows, HEAD_SIZE:] = back_ref[1]


def key_value_cotan(order, back, plain, cosines, sines):
    vmem = pl.BlockSpec(memory_space=pltpu.VMEM)
    return pl.pallas_call(
        cotan_kernel,
        in_specs=[pl.BlockSpec(memory_space=pltpu.SMEM)] + [vmem] * 7,
        out_specs=vmem,
        out_shape=jax.ShapeDtypeStruct(plain.shape, BF),
        compiler_params=params(),
        name="key_value_cotan",
    )(order, *back, plain, cosines, sines)


def grad_token_kernel(x_ref, mine_ref, layer_ref, *refs):
    out_ref = refs[-1]
    cotan = mine_ref[...].astype(F32) + layer_ref[...].astype(F32)
    field = x_ref[...].astype(F32)
    out_ref[...] = norm_back(field, norm_scale(field), cotan).astype(BF)


def grad_tokens(tokens, mine, from_layer, start, given=None):
    step, width = from_layer.shape[0], tokens.shape[1]
    first = start // step
    here = pl.BlockSpec((step, width), lambda i: (first + i, 0))
    specs = [here, here, pl.BlockSpec((step, width), lambda i: (i, 0))]
    operands = [tokens, mine, from_layer]
    if given is not None:
        specs.append(pl.BlockSpec(memory_space=pl.ANY))
        operands.append(given)
    return pl.pallas_call(
        grad_token_kernel,
        grid=(from_layer.shape[0] // step,),
        in_specs=specs,
        out_specs=here,
        out_shape=jax.ShapeDtypeStruct(tokens.shape, BF),
        input_output_aliases={} if given is None else {3: 0},
        compiler_params=params(60),
        name="grad_tokens",
    )(*operands)


def plane_pairs(first, step):
    pairs = []
    for x in range(4):
        for y in range(4):
            for c in range(2):
                along_x = (c == 0) == first
                to_x = (x + step) % 4 if along_x else x
                to_y = y if along_x else (y + step) % 4
                pairs.append(((x * 4 + y) * 2 + c, (to_x * 4 + to_y) * 2 + c))
    return pairs


def far(block, step):
    return lax.ppermute(block, ("x", "y", "c"), plane_pairs(True, step))


def near(block, step):
    return lax.ppermute(block, ("x", "y", "c"), plane_pairs(False, step))


def swap_cores(block):
    return lax.ppermute(block, "c", [(0, 1), (1, 0)])


def group_pairs(target):
    pairs = []
    for g in range(4):
        for t in range(4):
            to_g, to_t = target(g, t)
            pairs.append((g * 4 + t, (to_g % 4) * 4 + to_t % 4))
    return pairs


def to_heads(block, k):
    return lax.ppermute(block, ("zl", "c", "t"), group_pairs(lambda g, t: (t, g + k)))


def from_heads(block, k):
    return lax.ppermute(block, ("zl", "c", "t"), group_pairs(lambda g, t: (t + k, g)))


def swap_layers(block):
    return lax.ppermute(block, "zl", [(0, 1), (1, 0)])


def after(first, *later):
    return lax.optimization_barrier((first,) + later)[1:]


def per_device(
    tokens,
    queries,
    grad_out,
    key_value_master_weight,
    key_value_first_moment,
    key_value_second_moment,
    writer,
):
    own_tokens, model_width = tokens.shape
    unit_scale = 1.0 / math.sqrt(model_width)
    length = queries.shape[0]
    rows = key_value_master_weight.shape[1]
    core = lax.axis_index("c")
    x_index, y_index = lax.axis_index("x"), lax.axis_index("y")
    t_index = lax.axis_index("t")
    g_index = 2 * lax.axis_index("zl") + core

    own_weight = key_value_master_weight.astype(BF)
    own_weight = jnp.concatenate([own_weight[0], own_weight[1]], axis=1)
    stage_parts = [to_heads(own_weight, k) for k in range(4)]
    stage = jnp.concatenate(stage_parts, axis=0)
    own_block = normed(tokens)
    from_z = swap_layers(after(stage_parts[0], own_block)[0])
    from_core = swap_cores(own_block)
    shard = jnp.concatenate([stage, near(stage, 1), near(stage, -1), near(stage, 2)], axis=0)
    pieces = [shard, far(shard, 1), far(shard, -1), far(shard, 2)]

    place = jnp.array(PLACES, jnp.int32)
    count = jnp.arange(4, dtype=jnp.int32)
    far_place = (jnp.where(core == 0, x_index, y_index) + place) % 4
    near_place = (jnp.where(core == 0, y_index, x_index) + place) % 4
    far_step = jnp.where(core == 0, 8 * rows, 2 * rows)
    near_step = jnp.where(core == 0, 2 * rows, 8 * rows)
    source = (t_index - count) % 4
    offsets = (
        far_place[:, None, None] * far_step
        + near_place[None, :, None] * near_step
        + ((source // 2) * (32 * rows) + (source % 2) * rows)[None, None, :]
    )
    offsets = offsets.reshape(64).astype(jnp.int32)
    sequence_order = ((t_index + count) % 4) ^ g_index
    block_order = (g_index - count) % 4

    cosines, sines = rope_tables(length, HEAD_SIZE)
    cosines = jnp.concatenate([cosines, cosines], axis=1)
    sines = jnp.concatenate([-sines, sines], axis=1)
    own_cos = lax.dynamic_slice_in_dim(cosines, t_index * own_tokens, own_tokens, 0)
    own_sin = lax.dynamic_slice_in_dim(sines, t_index * own_tokens, own_tokens, 0)
    rotated = rotated_queries(queries, cosines, sines)

    early = turned(offsets, own_block, from_core)
    from_core, from_z, own_cos, own_sin, sequence_order, block_order, offsets = after(
        (pieces, rotated, early), from_core, from_z, own_cos, own_sin, sequence_order, block_order, offsets
    )
    blocks = [own_block, from_core, from_z, swap_cores(from_z)]
    weights, plain_early = project_early(offsets, blocks[0], blocks[1], pieces, unit_scale)
    plain, projected = project(
        sequence_order, blocks[2], blocks[3], weights, plain_early, own_cos, own_sin, unit_scale
    )
    arrived = [from_heads(block, k) for k, block in enumerate(projected)]
    late = turned(offsets, *after(plain, blocks[2], blocks[3]))
    (arrived,) = after(late, arrived)

    returning, key, ds0, ds1 = attention(block_order, rotated, grad_out, arrived)
    back = [to_heads(block, -k) for k, block in enumerate(returning)]
    grad_q = grad_queries(queries, key, ds0, ds1, cosines, sines, 0)
    (back,) = after(grad_q, back)
    cotan = key_value_cotan(sequence_order, back, plain, own_cos, own_sin)

    part = weight_grads(early, late, cotan)
    arriving = [far(part[1], -1), far(part[2], 1), far(part[3], 2)]

    rows_of = after(part[0], cotan)[0].reshape(4, own_tokens, -1)
    sent = dot(jnp.concatenate([rows_of[1], rows_of[3]], axis=0), weights, NT) * unit_scale
    sent = sent.astype(BF)
    swapped = swap_cores(sent)
    (kept_from,) = after(sent, jnp.concatenate([rows_of[0], rows_of[2]], axis=0))
    kept = dot(kept_from, weights, NT) * unit_scale
    to_z = (kept[own_tokens:] + swapped[own_tokens:].astype(F32)).astype(BF)
    starts, cut = (96, 0, 48), (96, 48)
    to_z = [to_z[cut[0] :], to_z[: cut[1]], to_z[cut[1] : cut[0]]]
    z_first = swap_layers(to_z[0])

    kept, swapped = after(to_z, kept, swapped)
    mine = (kept[:own_tokens] + swapped[:own_tokens].astype(F32)).astype(BF)
    grad_x = grad_tokens(tokens, mine, z_first, starts[0])
    own_part, to_z[1], mine = after(grad_x, part[0], to_z[1], mine)
    own = sum_of(own_part, arriving, F32)
    z_second = swap_layers(to_z[1])
    summed = sum_of(own[0], [near(own[1], -1), near(own[2], 1), near(own[3], 2)], BF)
    grad_q = grad_queries(
        queries, key, after(own, ds0)[0], ds1, cosines, sines, queries.shape[1] // HEAD_SIZE // 2, grad_q
    )
    (summed,) = after((z_second, grad_q), summed)
    final = [from_heads(summed[k], -k) for k in range(4)]
    grad_x = grad_tokens(tokens, mine, after(summed, z_second)[0], starts[1], grad_x)
    (final,) = after(grad_x, final)
    final = sum(block.astype(F32) for block in final) * unit_scale
    weight_grad = jnp.stack([final[:, :HEAD_SIZE], final[:, HEAD_SIZE:]], axis=0)

    (to_z[2],) = after(final, to_z[2])
    grad_x = grad_tokens(tokens, mine, swap_layers(to_z[2]), starts[2], grad_x)

    new_first = beta_one * key_value_first_moment + (1.0 - beta_one) * weight_grad
    new_second = beta_two * key_value_second_moment + (1.0 - beta_two) * weight_grad * weight_grad
    first_hat = new_first / (1.0 - beta_one**step_count)
    second_hat = new_second / (1.0 - beta_two**step_count)
    new_master = key_value_master_weight - learn_rate * (
        first_hat / (jnp.sqrt(second_hat) + adam_eps) + weight_decay * key_value_master_weight
    )
    replicas = writer.shape[0]
    pieces = new_master.astype(BF).reshape(replicas, 2, -1)
    rank_ids = jnp.arange(replicas, dtype=jnp.int32)
    inverse = jnp.sum(jnp.where(writer[None, :] == rank_ids[:, None], rank_ids[None, :], 0), axis=1)
    outgoing = pieces.at[inverse].get(mode="promise_in_bounds")
    saved = lax.all_to_all(outgoing, ("zl", "x", "y", "c"), 0, 0, tiled=True)
    saved = after(grad_x, saved)[0].reshape(replicas, -1)
    return (grad_x, grad_q, new_master, new_first, new_second, saved)


def solution(mesh):
    fine = Mesh(mesh.devices.reshape(2, 4, 4, 2, 4), ("zl", "x", "y", "c", "t"))
    dp = ("zl", "x", "y", "c")
    every = dp + ("t",)
    weight = P(None, dp, "t")
    return jax.shard_map(
        per_device,
        mesh=fine,
        in_specs=(P(every, None), P(dp, "t"), P(dp, "t"), weight, weight, weight, P()),
        out_specs=(P(every, None), P(dp, "t"), weight, weight, weight, P(dp, "t")),
        check_vma=False,
    )
```

```python
import functools
import math

import jax
import jax.numpy as jnp
from jax import lax
from jax.experimental import pallas as pl
from jax.experimental.pallas import tpu as pltpu
from jax.sharding import Mesh, PartitionSpec as P

HEAD_SIZE = 128


norm_eps = 1e-06
rope_base = 1000000.0
beta_one = 0.9
beta_two = 0.95
adam_eps = 1e-08
learn_rate = 0.02
weight_decay = 0.1
step_count = 10.0


def rope_tables(length, head_width):
    half_width = head_width // 2
    index_float = jnp.arange(half_width, dtype=jnp.float32)
    inverse_freq = rope_base ** (-2.0 * index_float / head_width)
    positions = jnp.arange(length, dtype=jnp.float32)
    angles = positions[:, None] * inverse_freq[None, :]
    return (jnp.cos(angles), jnp.sin(angles))


BF = jnp.bfloat16
F32 = jnp.float32
HALF = HEAD_SIZE // 2
PLACES = (0, -1, 1, 2)
NT = (((1,), (1,)), ((), ()))
TT = (((0,), (0,)), ((), ()))


def dot(left, right, dims=None):
    if dims is None:
        dims = (((1,), (0,)), ((), ()))
    return lax.dot_general(left, right, dims, preferred_element_type=F32)


def params(mebibytes=20):
    return pltpu.CompilerParams(vmem_limit_bytes=mebibytes * 1024 * 1024)


def norm_scale(field):
    return lax.rsqrt(jnp.mean(field * field, axis=-1, keepdims=True) + norm_eps)


def norm_back(field, factor, cotan):
    return factor * cotan - field * (factor * factor * factor) * jnp.mean(
        cotan * field, axis=-1, keepdims=True
    )


def turn(field, cosines, sines):
    return field * cosines + pltpu.roll(field, HALF, 1) * sines


def query_kernel(q_ref, cos_ref, sin_ref, out_ref):
    field = q_ref[...].astype(F32)
    out_ref[...] = turn(field * norm_scale(field), cos_ref[...], sin_ref[...]).astype(BF)


def rotated_queries(queries, cosines, sines):
    length, width = queries.shape
    column = pl.BlockSpec((length, HEAD_SIZE), lambda h: (0, h))
    table = pl.BlockSpec((length, HEAD_SIZE), lambda h: (0, 0))
    return pl.pallas_call(
        query_kernel,
        grid=(width // HEAD_SIZE,),
        in_specs=[column, table, table],
        out_specs=column,
        out_shape=jax.ShapeDtypeStruct(queries.shape, BF),
        compiler_params=params(),
        name="query_rope",
    )(queries, cosines, sines)


def row_loop(rows, step, body):
    def run(i, carry):
        body(pl.ds(pl.multiple_of(i * step, step), step))
        return carry

    lax.fori_loop(0, rows // step, run, 0)


def norm_kernel(in_ref, out_ref):
    def body(rows):
        field = in_ref[rows, :].astype(F32)
        out_ref[rows, :] = (field * norm_scale(field)).astype(BF)

    row_loop(in_ref.shape[0], 16, body)


def normed(tokens):
    block = pl.BlockSpec((tokens.shape[0] // 4, tokens.shape[1]), lambda i: (i, 0))
    return pl.pallas_call(
        norm_kernel,
        grid=(4,),
        in_specs=[block],
        out_specs=block,
        out_shape=jax.ShapeDtypeStruct(tokens.shape, BF),
        compiler_params=params(),
        name="norm",
    )(tokens)


def project_early_kernel(scale, offset_ref, first_ref, second_ref, *refs):
    w_refs, whole_ref, plain_ref = refs[:-2], refs[-2], refs[-1]
    block = whole_ref.shape[0] // offset_ref.shape[0]
    at = 0
    for w_ref in w_refs:
        count = w_ref.shape[0] // block

        def body(k, carry, at=at, w_ref=w_ref):
            row = pl.ds(pl.multiple_of(offset_ref[at + k], 16), block)
            whole_ref[row, :] = w_ref[pl.ds(pl.multiple_of(k * block, 16), block), :]
            return carry

        lax.fori_loop(0, count, body, 0)
        at += count
    plain_ref[...] = rows_times(first_ref, second_ref, whole_ref) * scale


def rows_times(first_ref, second_ref, whole_ref):
    chunk = whole_ref.shape[0] // 4
    total = 0.0
    for j in range(4):
        columns = slice(j * chunk, (j + 1) * chunk)
        field = jnp.concatenate([first_ref[:, columns], second_ref[:, columns]], axis=0)
        total = total + dot(field, whole_ref[columns])
    return total


def project_early(offsets, first, second, pieces, scale):
    vmem = pl.BlockSpec(memory_space=pltpu.VMEM)
    shape = (first.shape[1], pieces[0].shape[1])
    return pl.pallas_call(
        functools.partial(project_early_kernel, scale),
        in_specs=[pl.BlockSpec(memory_space=pltpu.SMEM)] + [vmem] * (2 + len(pieces)),
        out_specs=[vmem, vmem],
        out_shape=[
            jax.ShapeDtypeStruct(shape, BF),
            jax.ShapeDtypeStruct((2 * first.shape[0], shape[1]), F32),
        ],
        compiler_params=params(),
        name="project_early",
    )(offsets, first, second, *pieces)


def project_kernel(scale, order_ref, first_ref, second_ref, whole_ref, early_ref, cos_ref, sin_ref, plain_ref, *out_refs):
    tokens = cos_ref.shape[0]
    plain_ref[: 2 * tokens] = early_ref[...]
    plain_ref[2 * tokens :] = rows_times(first_ref, second_ref, whole_ref) * scale
    for k in range(4):
        rows = pl.ds(pl.multiple_of(order_ref[k] * tokens, tokens), tokens)
        u = plain_ref[rows, :HEAD_SIZE]
        out_refs[k][0] = turn(u * norm_scale(u), cos_ref[...], sin_ref[...]).astype(BF)
        out_refs[k][1] = plain_ref[rows, HEAD_SIZE:].astype(BF)


def project(order, first, second, weights, early, cosines, sines, scale):
    tokens = cosines.shape[0]
    vmem = pl.BlockSpec(memory_space=pltpu.VMEM)
    result = pl.pallas_call(
        functools.partial(project_kernel, scale),
        in_specs=[pl.BlockSpec(memory_space=pltpu.SMEM)] + [vmem] * 6,
        out_specs=[vmem] * 5,
        out_shape=[jax.ShapeDtypeStruct((4 * tokens, weights.shape[1]), F32)]
        + [jax.ShapeDtypeStruct((2, tokens, HEAD_SIZE), BF)] * 4,
        compiler_params=params(),
        name="project",
    )(order, first, second, weights, early, cosines, sines)
    return result[0], result[1:]


def sum_kernel(*refs):
    in_refs, out_refs = refs[:4], refs[4:]
    rows = out_refs[0].shape[0]
    for index, out_ref in enumerate(out_refs):
        part = slice(index * rows, (index + 1) * rows)
        total = sum(ref[part].astype(F32) for ref in in_refs[-3:]) + in_refs[0][part].astype(F32)
        out_ref[...] = total.astype(out_ref.dtype)


def sum_of(own, arrived, first_type):
    shape = (own.shape[0] // 4, own.shape[1])
    vmem = pl.BlockSpec(memory_space=pltpu.VMEM)
    return pl.pallas_call(
        sum_kernel,
        in_specs=[vmem] * 4,
        out_specs=[vmem] * 4,
        out_shape=[jax.ShapeDtypeStruct(shape, first_type)] + [jax.ShapeDtypeStruct(shape, BF)] * 3,
        compiler_params=params(),
        name="sum",
    )(own, *arrived)


def turn_kernel(offset_ref, first_ref, second_ref, out_ref, scratch):
    rows = first_ref.shape[0]
    block = scratch.shape[0] // offset_ref.shape[0]

    def turn_some(columns):
        scratch[columns, :rows] = first_ref[:, columns].T
        scratch[columns, rows:] = second_ref[:, columns].T

    row_loop(scratch.shape[0], 512, turn_some)

    def body(k, carry):
        row = pl.ds(pl.multiple_of(offset_ref[k], 16), block)
        out_ref[pl.ds(pl.multiple_of(k * block, 16), block), :] = scratch[row, :]
        return carry

    lax.fori_loop(0, offset_ref.shape[0], body, 0)


def turned(offsets, first, second):
    shape = (first.shape[1], 2 * first.shape[0])
    vmem = pl.BlockSpec(memory_space=pltpu.VMEM)
    return pl.pallas_call(
        turn_kernel,
        in_specs=[pl.BlockSpec(memory_space=pltpu.SMEM), vmem, vmem],
        out_specs=vmem,
        out_shape=jax.ShapeDtypeStruct(shape, BF),
        scratch_shapes=[pltpu.VMEM(shape, BF)],
        compiler_params=params(),
        name="turn",
    )(offsets, first, second)


def weight_grad_kernel(quarters, early_ref, late_ref, cotan_ref, *out_refs):
    rows = out_refs[0].shape[0]
    for index, out_ref in zip(quarters, out_refs):
        part = slice(index * rows, (index + 1) * rows)
        field = jnp.concatenate([early_ref[part], late_ref[part]], axis=1)
        out_ref[...] = dot(field, cotan_ref[...]).astype(BF)


def weight_grads(early, late, cotan, quarters):
    vmem = pl.BlockSpec(memory_space=pltpu.VMEM)
    shape = (early.shape[0] // 4, cotan.shape[1])
    return pl.pallas_call(
        functools.partial(weight_grad_kernel, quarters),
        in_specs=[vmem] * 3,
        out_specs=[vmem] * len(quarters),
        out_shape=[jax.ShapeDtypeStruct(shape, BF)] * len(quarters),
        compiler_params=params(),
        name="weight_grads",
    )(early, late, cotan)


def attention_kernel(order_ref, q_ref, g_ref, *refs):
    kv_refs, dkv_refs = refs[:4], refs[4:8]
    k_ref, ds0_ref, ds1_ref, v_ref, dk_acc, dv_acc = refs[8:]
    step = pl.program_id(0)
    length, width = q_ref.shape
    tokens, mid, heads = length // 4, length // 2, width // HEAD_SIZE
    scale = 1.0 / math.sqrt(HEAD_SIZE)

    @pl.when(step == 0)
    def _():
        dk_acc[...] = jnp.zeros_like(dk_acc)
        dv_acc[...] = jnp.zeros_like(dv_acc)
        for k in range(4):
            rows = pl.ds(pl.multiple_of(order_ref[k] * tokens, tokens), tokens)
            k_ref[rows, :] = kv_refs[k][0]
            v_ref[rows, :] = kv_refs[k][1]

    early, late = slice(0, mid), slice(mid, length)
    row = lax.broadcasted_iota(jnp.int32, (mid, mid), 0)
    column = lax.broadcasted_iota(jnp.int32, (mid, mid), 1)
    allowed = row <= column
    factor = scale * math.log2(math.e)
    each = range(heads)

    def at(ref, rows, h):
        return ref[rows, h * HEAD_SIZE : (h + 1) * HEAD_SIZE]

    def products(left_ref, right_ref):
        return [
            [
                dot(left_ref[early], at(right_ref, early, h), NT),
                dot(left_ref[early], at(right_ref, late, h), NT),
                dot(left_ref[late], at(right_ref, late, h), NT),
            ]
            for h in each
        ]

    def add(acc, terms, right_ref):
        acc[early] += sum(
            dot(terms[h][0], at(right_ref, early, h)) + dot(terms[h][1], at(right_ref, late, h))
            for h in each
        )
        acc[late] += sum(dot(terms[h][2], at(right_ref, late, h)) for h in each)

    def column_sums(terms):
        first, second, third = (jnp.sum(term, axis=0, keepdims=True) for term in terms)
        return first, second + third

    scores = products(k_ref, q_ref)
    d_probs = products(v_ref, g_ref)
    probs = []
    for h in each:
        a, b, c = scores[h]
        a = jnp.where(allowed, jnp.exp2(a * factor), 0.0)
        b = jnp.exp2(b * factor)
        c = jnp.where(allowed, jnp.exp2(c * factor), 0.0)
        sum_a, sum_b = column_sums((a, b, c))
        inv_a, inv_b = 1.0 / sum_a, 1.0 / sum_b
        probs.append((a * inv_a, b * inv_b, c * inv_b))
    add(dv_acc, [[term.astype(BF) for term in probs[h]] for h in each], g_ref)
    d_scores = []
    for h in each:
        sum_a, sum_b = column_sums([p * d for p, d in zip(probs[h], d_probs[h])])
        d_scores.append(
            [
                (p * (d - total)).astype(BF)
                for p, d, total in zip(probs[h], d_probs[h], (sum_a, sum_b, sum_b))
            ]
        )
        ds0_ref[h, :, :mid] = d_scores[h][0]
        ds0_ref[h, :, mid:] = d_scores[h][1]
        ds1_ref[h] = d_scores[h][2]
    add(dk_acc, d_scores, q_ref)

    @pl.when(step == pl.num_programs(0) - 1)
    def _():
        for k in range(4):
            rows = pl.ds(pl.multiple_of(order_ref[k] * tokens, tokens), tokens)
            dkv_refs[k][0] = (dk_acc[rows, :] * scale).astype(BF)
            dkv_refs[k][1] = dv_acc[rows, :].astype(BF)


def attention(order, rotated, incoming, pieces):
    length, width = rotated.shape
    heads, mid, pair = width // HEAD_SIZE, length // 2, 2
    columns = pl.BlockSpec((length, pair * HEAD_SIZE), lambda h: (0, h))
    whole = pl.BlockSpec((length, HEAD_SIZE), lambda h: (0, 0))
    piece = pl.BlockSpec(pieces[0].shape, lambda h: (0, 0, 0))
    result = pl.pallas_call(
        attention_kernel,
        grid=(heads // pair,),
        in_specs=[pl.BlockSpec(memory_space=pltpu.SMEM), columns, columns] + [piece] * 4,
        out_specs=[piece] * 4
        + [
            whole,
            pl.BlockSpec((pair, mid, length), lambda h: (h, 0, 0)),
            pl.BlockSpec((pair, mid, mid), lambda h: (h, 0, 0)),
        ],
        out_shape=[jax.ShapeDtypeStruct(pieces[0].shape, BF)] * 4
        + [
            jax.ShapeDtypeStruct((length, HEAD_SIZE), BF),
            jax.ShapeDtypeStruct((heads, mid, length), BF),
            jax.ShapeDtypeStruct((heads, mid, mid), BF),
        ],
        scratch_shapes=[pltpu.VMEM((length, HEAD_SIZE), BF)]
        + [pltpu.VMEM((length, HEAD_SIZE), F32)] * 2,
        compiler_params=params(32),
        name="attention",
    )(order, rotated, incoming, *pieces)
    return result[:4], result[4], result[5], result[6]


def grad_query_kernel(q_ref, k_ref, ds0_ref, ds1_ref, cos_ref, sin_ref, *refs):
    out_ref = refs[-1]
    mid = ds0_ref.shape[1]
    scale = 1.0 / math.sqrt(HEAD_SIZE)
    k0, k1 = k_ref[:mid], k_ref[mid:]
    both = dot(k0, ds0_ref[0], TT)
    early = both[:, :mid]
    late = both[:, mid:] + dot(k1, ds1_ref[0], TT)
    cotan = jnp.concatenate([early.T, late.T], axis=0) * scale
    field = q_ref[...].astype(F32)
    cotan = turn(cotan, cos_ref[...], -sin_ref[...])
    out_ref[...] = norm_back(field, norm_scale(field), cotan).astype(BF)


def grad_queries(queries, key, ds0, ds1, cosines, sines, first, given=None):
    length, width = queries.shape
    heads, mid = width // HEAD_SIZE, length // 2
    column = pl.BlockSpec((length, HEAD_SIZE), lambda h: (0, first + h))
    whole = pl.BlockSpec((length, HEAD_SIZE), lambda h: (0, 0))
    specs = [
        column,
        whole,
        pl.BlockSpec((1, mid, length), lambda h: (first + h, 0, 0)),
        pl.BlockSpec((1, mid, mid), lambda h: (first + h, 0, 0)),
        whole,
        whole,
    ]
    operands = [queries, key, ds0, ds1, cosines, sines]
    if given is not None:
        specs.append(pl.BlockSpec(memory_space=pl.ANY))
        operands.append(given)
    return pl.pallas_call(
        grad_query_kernel,
        grid=(heads // 2,),
        in_specs=specs,
        out_specs=column,
        out_shape=jax.ShapeDtypeStruct(queries.shape, BF),
        input_output_aliases={} if given is None else {6: 0},
        compiler_params=params(16),
        name="grad_query",
    )(*operands)


def cotan_kernel(order_ref, b0_ref, b1_ref, b2_ref, b3_ref, plain_ref, cos_ref, sin_ref, out_ref):
    tokens = cos_ref.shape[0]
    for k, back_ref in enumerate((b0_ref, b1_ref, b2_ref, b3_ref)):
        rows = pl.ds(pl.multiple_of(order_ref[k] * tokens, tokens), tokens)
        u = plain_ref[rows, :HEAD_SIZE]
        back = turn(back_ref[0].astype(F32), cos_ref[...], -sin_ref[...])
        out_ref[rows, :HEAD_SIZE] = norm_back(u, norm_scale(u), back).astype(BF)
        out_ref[rows, HEAD_SIZE:] = back_ref[1]


def key_value_cotan(order, back, plain, cosines, sines):
    vmem = pl.BlockSpec(memory_space=pltpu.VMEM)
    return pl.pallas_call(
        cotan_kernel,
        in_specs=[pl.BlockSpec(memory_space=pltpu.SMEM)] + [vmem] * 7,
        out_specs=vmem,
        out_shape=jax.ShapeDtypeStruct(plain.shape, BF),
        compiler_params=params(),
        name="key_value_cotan",
    )(order, *back, plain, cosines, sines)


def grad_token_kernel(x_ref, mine_ref, layer_ref, *refs):
    out_ref = refs[-1]

    def body(rows):
        cotan = mine_ref[rows, :].astype(F32) + layer_ref[rows, :].astype(F32)
        field = x_ref[rows, :].astype(F32)
        out_ref[rows, :] = norm_back(field, norm_scale(field), cotan).astype(BF)

    row_loop(x_ref.shape[0], 16, body)


def grad_tokens(tokens, mine, from_layer, start, given=None):
    step, width = from_layer.shape[0], tokens.shape[1]
    first = start // step
    here = pl.BlockSpec((step, width), lambda i: (first + i, 0))
    specs = [here, here, pl.BlockSpec((step, width), lambda i: (i, 0))]
    operands = [tokens, mine, from_layer]
    if given is not None:
        specs.append(pl.BlockSpec(memory_space=pl.ANY))
        operands.append(given)
    return pl.pallas_call(
        grad_token_kernel,
        grid=(from_layer.shape[0] // step,),
        in_specs=specs,
        out_specs=here,
        out_shape=jax.ShapeDtypeStruct(tokens.shape, BF),
        input_output_aliases={} if given is None else {3: 0},
        compiler_params=params(60),
        name="grad_tokens",
    )(*operands)


def plane_pairs(first, step):
    pairs = []
    for x in range(4):
        for y in range(4):
            for c in range(2):
                along_x = (c == 0) == first
                to_x = (x + step) % 4 if along_x else x
                to_y = y if along_x else (y + step) % 4
                pairs.append(((x * 4 + y) * 2 + c, (to_x * 4 + to_y) * 2 + c))
    return pairs


def far(block, step):
    return lax.ppermute(block, ("x", "y", "c"), plane_pairs(True, step))


def near(block, step):
    return lax.ppermute(block, ("x", "y", "c"), plane_pairs(False, step))


def swap_cores(block):
    return lax.ppermute(block, "c", [(0, 1), (1, 0)])


def group_pairs(target):
    pairs = []
    for g in range(4):
        for t in range(4):
            to_g, to_t = target(g, t)
            pairs.append((g * 4 + t, (to_g % 4) * 4 + to_t % 4))
    return pairs


def to_heads(block, k):
    return lax.ppermute(block, ("zl", "c", "t"), group_pairs(lambda g, t: (t, g + k)))


def from_heads(block, k):
    return lax.ppermute(block, ("zl", "c", "t"), group_pairs(lambda g, t: (t + k, g)))


def swap_layers(block):
    return lax.ppermute(block, "zl", [(0, 1), (1, 0)])


def after(first, *later):
    return lax.optimization_barrier((first,) + later)[1:]


def per_device(
    tokens,
    queries,
    grad_out,
    key_value_master_weight,
    key_value_first_moment,
    key_value_second_moment,
    writer,
):
    own_tokens, model_width = tokens.shape
    unit_scale = 1.0 / math.sqrt(model_width)
    length = queries.shape[0]
    rows = key_value_master_weight.shape[1]
    core = lax.axis_index("c")
    x_index, y_index = lax.axis_index("x"), lax.axis_index("y")
    t_index = lax.axis_index("t")
    g_index = 2 * lax.axis_index("zl") + core

    own_weight = key_value_master_weight.astype(BF)
    own_weight = jnp.concatenate([own_weight[0], own_weight[1]], axis=1)
    stage_parts = [to_heads(own_weight, k) for k in range(4)]
    stage = jnp.concatenate(stage_parts, axis=0)
    own_block = normed(tokens)
    from_z = swap_layers(after(stage_parts[0], own_block)[0])
    from_core = swap_cores(own_block)
    shard = jnp.concatenate([stage, near(stage, 1), near(stage, -1), near(stage, 2)], axis=0)
    pieces = [shard, far(shard, 1), far(shard, -1), far(shard, 2)]

    place = jnp.array(PLACES, jnp.int32)
    count = jnp.arange(4, dtype=jnp.int32)
    far_place = (jnp.where(core == 0, x_index, y_index) + place) % 4
    near_place = (jnp.where(core == 0, y_index, x_index) + place) % 4
    far_step = jnp.where(core == 0, 8 * rows, 2 * rows)
    near_step = jnp.where(core == 0, 2 * rows, 8 * rows)
    source = (t_index - count) % 4
    offsets = (
        far_place[:, None, None] * far_step
        + near_place[None, :, None] * near_step
        + ((source // 2) * (32 * rows) + (source % 2) * rows)[None, None, :]
    )
    offsets = offsets.reshape(64).astype(jnp.int32)
    sequence_order = ((t_index + count) % 4) ^ g_index
    block_order = (g_index - count) % 4

    cosines, sines = rope_tables(length, HEAD_SIZE)
    cosines = jnp.concatenate([cosines, cosines], axis=1)
    sines = jnp.concatenate([-sines, sines], axis=1)
    own_cos = lax.dynamic_slice_in_dim(cosines, t_index * own_tokens, own_tokens, 0)
    own_sin = lax.dynamic_slice_in_dim(sines, t_index * own_tokens, own_tokens, 0)
    rotated = rotated_queries(queries, cosines, sines)

    early = turned(offsets, own_block, from_core)
    from_core, from_z, own_cos, own_sin, sequence_order, block_order, offsets = after(
        (pieces, rotated, early), from_core, from_z, own_cos, own_sin, sequence_order, block_order, offsets
    )
    blocks = [own_block, from_core, from_z, swap_cores(from_z)]
    weights, plain_early = project_early(offsets, blocks[0], blocks[1], pieces, unit_scale)
    plain, projected = project(
        sequence_order, blocks[2], blocks[3], weights, plain_early, own_cos, own_sin, unit_scale
    )
    arrived = [from_heads(block, k) for k, block in enumerate(projected)]
    late = turned(offsets, *after(plain, blocks[2], blocks[3]))
    (arrived,) = after(late, arrived)

    returning, key, ds0, ds1 = attention(block_order, rotated, grad_out, arrived)
    back = [to_heads(block, -k) for k, block in enumerate(returning)]
    grad_q = grad_queries(queries, key, ds0, ds1, cosines, sines, 0)
    (back,) = after(grad_q, back)
    cotan = key_value_cotan(sequence_order, back, plain, own_cos, own_sin)

    part = [None] + list(weight_grads(early, late, cotan, (1, 2, 3)))
    arriving = [far(part[1], -1), far(part[2], 1), far(part[3], 2)]

    (cotan,) = after(part[1], cotan)
    rows_of = cotan.reshape(4, own_tokens, -1)
    sent = dot(jnp.concatenate([rows_of[1], rows_of[3]], axis=0), weights, NT) * unit_scale
    sent = sent.astype(BF)
    swapped = swap_cores(sent)
    (kept_from,) = after(sent, jnp.concatenate([rows_of[0], rows_of[2]], axis=0))
    kept = dot(kept_from, weights, NT) * unit_scale
    to_z = (kept[own_tokens:] + swapped[own_tokens:].astype(F32)).astype(BF)
    starts, cut = (96, 0, 48), (96, 48)
    to_z = [to_z[cut[0] :], to_z[: cut[1]], to_z[cut[1] : cut[0]]]
    z_first = swap_layers(to_z[0])

    kept, swapped, cotan = after(to_z, kept, swapped, cotan)
    part[0] = weight_grads(early, late, cotan, (0,))[0]
    mine = (kept[:own_tokens] + swapped[:own_tokens].astype(F32)).astype(BF)
    grad_x = grad_tokens(tokens, mine, z_first, starts[0])
    own_part, to_z[1], mine = after(grad_x, part[0], to_z[1], mine)
    own = sum_of(own_part, arriving, F32)
    z_second = swap_layers(to_z[1])
    summed = sum_of(own[0], [near(own[1], -1), near(own[2], 1), near(own[3], 2)], BF)
    grad_q = grad_queries(
        queries, key, after(own, ds0)[0], ds1, cosines, sines, queries.shape[1] // HEAD_SIZE // 2, grad_q
    )
    (summed,) = after((z_second, grad_q), summed)
    final = [from_heads(summed[k], -k) for k in range(4)]
    grad_x = grad_tokens(tokens, mine, after(summed, z_second)[0], starts[1], grad_x)
    (final,) = after(grad_x, final)
    final = sum(block.astype(F32) for block in final) * unit_scale
    weight_grad = jnp.stack([final[:, :HEAD_SIZE], final[:, HEAD_SIZE:]], axis=0)

    (to_z[2],) = after(final, to_z[2])
    grad_x = grad_tokens(tokens, mine, swap_layers(to_z[2]), starts[2], grad_x)

    new_first = beta_one * key_value_first_moment + (1.0 - beta_one) * weight_grad
    new_second = beta_two * key_value_second_moment + (1.0 - beta_two) * weight_grad * weight_grad
    first_hat = new_first / (1.0 - beta_one**step_count)
    second_hat = new_second / (1.0 - beta_two**step_count)
    new_master = key_value_master_weight - learn_rate * (
        first_hat / (jnp.sqrt(second_hat) + adam_eps) + weight_decay * key_value_master_weight
    )
    replicas = writer.shape[0]
    pieces = new_master.astype(BF).reshape(replicas, 2, -1)
    rank_ids = jnp.arange(replicas, dtype=jnp.int32)
    inverse = jnp.sum(jnp.where(writer[None, :] == rank_ids[:, None], rank_ids[None, :], 0), axis=1)
    outgoing = pieces.at[inverse].get(mode="promise_in_bounds")
    saved = lax.all_to_all(outgoing, ("zl", "x", "y", "c"), 0, 0, tiled=True)
    saved = after(grad_x, saved)[0].reshape(replicas, -1)
    return (grad_x, grad_q, new_master, new_first, new_second, saved)


def solution(mesh):
    fine = Mesh(mesh.devices.reshape(2, 4, 4, 2, 4), ("zl", "x", "y", "c", "t"))
    dp = ("zl", "x", "y", "c")
    every = dp + ("t",)
    weight = P(None, dp, "t")
    return jax.shard_map(
        per_device,
        mesh=fine,
        in_specs=(P(every, None), P(dp, "t"), P(dp, "t"), weight, weight, weight, P()),
        out_specs=(P(every, None), P(dp, "t"), weight, weight, weight, P(dp, "t")),
        check_vma=False,
    )
```

```python
import functools
import math

import jax
import jax.numpy as jnp
from jax import lax
from jax.experimental import pallas as pl
from jax.experimental.pallas import tpu as pltpu
from jax.sharding import Mesh, PartitionSpec as P

HEAD_SIZE = 128


norm_eps = 1e-06
rope_base = 1000000.0
beta_one = 0.9
beta_two = 0.95
adam_eps = 1e-08
learn_rate = 0.02
weight_decay = 0.1
step_count = 10.0


def rope_tables(length, head_width):
    half_width = head_width // 2
    index_float = jnp.arange(half_width, dtype=jnp.float32)
    inverse_freq = rope_base ** (-2.0 * index_float / head_width)
    positions = jnp.arange(length, dtype=jnp.float32)
    angles = positions[:, None] * inverse_freq[None, :]
    return (jnp.cos(angles), jnp.sin(angles))


BF = jnp.bfloat16
F32 = jnp.float32
HALF = HEAD_SIZE // 2
PLACES = (0, -1, 1, 2)
NT = (((1,), (1,)), ((), ()))
TT = (((0,), (0,)), ((), ()))


def dot(left, right, dims=None):
    if dims is None:
        dims = (((1,), (0,)), ((), ()))
    return lax.dot_general(left, right, dims, preferred_element_type=F32)


def params(mebibytes=20):
    return pltpu.CompilerParams(vmem_limit_bytes=mebibytes * 1024 * 1024)


def norm_scale(field):
    return lax.rsqrt(jnp.mean(field * field, axis=-1, keepdims=True) + norm_eps)


def norm_back(field, factor, cotan):
    return factor * cotan - field * (factor * factor * factor) * jnp.mean(
        cotan * field, axis=-1, keepdims=True
    )


def turn(field, cosines, sines):
    return field * cosines + pltpu.roll(field, HALF, 1) * sines


def query_kernel(q_ref, cos_ref, sin_ref, out_ref):
    field = q_ref[...].astype(F32)
    out_ref[...] = turn(field * norm_scale(field), cos_ref[...], sin_ref[...]).astype(BF)


def rotated_queries(queries, cosines, sines):
    length, width = queries.shape
    column = pl.BlockSpec((length, HEAD_SIZE), lambda h: (0, h))
    table = pl.BlockSpec((length, HEAD_SIZE), lambda h: (0, 0))
    return pl.pallas_call(
        query_kernel,
        grid=(width // HEAD_SIZE,),
        in_specs=[column, table, table],
        out_specs=column,
        out_shape=jax.ShapeDtypeStruct(queries.shape, BF),
        compiler_params=params(),
        name="query_rope",
    )(queries, cosines, sines)


def row_loop(rows, step, body):
    def run(i, carry):
        body(pl.ds(pl.multiple_of(i * step, step), step))
        return carry

    lax.fori_loop(0, rows // step, run, 0)


def norm_kernel(in_ref, out_ref):
    def body(rows):
        field = in_ref[rows, :].astype(F32)
        out_ref[rows, :] = (field * norm_scale(field)).astype(BF)

    row_loop(in_ref.shape[0], 16, body)


def normed(tokens):
    block = pl.BlockSpec((tokens.shape[0] // 4, tokens.shape[1]), lambda i: (i, 0))
    return pl.pallas_call(
        norm_kernel,
        grid=(4,),
        in_specs=[block],
        out_specs=block,
        out_shape=jax.ShapeDtypeStruct(tokens.shape, BF),
        compiler_params=params(),
        name="norm",
    )(tokens)


def project_early_kernel(scale, offset_ref, first_ref, second_ref, *refs):
    w_refs, whole_ref, plain_ref = refs[:-2], refs[-2], refs[-1]
    block = whole_ref.shape[0] // offset_ref.shape[0]
    at = 0
    for w_ref in w_refs:
        count = w_ref.shape[0] // block

        def body(k, carry, at=at, w_ref=w_ref):
            row = pl.ds(pl.multiple_of(offset_ref[at + k], 16), block)
            whole_ref[row, :] = w_ref[pl.ds(pl.multiple_of(k * block, 16), block), :]
            return carry

        lax.fori_loop(0, count, body, 0)
        at += count
    plain_ref[...] = rows_times(first_ref, second_ref, whole_ref) * scale


def rows_times(first_ref, second_ref, whole_ref):
    chunk = whole_ref.shape[0] // 4
    total = 0.0
    for j in range(4):
        columns = slice(j * chunk, (j + 1) * chunk)
        field = jnp.concatenate([first_ref[:, columns], second_ref[:, columns]], axis=0)
        total = total + dot(field, whole_ref[columns])
    return total


def project_early(offsets, first, second, pieces, scale):
    vmem = pl.BlockSpec(memory_space=pltpu.VMEM)
    shape = (first.shape[1], pieces[0].shape[1])
    return pl.pallas_call(
        functools.partial(project_early_kernel, scale),
        in_specs=[pl.BlockSpec(memory_space=pltpu.SMEM)] + [vmem] * (2 + len(pieces)),
        out_specs=[vmem, vmem],
        out_shape=[
            jax.ShapeDtypeStruct(shape, BF),
            jax.ShapeDtypeStruct((2 * first.shape[0], shape[1]), F32),
        ],
        compiler_params=params(),
        name="project_early",
    )(offsets, first, second, *pieces)


def project_kernel(scale, order_ref, first_ref, second_ref, whole_ref, early_ref, cos_ref, sin_ref, plain_ref, *out_refs):
    tokens = cos_ref.shape[0]
    plain_ref[: 2 * tokens] = early_ref[...]
    plain_ref[2 * tokens :] = rows_times(first_ref, second_ref, whole_ref) * scale
    for k in range(4):
        rows = pl.ds(pl.multiple_of(order_ref[k] * tokens, tokens), tokens)
        u = plain_ref[rows, :HEAD_SIZE]
        out_refs[k][0] = turn(u * norm_scale(u), cos_ref[...], sin_ref[...]).astype(BF)
        out_refs[k][1] = plain_ref[rows, HEAD_SIZE:].astype(BF)


def project(order, first, second, weights, early, cosines, sines, scale):
    tokens = cosines.shape[0]
    vmem = pl.BlockSpec(memory_space=pltpu.VMEM)
    result = pl.pallas_call(
        functools.partial(project_kernel, scale),
        in_specs=[pl.BlockSpec(memory_space=pltpu.SMEM)] + [vmem] * 6,
        out_specs=[vmem] * 5,
        out_shape=[jax.ShapeDtypeStruct((4 * tokens, weights.shape[1]), F32)]
        + [jax.ShapeDtypeStruct((2, tokens, HEAD_SIZE), BF)] * 4,
        compiler_params=params(),
        name="project",
    )(order, first, second, weights, early, cosines, sines)
    return result[0], result[1:]


def sum_kernel(*refs):
    in_refs, out_refs = refs[:4], refs[4:]
    rows = out_refs[0].shape[0]
    for index, out_ref in enumerate(out_refs):
        part = slice(index * rows, (index + 1) * rows)
        total = sum(ref[part].astype(F32) for ref in in_refs[-3:]) + in_refs[0][part].astype(F32)
        out_ref[...] = total.astype(out_ref.dtype)


def sum_of(own, arrived, first_type):
    shape = (own.shape[0] // 4, own.shape[1])
    vmem = pl.BlockSpec(memory_space=pltpu.VMEM)
    return pl.pallas_call(
        sum_kernel,
        in_specs=[vmem] * 4,
        out_specs=[vmem] * 4,
        out_shape=[jax.ShapeDtypeStruct(shape, first_type)] + [jax.ShapeDtypeStruct(shape, BF)] * 3,
        compiler_params=params(),
        name="sum",
    )(own, *arrived)


def turn_kernel(offset_ref, first_ref, second_ref, out_ref, scratch):
    rows = first_ref.shape[0]
    block = scratch.shape[0] // offset_ref.shape[0]

    def turn_some(columns):
        scratch[columns, :rows] = first_ref[:, columns].T
        scratch[columns, rows:] = second_ref[:, columns].T

    row_loop(scratch.shape[0], 512, turn_some)

    def body(k, carry):
        row = pl.ds(pl.multiple_of(offset_ref[k], 16), block)
        out_ref[pl.ds(pl.multiple_of(k * block, 16), block), :] = scratch[row, :]
        return carry

    lax.fori_loop(0, offset_ref.shape[0], body, 0)


def turned(offsets, first, second):
    shape = (first.shape[1], 2 * first.shape[0])
    vmem = pl.BlockSpec(memory_space=pltpu.VMEM)
    return pl.pallas_call(
        turn_kernel,
        in_specs=[pl.BlockSpec(memory_space=pltpu.SMEM), vmem, vmem],
        out_specs=vmem,
        out_shape=jax.ShapeDtypeStruct(shape, BF),
        scratch_shapes=[pltpu.VMEM(shape, BF)],
        compiler_params=params(),
        name="turn",
    )(offsets, first, second)


def weight_grad_kernel(quarters, early_ref, late_ref, cotan_ref, *out_refs):
    rows = out_refs[0].shape[0]
    for index, out_ref in zip(quarters, out_refs):
        part = slice(index * rows, (index + 1) * rows)
        field = jnp.concatenate([early_ref[part], late_ref[part]], axis=1)
        out_ref[...] = dot(field, cotan_ref[...]).astype(BF)


def weight_grads(early, late, cotan, quarters):
    vmem = pl.BlockSpec(memory_space=pltpu.VMEM)
    shape = (early.shape[0] // 4, cotan.shape[1])
    return pl.pallas_call(
        functools.partial(weight_grad_kernel, quarters),
        in_specs=[vmem] * 3,
        out_specs=[vmem] * len(quarters),
        out_shape=[jax.ShapeDtypeStruct(shape, BF)] * len(quarters),
        compiler_params=params(),
        name="weight_grads",
    )(early, late, cotan)


def attention_kernel(order_ref, q_ref, g_ref, *refs):
    kv_refs, dkv_refs = refs[:4], refs[4:8]
    k_ref, ds0_ref, ds1_ref, v_ref, dk_acc, dv_acc = refs[8:]
    step = pl.program_id(0)
    length, width = q_ref.shape
    tokens, mid, heads = length // 4, length // 2, width // HEAD_SIZE
    scale = 1.0 / math.sqrt(HEAD_SIZE)

    @pl.when(step == 0)
    def _():
        dk_acc[...] = jnp.zeros_like(dk_acc)
        dv_acc[...] = jnp.zeros_like(dv_acc)
        for k in range(4):
            rows = pl.ds(pl.multiple_of(order_ref[k] * tokens, tokens), tokens)
            k_ref[rows, :] = kv_refs[k][0]
            v_ref[rows, :] = kv_refs[k][1]

    early, late = slice(0, mid), slice(mid, length)
    row = lax.broadcasted_iota(jnp.int32, (mid, mid), 0)
    column = lax.broadcasted_iota(jnp.int32, (mid, mid), 1)
    allowed = row <= column
    factor = scale * math.log2(math.e)
    each = range(heads)

    def at(ref, rows, h):
        return ref[rows, h * HEAD_SIZE : (h + 1) * HEAD_SIZE]

    def products(left_ref, right_ref):
        return [
            [
                dot(left_ref[early], at(right_ref, early, h), NT),
                dot(left_ref[early], at(right_ref, late, h), NT),
                dot(left_ref[late], at(right_ref, late, h), NT),
            ]
            for h in each
        ]

    def add(acc, terms, right_ref):
        acc[early] += sum(
            dot(terms[h][0], at(right_ref, early, h)) + dot(terms[h][1], at(right_ref, late, h))
            for h in each
        )
        acc[late] += sum(dot(terms[h][2], at(right_ref, late, h)) for h in each)

    def column_sums(terms):
        first, second, third = (jnp.sum(term, axis=0, keepdims=True) for term in terms)
        return first, second + third

    scores = products(k_ref, q_ref)
    d_probs = products(v_ref, g_ref)
    probs = []
    for h in each:
        a, b, c = scores[h]
        a = jnp.where(allowed, jnp.exp2(a * factor), 0.0)
        b = jnp.exp2(b * factor)
        c = jnp.where(allowed, jnp.exp2(c * factor), 0.0)
        sum_a, sum_b = column_sums((a, b, c))
        inv_a, inv_b = 1.0 / sum_a, 1.0 / sum_b
        probs.append((a * inv_a, b * inv_b, c * inv_b))
    add(dv_acc, [[term.astype(BF) for term in probs[h]] for h in each], g_ref)
    d_scores = []
    for h in each:
        sum_a, sum_b = column_sums([p * d for p, d in zip(probs[h], d_probs[h])])
        d_scores.append(
            [
                (p * (d - total)).astype(BF)
                for p, d, total in zip(probs[h], d_probs[h], (sum_a, sum_b, sum_b))
            ]
        )
        ds0_ref[h, :, :mid] = d_scores[h][0]
        ds0_ref[h, :, mid:] = d_scores[h][1]
        ds1_ref[h] = d_scores[h][2]
    add(dk_acc, d_scores, q_ref)

    @pl.when(step == pl.num_programs(0) - 1)
    def _():
        for k in range(4):
            rows = pl.ds(pl.multiple_of(order_ref[k] * tokens, tokens), tokens)
            dkv_refs[k][0] = (dk_acc[rows, :] * scale).astype(BF)
            dkv_refs[k][1] = dv_acc[rows, :].astype(BF)


def attention(order, rotated, incoming, pieces):
    length, width = rotated.shape
    heads, mid, pair = width // HEAD_SIZE, length // 2, 2
    columns = pl.BlockSpec((length, pair * HEAD_SIZE), lambda h: (0, h))
    whole = pl.BlockSpec((length, HEAD_SIZE), lambda h: (0, 0))
    piece = pl.BlockSpec(pieces[0].shape, lambda h: (0, 0, 0))
    result = pl.pallas_call(
        attention_kernel,
        grid=(heads // pair,),
        in_specs=[pl.BlockSpec(memory_space=pltpu.SMEM), columns, columns] + [piece] * 4,
        out_specs=[piece] * 4
        + [
            whole,
            pl.BlockSpec((pair, mid, length), lambda h: (h, 0, 0)),
            pl.BlockSpec((pair, mid, mid), lambda h: (h, 0, 0)),
        ],
        out_shape=[jax.ShapeDtypeStruct(pieces[0].shape, BF)] * 4
        + [
            jax.ShapeDtypeStruct((length, HEAD_SIZE), BF),
            jax.ShapeDtypeStruct((heads, mid, length), BF),
            jax.ShapeDtypeStruct((heads, mid, mid), BF),
        ],
        scratch_shapes=[pltpu.VMEM((length, HEAD_SIZE), BF)]
        + [pltpu.VMEM((length, HEAD_SIZE), F32)] * 2,
        compiler_params=params(32),
        name="attention",
    )(order, rotated, incoming, *pieces)
    return result[:4], result[4], result[5], result[6]


def grad_query_kernel(q_ref, k_ref, ds0_ref, ds1_ref, cos_ref, sin_ref, *refs):
    out_ref = refs[-1]
    mid = ds0_ref.shape[1]
    scale = 1.0 / math.sqrt(HEAD_SIZE)
    k0, k1 = k_ref[:mid], k_ref[mid:]
    both = dot(k0, ds0_ref[0], TT)
    early = both[:, :mid]
    late = both[:, mid:] + dot(k1, ds1_ref[0], TT)
    cotan = jnp.concatenate([early.T, late.T], axis=0) * scale
    field = q_ref[...].astype(F32)
    cotan = turn(cotan, cos_ref[...], -sin_ref[...])
    out_ref[...] = norm_back(field, norm_scale(field), cotan).astype(BF)


def grad_queries(queries, key, ds0, ds1, cosines, sines, first, given=None):
    length, width = queries.shape
    heads, mid = width // HEAD_SIZE, length // 2
    column = pl.BlockSpec((length, HEAD_SIZE), lambda h: (0, first + h))
    whole = pl.BlockSpec((length, HEAD_SIZE), lambda h: (0, 0))
    specs = [
        column,
        whole,
        pl.BlockSpec((1, mid, length), lambda h: (first + h, 0, 0)),
        pl.BlockSpec((1, mid, mid), lambda h: (first + h, 0, 0)),
        whole,
        whole,
    ]
    operands = [queries, key, ds0, ds1, cosines, sines]
    if given is not None:
        specs.append(pl.BlockSpec(memory_space=pl.ANY))
        operands.append(given)
    return pl.pallas_call(
        grad_query_kernel,
        grid=(heads // 2,),
        in_specs=specs,
        out_specs=column,
        out_shape=jax.ShapeDtypeStruct(queries.shape, BF),
        input_output_aliases={} if given is None else {6: 0},
        compiler_params=params(16),
        name="grad_query",
    )(*operands)


def cotan_kernel(quarters, order_ref, b0_ref, b1_ref, b2_ref, b3_ref, plain_ref, cos_ref, sin_ref, *refs):
    early_ref, late_ref, out_ref, part_refs = refs[0], refs[1], refs[2], refs[3:]
    tokens = cos_ref.shape[0]
    for k, back_ref in enumerate((b0_ref, b1_ref, b2_ref, b3_ref)):
        rows = pl.ds(pl.multiple_of(order_ref[k] * tokens, tokens), tokens)
        u = plain_ref[rows, :HEAD_SIZE]
        back = turn(back_ref[0].astype(F32), cos_ref[...], -sin_ref[...])
        out_ref[rows, :HEAD_SIZE] = norm_back(u, norm_scale(u), back).astype(BF)
        out_ref[rows, HEAD_SIZE:] = back_ref[1]
    weight_grad_kernel(quarters, early_ref, late_ref, out_ref, *part_refs)


def key_value_cotan(order, back, plain, cosines, sines, early, late, quarters):
    vmem = pl.BlockSpec(memory_space=pltpu.VMEM)
    part = jax.ShapeDtypeStruct((early.shape[0] // 4, plain.shape[1]), BF)
    result = pl.pallas_call(
        functools.partial(cotan_kernel, quarters),
        in_specs=[pl.BlockSpec(memory_space=pltpu.SMEM)] + [vmem] * 9,
        out_specs=[vmem] * (1 + len(quarters)),
        out_shape=[jax.ShapeDtypeStruct(plain.shape, BF)] + [part] * len(quarters),
        compiler_params=params(),
        name="key_value_cotan",
    )(order, *back, plain, cosines, sines, early, late)
    return result[0], result[1:]


def grad_token_kernel(x_ref, mine_ref, layer_ref, *refs):
    out_ref = refs[-1]

    def body(rows):
        cotan = mine_ref[rows, :].astype(F32) + layer_ref[rows, :].astype(F32)
        field = x_ref[rows, :].astype(F32)
        out_ref[rows, :] = norm_back(field, norm_scale(field), cotan).astype(BF)

    row_loop(x_ref.shape[0], 16, body)


def grad_tokens(tokens, mine, from_layer, start, given=None):
    step, width = from_layer.shape[0], tokens.shape[1]
    first = start // step
    here = pl.BlockSpec((step, width), lambda i: (first + i, 0))
    specs = [here, here, pl.BlockSpec((step, width), lambda i: (i, 0))]
    operands = [tokens, mine, from_layer]
    if given is not None:
        specs.append(pl.BlockSpec(memory_space=pl.ANY))
        operands.append(given)
    return pl.pallas_call(
        grad_token_kernel,
        grid=(from_layer.shape[0] // step,),
        in_specs=specs,
        out_specs=here,
        out_shape=jax.ShapeDtypeStruct(tokens.shape, BF),
        input_output_aliases={} if given is None else {3: 0},
        compiler_params=params(60),
        name="grad_tokens",
    )(*operands)


def plane_pairs(first, step):
    pairs = []
    for x in range(4):
        for y in range(4):
            for c in range(2):
                along_x = (c == 0) == first
                to_x = (x + step) % 4 if along_x else x
                to_y = y if along_x else (y + step) % 4
                pairs.append(((x * 4 + y) * 2 + c, (to_x * 4 + to_y) * 2 + c))
    return pairs


def far(block, step):
    return lax.ppermute(block, ("x", "y", "c"), plane_pairs(True, step))


def near(block, step):
    return lax.ppermute(block, ("x", "y", "c"), plane_pairs(False, step))


def swap_cores(block):
    return lax.ppermute(block, "c", [(0, 1), (1, 0)])


def group_pairs(target):
    pairs = []
    for g in range(4):
        for t in range(4):
            to_g, to_t = target(g, t)
            pairs.append((g * 4 + t, (to_g % 4) * 4 + to_t % 4))
    return pairs


def to_heads(block, k):
    return lax.ppermute(block, ("zl", "c", "t"), group_pairs(lambda g, t: (t, g + k)))


def from_heads(block, k):
    return lax.ppermute(block, ("zl", "c", "t"), group_pairs(lambda g, t: (t + k, g)))


def swap_layers(block):
    return lax.ppermute(block, "zl", [(0, 1), (1, 0)])


def after(first, *later):
    return lax.optimization_barrier((first,) + later)[1:]


def per_device(
    tokens,
    queries,
    grad_out,
    key_value_master_weight,
    key_value_first_moment,
    key_value_second_moment,
    writer,
):
    own_tokens, model_width = tokens.shape
    unit_scale = 1.0 / math.sqrt(model_width)
    length = queries.shape[0]
    rows = key_value_master_weight.shape[1]
    core = lax.axis_index("c")
    x_index, y_index = lax.axis_index("x"), lax.axis_index("y")
    t_index = lax.axis_index("t")
    g_index = 2 * lax.axis_index("zl") + core

    own_weight = key_value_master_weight.astype(BF)
    own_weight = jnp.concatenate([own_weight[0], own_weight[1]], axis=1)
    stage_parts = [to_heads(own_weight, k) for k in range(4)]
    stage = jnp.concatenate(stage_parts, axis=0)
    own_block = normed(tokens)
    from_z = swap_layers(after(stage_parts[0], own_block)[0])
    from_core = swap_cores(own_block)
    shard = jnp.concatenate([stage, near(stage, 1), near(stage, -1), near(stage, 2)], axis=0)
    pieces = [shard, far(shard, 1), far(shard, -1), far(shard, 2)]

    place = jnp.array(PLACES, jnp.int32)
    count = jnp.arange(4, dtype=jnp.int32)
    far_place = (jnp.where(core == 0, x_index, y_index) + place) % 4
    near_place = (jnp.where(core == 0, y_index, x_index) + place) % 4
    far_step = jnp.where(core == 0, 8 * rows, 2 * rows)
    near_step = jnp.where(core == 0, 2 * rows, 8 * rows)
    source = (t_index - count) % 4
    offsets = (
        far_place[:, None, None] * far_step
        + near_place[None, :, None] * near_step
        + ((source // 2) * (32 * rows) + (source % 2) * rows)[None, None, :]
    )
    offsets = offsets.reshape(64).astype(jnp.int32)
    sequence_order = ((t_index + count) % 4) ^ g_index
    block_order = (g_index - count) % 4

    cosines, sines = rope_tables(length, HEAD_SIZE)
    cosines = jnp.concatenate([cosines, cosines], axis=1)
    sines = jnp.concatenate([-sines, sines], axis=1)
    own_cos = lax.dynamic_slice_in_dim(cosines, t_index * own_tokens, own_tokens, 0)
    own_sin = lax.dynamic_slice_in_dim(sines, t_index * own_tokens, own_tokens, 0)
    rotated = rotated_queries(queries, cosines, sines)

    early = turned(offsets, own_block, from_core)
    from_core, from_z, own_cos, own_sin, sequence_order, block_order, offsets = after(
        (pieces, rotated, early), from_core, from_z, own_cos, own_sin, sequence_order, block_order, offsets
    )
    blocks = [own_block, from_core, from_z, swap_cores(from_z)]
    weights, plain_early = project_early(offsets, blocks[0], blocks[1], pieces, unit_scale)
    plain, projected = project(
        sequence_order, blocks[2], blocks[3], weights, plain_early, own_cos, own_sin, unit_scale
    )
    arrived = [from_heads(block, k) for k, block in enumerate(projected)]
    late = turned(offsets, *after(plain, blocks[2], blocks[3]))
    (arrived,) = after(late, arrived)

    returning, key, ds0, ds1 = attention(block_order, rotated, grad_out, arrived)
    back = [to_heads(block, -k) for k, block in enumerate(returning)]
    grad_q = grad_queries(queries, key, ds0, ds1, cosines, sines, 0)
    (back,) = after(grad_q, back)
    cotan, sent_parts = key_value_cotan(
        sequence_order, back, plain, own_cos, own_sin, early, late, (1, 2, 3)
    )

    part = [None] + list(sent_parts)
    arriving = [far(part[1], -1), far(part[2], 1), far(part[3], 2)]

    (cotan,) = after(part[1], cotan)
    rows_of = cotan.reshape(4, own_tokens, -1)
    sent = dot(jnp.concatenate([rows_of[1], rows_of[3]], axis=0), weights, NT) * unit_scale
    sent = sent.astype(BF)
    swapped = swap_cores(sent)
    (kept_from,) = after(sent, jnp.concatenate([rows_of[0], rows_of[2]], axis=0))
    kept = dot(kept_from, weights, NT) * unit_scale
    to_z = (kept[own_tokens:] + swapped[own_tokens:].astype(F32)).astype(BF)
    starts = (0, 48, 96)
    to_z = [to_z[starts[0] : starts[1]], to_z[starts[1] : starts[2]], to_z[starts[2] :]]
    z_first = swap_layers(to_z[0])

    kept, swapped, cotan = after(to_z, kept, swapped, cotan)
    part[0] = weight_grads(early, late, cotan, (0,))[0]
    mine = (kept[:own_tokens] + swapped[:own_tokens].astype(F32)).astype(BF)
    own_part, to_z[1] = after((z_first, mine), part[0], to_z[1])
    own = sum_of(own_part, arriving, F32)
    z_second = swap_layers(to_z[1])
    summed = sum_of(own[0], [near(own[1], -1), near(own[2], 1), near(own[3], 2)], BF)
    grad_q = grad_queries(
        queries, key, after(own, ds0)[0], ds1, cosines, sines, queries.shape[1] // HEAD_SIZE // 2, grad_q
    )
    (summed,) = after((z_second, grad_q), summed)
    final = [from_heads(summed[k], -k) for k in range(4)]
    grad_x = grad_tokens(tokens, mine, after(summed, z_second)[0], starts[1])
    (final,) = after(grad_x, final)
    final = sum(block.astype(F32) for block in final) * unit_scale
    weight_grad = jnp.stack([final[:, :HEAD_SIZE], final[:, HEAD_SIZE:]], axis=0)

    to_z[2], z_first = after(final, to_z[2], z_first)
    grad_x = grad_tokens(tokens, mine, z_first, starts[0], grad_x)
    grad_x = grad_tokens(tokens, mine, swap_layers(to_z[2]), starts[2], grad_x)

    new_first = beta_one * key_value_first_moment + (1.0 - beta_one) * weight_grad
    new_second = beta_two * key_value_second_moment + (1.0 - beta_two) * weight_grad * weight_grad
    first_hat = new_first / (1.0 - beta_one**step_count)
    second_hat = new_second / (1.0 - beta_two**step_count)
    new_master = key_value_master_weight - learn_rate * (
        first_hat / (jnp.sqrt(second_hat) + adam_eps) + weight_decay * key_value_master_weight
    )
    replicas = writer.shape[0]
    pieces = new_master.astype(BF).reshape(replicas, 2, -1)
    rank_ids = jnp.arange(replicas, dtype=jnp.int32)
    inverse = jnp.sum(jnp.where(writer[None, :] == rank_ids[:, None], rank_ids[None, :], 0), axis=1)
    outgoing = pieces.at[inverse].get(mode="promise_in_bounds")
    saved = lax.all_to_all(outgoing, ("zl", "x", "y", "c"), 0, 0, tiled=True)
    saved = after(grad_x, saved)[0].reshape(replicas, -1)
    return (grad_x, grad_q, new_master, new_first, new_second, saved)


def solution(mesh):
    fine = Mesh(mesh.devices.reshape(2, 4, 4, 2, 4), ("zl", "x", "y", "c", "t"))
    dp = ("zl", "x", "y", "c")
    every = dp + ("t",)
    weight = P(None, dp, "t")
    return jax.shard_map(
        per_device,
        mesh=fine,
        in_specs=(P(every, None), P(dp, "t"), P(dp, "t"), weight, weight, weight, P()),
        out_specs=(P(every, None), P(dp, "t"), weight, weight, weight, P(dp, "t")),
        check_vma=False,
    )
```

```python
import functools
import math

import jax
import jax.numpy as jnp
from jax import lax
from jax.experimental import pallas as pl
from jax.experimental.pallas import tpu as pltpu
from jax.sharding import Mesh, PartitionSpec as P

HEAD_SIZE = 128


norm_eps = 1e-06
rope_base = 1000000.0
beta_one = 0.9
beta_two = 0.95
adam_eps = 1e-08
learn_rate = 0.02
weight_decay = 0.1
step_count = 10.0


def rope_tables(length, head_width):
    half_width = head_width // 2
    index_float = jnp.arange(half_width, dtype=jnp.float32)
    inverse_freq = rope_base ** (-2.0 * index_float / head_width)
    positions = jnp.arange(length, dtype=jnp.float32)
    angles = positions[:, None] * inverse_freq[None, :]
    return (jnp.cos(angles), jnp.sin(angles))


BF = jnp.bfloat16
F32 = jnp.float32
HALF = HEAD_SIZE // 2
PLACES = (0, -1, 1, 2)
NT = (((1,), (1,)), ((), ()))
TT = (((0,), (0,)), ((), ()))


def dot(left, right, dims=None):
    if dims is None:
        dims = (((1,), (0,)), ((), ()))
    return lax.dot_general(left, right, dims, preferred_element_type=F32)


def params(mebibytes=20):
    return pltpu.CompilerParams(vmem_limit_bytes=mebibytes * 1024 * 1024)


def norm_scale(field):
    return lax.rsqrt(jnp.mean(field * field, axis=-1, keepdims=True) + norm_eps)


def norm_back(field, factor, cotan):
    return factor * cotan - field * (factor * factor * factor) * jnp.mean(
        cotan * field, axis=-1, keepdims=True
    )


def turn(field, cosines, sines):
    return field * cosines + pltpu.roll(field, HALF, 1) * sines


def query_kernel(q_ref, cos_ref, sin_ref, out_ref):
    field = q_ref[...].astype(F32)
    out_ref[...] = turn(field * norm_scale(field), cos_ref[...], sin_ref[...]).astype(BF)


def rotated_queries(queries, cosines, sines):
    length, width = queries.shape
    column = pl.BlockSpec((length, HEAD_SIZE), lambda h: (0, h))
    table = pl.BlockSpec((length, HEAD_SIZE), lambda h: (0, 0))
    return pl.pallas_call(
        query_kernel,
        grid=(width // HEAD_SIZE,),
        in_specs=[column, table, table],
        out_specs=column,
        out_shape=jax.ShapeDtypeStruct(queries.shape, BF),
        compiler_params=params(),
        name="query_rope",
    )(queries, cosines, sines)


def row_loop(rows, step, body):
    def run(i, carry):
        body(pl.ds(pl.multiple_of(i * step, step), step))
        return carry

    lax.fori_loop(0, rows // step, run, 0)


def norm_kernel(in_ref, out_ref):
    def body(rows):
        field = in_ref[rows, :].astype(F32)
        out_ref[rows, :] = (field * norm_scale(field)).astype(BF)

    row_loop(in_ref.shape[0], 16, body)


def normed(tokens):
    block = pl.BlockSpec((tokens.shape[0] // 4, tokens.shape[1]), lambda i: (i, 0))
    return pl.pallas_call(
        norm_kernel,
        grid=(4,),
        in_specs=[block],
        out_specs=block,
        out_shape=jax.ShapeDtypeStruct(tokens.shape, BF),
        compiler_params=params(),
        name="norm",
    )(tokens)


def project_early_kernel(scale, offset_ref, first_ref, second_ref, *refs):
    w_refs, whole_ref, plain_ref = refs[:-2], refs[-2], refs[-1]
    block = whole_ref.shape[0] // offset_ref.shape[0]
    at = 0
    for w_ref in w_refs:
        count = w_ref.shape[0] // block

        def body(k, carry, at=at, w_ref=w_ref):
            row = pl.ds(pl.multiple_of(offset_ref[at + k], 16), block)
            whole_ref[row, :] = w_ref[pl.ds(pl.multiple_of(k * block, 16), block), :]
            return carry

        lax.fori_loop(0, count, body, 0)
        at += count
    plain_ref[...] = rows_times(first_ref, second_ref, whole_ref) * scale


def rows_times(first_ref, second_ref, whole_ref):
    chunk = whole_ref.shape[0] // 4
    total = 0.0
    for j in range(4):
        columns = slice(j * chunk, (j + 1) * chunk)
        field = jnp.concatenate([first_ref[:, columns], second_ref[:, columns]], axis=0)
        total = total + dot(field, whole_ref[columns])
    return total


def project_early(offsets, first, second, pieces, scale):
    vmem = pl.BlockSpec(memory_space=pltpu.VMEM)
    shape = (first.shape[1], pieces[0].shape[1])
    return pl.pallas_call(
        functools.partial(project_early_kernel, scale),
        in_specs=[pl.BlockSpec(memory_space=pltpu.SMEM)] + [vmem] * (2 + len(pieces)),
        out_specs=[vmem, vmem],
        out_shape=[
            jax.ShapeDtypeStruct(shape, BF),
            jax.ShapeDtypeStruct((2 * first.shape[0], shape[1]), F32),
        ],
        compiler_params=params(),
        name="project_early",
    )(offsets, first, second, *pieces)


def project_kernel(scale, order_ref, first_ref, second_ref, whole_ref, early_ref, cos_ref, sin_ref, plain_ref, *out_refs):
    tokens = cos_ref.shape[0]
    plain_ref[: 2 * tokens] = early_ref[...]
    plain_ref[2 * tokens :] = rows_times(first_ref, second_ref, whole_ref) * scale
    for k in range(4):
        rows = pl.ds(pl.multiple_of(order_ref[k] * tokens, tokens), tokens)
        u = plain_ref[rows, :HEAD_SIZE]
        out_refs[k][0] = turn(u * norm_scale(u), cos_ref[...], sin_ref[...]).astype(BF)
        out_refs[k][1] = plain_ref[rows, HEAD_SIZE:].astype(BF)


def project(order, first, second, weights, early, cosines, sines, scale):
    tokens = cosines.shape[0]
    vmem = pl.BlockSpec(memory_space=pltpu.VMEM)
    result = pl.pallas_call(
        functools.partial(project_kernel, scale),
        in_specs=[pl.BlockSpec(memory_space=pltpu.SMEM)] + [vmem] * 6,
        out_specs=[vmem] * 5,
        out_shape=[jax.ShapeDtypeStruct((4 * tokens, weights.shape[1]), F32)]
        + [jax.ShapeDtypeStruct((2, tokens, HEAD_SIZE), BF)] * 4,
        compiler_params=params(),
        name="project",
    )(order, first, second, weights, early, cosines, sines)
    return result[0], result[1:]


def sum_kernel(*refs):
    in_refs, out_refs = refs[:4], refs[4:]
    rows = out_refs[0].shape[0]
    for index, out_ref in enumerate(out_refs):
        part = slice(index * rows, (index + 1) * rows)
        total = sum(ref[part].astype(F32) for ref in in_refs[-3:]) + in_refs[0][part].astype(F32)
        out_ref[...] = total.astype(out_ref.dtype)


def sum_of(own, arrived, first_type):
    shape = (own.shape[0] // 4, own.shape[1])
    vmem = pl.BlockSpec(memory_space=pltpu.VMEM)
    return pl.pallas_call(
        sum_kernel,
        in_specs=[vmem] * 4,
        out_specs=[vmem] * 4,
        out_shape=[jax.ShapeDtypeStruct(shape, first_type)] + [jax.ShapeDtypeStruct(shape, BF)] * 3,
        compiler_params=params(),
        name="sum",
    )(own, *arrived)


def turn_kernel(offset_ref, first_ref, second_ref, out_ref, scratch):
    rows = first_ref.shape[0]
    block = scratch.shape[0] // offset_ref.shape[0]

    def turn_some(columns):
        scratch[columns, :rows] = first_ref[:, columns].T
        scratch[columns, rows:] = second_ref[:, columns].T

    row_loop(scratch.shape[0], 512, turn_some)

    def body(k, carry):
        row = pl.ds(pl.multiple_of(offset_ref[k], 16), block)
        out_ref[pl.ds(pl.multiple_of(k * block, 16), block), :] = scratch[row, :]
        return carry

    lax.fori_loop(0, offset_ref.shape[0], body, 0)


def turned(offsets, first, second):
    shape = (first.shape[1], 2 * first.shape[0])
    vmem = pl.BlockSpec(memory_space=pltpu.VMEM)
    return pl.pallas_call(
        turn_kernel,
        in_specs=[pl.BlockSpec(memory_space=pltpu.SMEM), vmem, vmem],
        out_specs=vmem,
        out_shape=jax.ShapeDtypeStruct(shape, BF),
        scratch_shapes=[pltpu.VMEM(shape, BF)],
        compiler_params=params(),
        name="turn",
    )(offsets, first, second)


def weight_grad_kernel(quarters, early_ref, late_ref, cotan_ref, *out_refs):
    rows = out_refs[0].shape[0]
    for index, out_ref in zip(quarters, out_refs):
        part = slice(index * rows, (index + 1) * rows)
        field = jnp.concatenate([early_ref[part], late_ref[part]], axis=1)
        out_ref[...] = dot(field, cotan_ref[...]).astype(BF)


def weight_grads(early, late, cotan, quarters):
    vmem = pl.BlockSpec(memory_space=pltpu.VMEM)
    shape = (early.shape[0] // 4, cotan.shape[1])
    return pl.pallas_call(
        functools.partial(weight_grad_kernel, quarters),
        in_specs=[vmem] * 3,
        out_specs=[vmem] * len(quarters),
        out_shape=[jax.ShapeDtypeStruct(shape, BF)] * len(quarters),
        compiler_params=params(),
        name="weight_grads",
    )(early, late, cotan)


def attention_kernel(order_ref, q_ref, g_ref, *refs):
    kv_refs, dkv_refs = refs[:4], refs[4:8]
    k_ref, ds0_ref, ds1_ref, v_ref, dk_acc, dv_acc = refs[8:]
    step = pl.program_id(0)
    length, width = q_ref.shape
    tokens, mid, heads = length // 4, length // 2, width // HEAD_SIZE
    scale = 1.0 / math.sqrt(HEAD_SIZE)

    @pl.when(step == 0)
    def _():
        dk_acc[...] = jnp.zeros_like(dk_acc)
        dv_acc[...] = jnp.zeros_like(dv_acc)
        for k in range(4):
            rows = pl.ds(pl.multiple_of(order_ref[k] * tokens, tokens), tokens)
            k_ref[rows, :] = kv_refs[k][0]
            v_ref[rows, :] = kv_refs[k][1]

    early, late = slice(0, mid), slice(mid, length)
    row = lax.broadcasted_iota(jnp.int32, (mid, mid), 0)
    column = lax.broadcasted_iota(jnp.int32, (mid, mid), 1)
    allowed = row <= column
    factor = scale * math.log2(math.e)
    each = range(heads)

    def at(ref, rows, h):
        return ref[rows, h * HEAD_SIZE : (h + 1) * HEAD_SIZE]

    def products(left_ref, right_ref):
        return [
            [
                dot(left_ref[early], at(right_ref, early, h), NT),
                dot(left_ref[early], at(right_ref, late, h), NT),
                dot(left_ref[late], at(right_ref, late, h), NT),
            ]
            for h in each
        ]

    def add(acc, terms, right_ref):
        acc[early] += sum(
            dot(terms[h][0], at(right_ref, early, h)) + dot(terms[h][1], at(right_ref, late, h))
            for h in each
        )
        acc[late] += sum(dot(terms[h][2], at(right_ref, late, h)) for h in each)

    def column_sums(terms):
        first, second, third = (jnp.sum(term, axis=0, keepdims=True) for term in terms)
        return first, second + third

    scores = products(k_ref, q_ref)
    d_probs = products(v_ref, g_ref)
    probs = []
    for h in each:
        a, b, c = scores[h]
        a = jnp.where(allowed, jnp.exp2(a * factor), 0.0)
        b = jnp.exp2(b * factor)
        c = jnp.where(allowed, jnp.exp2(c * factor), 0.0)
        sum_a, sum_b = column_sums((a, b, c))
        inv_a, inv_b = 1.0 / sum_a, 1.0 / sum_b
        probs.append((a * inv_a, b * inv_b, c * inv_b))
    add(dv_acc, [[term.astype(BF) for term in probs[h]] for h in each], g_ref)
    d_scores = []
    for h in each:
        sum_a, sum_b = column_sums([p * d for p, d in zip(probs[h], d_probs[h])])
        d_scores.append(
            [
                (p * (d - total)).astype(BF)
                for p, d, total in zip(probs[h], d_probs[h], (sum_a, sum_b, sum_b))
            ]
        )
        ds0_ref[h, :, :mid] = d_scores[h][0]
        ds0_ref[h, :, mid:] = d_scores[h][1]
        ds1_ref[h] = d_scores[h][2]
    add(dk_acc, d_scores, q_ref)

    @pl.when(step == pl.num_programs(0) - 1)
    def _():
        for k in range(4):
            rows = pl.ds(pl.multiple_of(order_ref[k] * tokens, tokens), tokens)
            dkv_refs[k][0] = (dk_acc[rows, :] * scale).astype(BF)
            dkv_refs[k][1] = dv_acc[rows, :].astype(BF)


def attention(order, rotated, incoming, pieces):
    length, width = rotated.shape
    heads, mid, pair = width // HEAD_SIZE, length // 2, 2
    columns = pl.BlockSpec((length, pair * HEAD_SIZE), lambda h: (0, h))
    whole = pl.BlockSpec((length, HEAD_SIZE), lambda h: (0, 0))
    piece = pl.BlockSpec(pieces[0].shape, lambda h: (0, 0, 0))
    result = pl.pallas_call(
        attention_kernel,
        grid=(heads // pair,),
        in_specs=[pl.BlockSpec(memory_space=pltpu.SMEM), columns, columns] + [piece] * 4,
        out_specs=[piece] * 4
        + [
            whole,
            pl.BlockSpec((pair, mid, length), lambda h: (h, 0, 0)),
            pl.BlockSpec((pair, mid, mid), lambda h: (h, 0, 0)),
        ],
        out_shape=[jax.ShapeDtypeStruct(pieces[0].shape, BF)] * 4
        + [
            jax.ShapeDtypeStruct((length, HEAD_SIZE), BF),
            jax.ShapeDtypeStruct((heads, mid, length), BF),
            jax.ShapeDtypeStruct((heads, mid, mid), BF),
        ],
        scratch_shapes=[pltpu.VMEM((length, HEAD_SIZE), BF)]
        + [pltpu.VMEM((length, HEAD_SIZE), F32)] * 2,
        compiler_params=params(32),
        name="attention",
    )(order, rotated, incoming, *pieces)
    return result[:4], result[4], result[5], result[6]


def grad_query_kernel(q_ref, k_ref, ds0_ref, ds1_ref, cos_ref, sin_ref, *refs):
    out_ref = refs[-1]
    mid = ds0_ref.shape[1]
    scale = 1.0 / math.sqrt(HEAD_SIZE)
    k0, k1 = k_ref[:mid], k_ref[mid:]
    both = dot(k0, ds0_ref[0], TT)
    early = both[:, :mid]
    late = both[:, mid:] + dot(k1, ds1_ref[0], TT)
    cotan = jnp.concatenate([early.T, late.T], axis=0) * scale
    field = q_ref[...].astype(F32)
    cotan = turn(cotan, cos_ref[...], -sin_ref[...])
    out_ref[...] = norm_back(field, norm_scale(field), cotan).astype(BF)


def grad_queries(queries, key, ds0, ds1, cosines, sines, first, given=None):
    length, width = queries.shape
    heads, mid = width // HEAD_SIZE, length // 2
    column = pl.BlockSpec((length, HEAD_SIZE), lambda h: (0, first + h))
    whole = pl.BlockSpec((length, HEAD_SIZE), lambda h: (0, 0))
    specs = [
        column,
        whole,
        pl.BlockSpec((1, mid, length), lambda h: (first + h, 0, 0)),
        pl.BlockSpec((1, mid, mid), lambda h: (first + h, 0, 0)),
        whole,
        whole,
    ]
    operands = [queries, key, ds0, ds1, cosines, sines]
    if given is not None:
        specs.append(pl.BlockSpec(memory_space=pl.ANY))
        operands.append(given)
    return pl.pallas_call(
        grad_query_kernel,
        grid=(heads // 2,),
        in_specs=specs,
        out_specs=column,
        out_shape=jax.ShapeDtypeStruct(queries.shape, BF),
        input_output_aliases={} if given is None else {6: 0},
        compiler_params=params(16),
        name="grad_query",
    )(*operands)


def cotan_kernel(quarters, order_ref, b0_ref, b1_ref, b2_ref, b3_ref, plain_ref, cos_ref, sin_ref, *refs):
    early_ref, late_ref, out_ref, part_refs = refs[0], refs[1], refs[2], refs[3:]
    tokens = cos_ref.shape[0]
    for k, back_ref in enumerate((b0_ref, b1_ref, b2_ref, b3_ref)):
        rows = pl.ds(pl.multiple_of(order_ref[k] * tokens, tokens), tokens)
        u = plain_ref[rows, :HEAD_SIZE]
        back = turn(back_ref[0].astype(F32), cos_ref[...], -sin_ref[...])
        out_ref[rows, :HEAD_SIZE] = norm_back(u, norm_scale(u), back).astype(BF)
        out_ref[rows, HEAD_SIZE:] = back_ref[1]
    weight_grad_kernel(quarters, early_ref, late_ref, out_ref, *part_refs)


def key_value_cotan(order, back, plain, cosines, sines, early, late, quarters):
    vmem = pl.BlockSpec(memory_space=pltpu.VMEM)
    part = jax.ShapeDtypeStruct((early.shape[0] // 4, plain.shape[1]), BF)
    result = pl.pallas_call(
        functools.partial(cotan_kernel, quarters),
        in_specs=[pl.BlockSpec(memory_space=pltpu.SMEM)] + [vmem] * 9,
        out_specs=[vmem] * (1 + len(quarters)),
        out_shape=[jax.ShapeDtypeStruct(plain.shape, BF)] + [part] * len(quarters),
        compiler_params=params(),
        name="key_value_cotan",
    )(order, *back, plain, cosines, sines, early, late)
    return result[0], result[1:]


def grad_token_kernel(x_ref, mine_ref, layer_ref, *refs):
    out_ref = refs[-1]

    def body(rows):
        cotan = mine_ref[rows, :].astype(F32) + layer_ref[rows, :].astype(F32)
        field = x_ref[rows, :].astype(F32)
        out_ref[rows, :] = norm_back(field, norm_scale(field), cotan).astype(BF)

    row_loop(x_ref.shape[0], 16, body)


def grad_tokens(tokens, mine, from_layer, start, given=None):
    step, width = from_layer.shape[0], tokens.shape[1]
    first = start // step
    here = pl.BlockSpec((step, width), lambda i: (first + i, 0))
    specs = [here, here, pl.BlockSpec((step, width), lambda i: (i, 0))]
    operands = [tokens, mine, from_layer]
    if given is not None:
        specs.append(pl.BlockSpec(memory_space=pl.ANY))
        operands.append(given)
    return pl.pallas_call(
        grad_token_kernel,
        grid=(from_layer.shape[0] // step,),
        in_specs=specs,
        out_specs=here,
        out_shape=jax.ShapeDtypeStruct(tokens.shape, BF),
        input_output_aliases={} if given is None else {3: 0},
        compiler_params=params(60),
        name="grad_tokens",
    )(*operands)


def plane_pairs(first, step):
    pairs = []
    for x in range(4):
        for y in range(4):
            for c in range(2):
                along_x = (c == 0) == first
                to_x = (x + step) % 4 if along_x else x
                to_y = y if along_x else (y + step) % 4
                pairs.append(((x * 4 + y) * 2 + c, (to_x * 4 + to_y) * 2 + c))
    return pairs


def far(block, step):
    return lax.ppermute(block, ("x", "y", "c"), plane_pairs(True, step))


def near(block, step):
    return lax.ppermute(block, ("x", "y", "c"), plane_pairs(False, step))


def swap_cores(block):
    return lax.ppermute(block, "c", [(0, 1), (1, 0)])


def group_pairs(target):
    pairs = []
    for g in range(4):
        for t in range(4):
            to_g, to_t = target(g, t)
            pairs.append((g * 4 + t, (to_g % 4) * 4 + to_t % 4))
    return pairs


def to_heads(block, k):
    return lax.ppermute(block, ("zl", "c", "t"), group_pairs(lambda g, t: (t, g + k)))


def from_heads(block, k):
    return lax.ppermute(block, ("zl", "c", "t"), group_pairs(lambda g, t: (t + k, g)))


def swap_layers(block):
    return lax.ppermute(block, "zl", [(0, 1), (1, 0)])


def after(first, *later):
    return lax.optimization_barrier((first,) + later)[1:]


def per_device(
    tokens,
    queries,
    grad_out,
    key_value_master_weight,
    key_value_first_moment,
    key_value_second_moment,
    writer,
):
    own_tokens, model_width = tokens.shape
    unit_scale = 1.0 / math.sqrt(model_width)
    length = queries.shape[0]
    rows = key_value_master_weight.shape[1]
    core = lax.axis_index("c")
    x_index, y_index = lax.axis_index("x"), lax.axis_index("y")
    t_index = lax.axis_index("t")
    g_index = 2 * lax.axis_index("zl") + core

    own_weight = key_value_master_weight.astype(BF)
    own_weight = jnp.concatenate([own_weight[0], own_weight[1]], axis=1)
    stage_parts = [to_heads(own_weight, k) for k in range(4)]
    stage = jnp.concatenate(stage_parts, axis=0)
    own_block = normed(tokens)
    from_z = swap_layers(after(stage_parts[0], own_block)[0])
    from_core = swap_cores(own_block)
    shard = jnp.concatenate([stage, near(stage, 1), near(stage, -1), near(stage, 2)], axis=0)
    pieces = [shard, far(shard, 1), far(shard, -1), far(shard, 2)]

    place = jnp.array(PLACES, jnp.int32)
    count = jnp.arange(4, dtype=jnp.int32)
    far_place = (jnp.where(core == 0, x_index, y_index) + place) % 4
    near_place = (jnp.where(core == 0, y_index, x_index) + place) % 4
    far_step = jnp.where(core == 0, 8 * rows, 2 * rows)
    near_step = jnp.where(core == 0, 2 * rows, 8 * rows)
    source = (t_index - count) % 4
    offsets = (
        far_place[:, None, None] * far_step
        + near_place[None, :, None] * near_step
        + ((source // 2) * (32 * rows) + (source % 2) * rows)[None, None, :]
    )
    offsets = offsets.reshape(64).astype(jnp.int32)
    sequence_order = ((t_index + count) % 4) ^ g_index
    block_order = (g_index - count) % 4

    cosines, sines = rope_tables(length, HEAD_SIZE)
    cosines = jnp.concatenate([cosines, cosines], axis=1)
    sines = jnp.concatenate([-sines, sines], axis=1)
    own_cos = lax.dynamic_slice_in_dim(cosines, t_index * own_tokens, own_tokens, 0)
    own_sin = lax.dynamic_slice_in_dim(sines, t_index * own_tokens, own_tokens, 0)
    rotated = rotated_queries(queries, cosines, sines)

    early = turned(offsets, own_block, from_core)
    from_core, from_z, own_cos, own_sin, sequence_order, block_order, offsets = after(
        (pieces, rotated, early), from_core, from_z, own_cos, own_sin, sequence_order, block_order, offsets
    )
    blocks = [own_block, from_core, from_z, swap_cores(from_z)]
    weights, plain_early = project_early(offsets, blocks[0], blocks[1], pieces, unit_scale)
    plain, projected = project(
        sequence_order, blocks[2], blocks[3], weights, plain_early, own_cos, own_sin, unit_scale
    )
    arrived = [from_heads(block, k) for k, block in enumerate(projected)]
    late = turned(offsets, *after(plain, blocks[2], blocks[3]))
    (arrived,) = after(late, arrived)

    returning, key, ds0, ds1 = attention(block_order, rotated, grad_out, arrived)
    back = [to_heads(block, -k) for k, block in enumerate(returning)]
    grad_q = grad_queries(queries, key, ds0, ds1, cosines, sines, 0)
    (back,) = after(grad_q, back)
    cotan, sent_parts = key_value_cotan(
        sequence_order, back, plain, own_cos, own_sin, early, late, (1, 2, 3)
    )

    part = [None] + list(sent_parts)
    arriving = [far(part[1], -1), far(part[2], 1), far(part[3], 2)]

    (cotan,) = after(part[1], cotan)
    rows_of = cotan.reshape(4, own_tokens, -1)
    sent = dot(jnp.concatenate([rows_of[1], rows_of[3]], axis=0), weights, NT) * unit_scale
    sent = sent.astype(BF)
    swapped = swap_cores(sent)
    (kept_from,) = after(sent, jnp.concatenate([rows_of[0], rows_of[2]], axis=0))
    kept = dot(kept_from, weights, NT) * unit_scale
    to_z = (kept[own_tokens:] + swapped[own_tokens:].astype(F32)).astype(BF)
    starts = (0, 48, 96)
    to_z = [to_z[starts[0] : starts[1]], to_z[starts[1] : starts[2]], to_z[starts[2] :]]
    z_first = swap_layers(to_z[0])

    kept, swapped, cotan = after(to_z, kept, swapped, cotan)
    part[0] = weight_grads(early, late, cotan, (0,))[0]
    mine = (kept[:own_tokens] + swapped[:own_tokens].astype(F32)).astype(BF)
    own_part, to_z[1] = after((z_first, mine), part[0], to_z[1])
    own = sum_of(own_part, arriving, F32)
    z_second = swap_layers(to_z[1])
    summed = sum_of(own[0], [near(own[1], -1), near(own[2], 1), near(own[3], 2)], BF)
    grad_q = grad_queries(
        queries, key, after(own, ds0)[0], ds1, cosines, sines, queries.shape[1] // HEAD_SIZE // 2, grad_q
    )
    (summed,) = after((z_second, grad_q), summed)
    final = [from_heads(summed[k], -k) for k in range(4)]
    grad_x = grad_tokens(tokens, mine, after(summed, z_second)[0], starts[1])
    (final,) = after(grad_x, final)
    final = sum(block.astype(F32) for block in final) * unit_scale
    weight_grad = jnp.stack([final[:, :HEAD_SIZE], final[:, HEAD_SIZE:]], axis=0)

    to_z[2], z_first = after(final, to_z[2], z_first)
    grad_x = grad_tokens(tokens, mine, z_first, starts[0], grad_x)
    grad_x = grad_tokens(tokens, mine, swap_layers(to_z[2]), starts[2], grad_x)

    new_first = beta_one * key_value_first_moment + (1.0 - beta_one) * weight_grad
    new_second = beta_two * key_value_second_moment + (1.0 - beta_two) * weight_grad * weight_grad
    first_hat = new_first / (1.0 - beta_one**step_count)
    second_hat = new_second / (1.0 - beta_two**step_count)
    new_master = key_value_master_weight - learn_rate * (
        first_hat / (jnp.sqrt(second_hat) + adam_eps) + weight_decay * key_value_master_weight
    )
    replicas = writer.shape[0]
    pieces = new_master.astype(BF).reshape(replicas, 2, -1)
    rank_ids = jnp.arange(replicas, dtype=jnp.int32)
    chosen = (writer[None, :] == rank_ids[:, None]).astype(BF)
    outgoing = dot(chosen, pieces).astype(BF)
    saved = lax.all_to_all(outgoing, ("zl", "x", "y", "c"), 0, 0, tiled=True)
    saved = after(grad_x, saved)[0].reshape(replicas, -1)
    return (grad_x, grad_q, new_master, new_first, new_second, saved)


def solution(mesh):
    fine = Mesh(mesh.devices.reshape(2, 4, 4, 2, 4), ("zl", "x", "y", "c", "t"))
    dp = ("zl", "x", "y", "c")
    every = dp + ("t",)
    weight = P(None, dp, "t")
    return jax.shard_map(
        per_device,
        mesh=fine,
        in_specs=(P(every, None), P(dp, "t"), P(dp, "t"), weight, weight, weight, P()),
        out_specs=(P(every, None), P(dp, "t"), weight, weight, weight, P(dp, "t")),
        check_vma=False,
    )
```
